128 devices in a mesh: px: 8 (over y, core), py: 16 (over x, z).
Axes of the slice: x: 4, y: 4, z: 4, core: 2. Of those that a mesh axis runs over, the one named last changes fastest.
Arguments:
- checkpoint_field: float32 [32, 128, 1024], P('px', 'py'), may hold values from -6 to 6
- checkpoint_memory: float32 [4, 32, 128, 1024], P(None, 'px', 'py'), may hold values from -3 to 3
- stiffness: bfloat16 [32, 128, 64, 512], P('px', 'py'), may hold values from -0.25 to 0.25
- block_offsets: int32 [32, 128, 8], P('px', 'py'), may hold values from 0 to 8, as said below
- chargeability: float32 [32, 128, 64], P('px', 'py'), may hold values from 0.05 to 0.5
- relaxation: float32 [4, 32, 128, 64], P(None, 'px', 'py'), may hold values from 0.2 to 0.95
- observed: float32 [32768, 128], P(('px', 'py')), may hold values from -6 to 6
- receiver_part: int32 [32768, 1], P(('px', 'py')), may hold values from 0 to 127; in each aligned block of 256 rows (0 to 255, 256 to 511, ...) at most 8 rows name the same one
- receiver_node: int32 [32768], P(('px', 'py')), may hold values from 0 to 2047
- gate_step: int32 [8], replicated, may hold values from 1 to 4
Outputs:
- adjoint_field: float32 [32, 128, 1024], P('px', 'py')
- charge_gradient: float32 [32, 128, 64], P('px', 'py')
The draws below stay inside these ranges and needn't reach their ends.
Inputs may be any that keep to these rules, and one draw needn't show every extreme that they name: `block_offsets`: each block row lists its own block (code 4) first and then 8 - 1 further distinct neighbour codes. `receiver_part`: within the 256 receivers of one owner (aligned blocks of rows) no partition is named more than 8 times, a bound that some block reaches.
All inputs are finite; a program needn't handle non-finite values.
Results may differ from the reference program's by a relative error of at most 0.0095.
Values may be sent and summed in bfloat16 or wider, within the bound.
No kernel may reach another device: no remote copies, remote signals or barrier semaphores. Data moves between devices by JAX's collectives and lax.ppermute only.
A program may use at most 128 MiB of HBM per device.

```python
import math
import jax
import jax.numpy as jnp
import numpy as np
from jax import lax

BX = 4
BY = 8
NODE_BLK = 64
NNZ = 8
S = 16
Q = 4
NT = 4
G = 8
R_DEV = 256
CAP = 8
GX = 32
GY = 128
R = 32768
N_PY = 16
DEVICES = 128


def draw_block_offsets(key, part):
    key = jax.random.fold_in(key, 11)
    scores = jax.random.randint(key, (GX, GY, 8), 0, 1 << 20) * 8 + jnp.arange(8, dtype=jnp.int32)
    order = jnp.argsort(scores, axis=-1)[..., :NNZ - 1]
    others = jnp.array([0, 1, 2, 3, 5, 6, 7, 8], dtype=jnp.int32)
    chosen = others[order]
    own = jnp.full((GX, GY, 1), 4, jnp.int32)
    return jnp.concatenate([own, chosen], axis=-1).astype(jnp.int32)


def set_ends(values, own_key, low, high):
    longest = values.shape.index(max(values.shape))
    spots = []
    for shift in (0, 1):
        where = [jax.random.randint(jax.random.fold_in(own_key, axis), (), 0, length) for axis, length in enumerate(values.shape)]
        where[longest] = (where[longest] + shift) % values.shape[longest]
        spots.append(tuple(where))
    return values.at[spots[0]].set(low).at[spots[1]].set(high)


def block_scale(own_key, extent, cuts, low, largest):
    loudness, own = 1.0, jax.random.fold_in(own_key, 6)
    for dim, shards_of in cuts:
        draws = jnp.exp(jax.random.uniform(jax.random.fold_in(own, dim), (shards_of,), jnp.float32, low / len(cuts), largest / len(cuts)))
        loudness = loudness * jnp.repeat(draws, extent[dim] // shards_of).reshape([-1 if axis == dim else 1 for axis in range(len(extent))])
    return loudness


def routed_block(key, own, number, rows, amount, top, reach, lean):
    ranking = jax.random.permutation(key, amount)
    heavy_load, ordinary = shares(amount, rows * top, reach, lean, True), shares(amount, rows * top, reach, lean, False)
    places = jnp.arange(amount)

    def named(tallies, offset_by):
        used = int((tallies > 0).sum())
        fixed = max(1, used // 4)
        passed = fixed + (places - fixed + offset_by * (used - fixed)) % max(1, amount - fixed)
        return jnp.zeros((amount,), jnp.int32).at[ranking[jnp.where(places < fixed, places, passed)]].set(jnp.asarray(tallies, jnp.int32))

    tallies = jnp.where(number % 4 == 0, named(heavy_load, number // 4), named(ordinary, number - number // 4 - 1))
    mixed = jax.random.permutation(jax.random.fold_in(own, 3), amount)
    source_of, taker = mixed[0:amount // 2 * 2:2], mixed[1:amount // 2 * 2:2]
    slack = jnp.minimum(tallies[source_of] - 1, reach - tallies[taker]) // 2
    slack = jnp.where((source_of == ranking[0]) | (taker == ranking[0]) | (tallies[taker] == 0), 0, jnp.maximum(slack, 0))
    passed = jax.random.randint(jax.random.fold_in(own, 4), (amount // 2,), 0, 1 << 20) % (slack + 1)
    tallies = tallies.at[source_of].add(-passed).at[taker].add(passed)
    items = jnp.searchsorted(jnp.cumsum(tallies), jnp.arange(rows * top), side="right").astype(jnp.int32)
    grid = items.reshape(top, rows).T
    grid = grid[jax.random.permutation(jax.random.fold_in(own, 1), rows)]
    offset_by = jax.random.randint(jax.random.fold_in(own, 2), (rows, 1), 0, top)
    return jnp.take_along_axis(grid, (jnp.arange(top)[None, :] + offset_by) % top, axis=1)


def shares(amount, total, limit, lean, full):
    loads = [(1 << 20) // math.isqrt(grade ** lean) + 1 for grade in range(1, amount + 1)]
    largest = limit if full else min(limit, max(-(-total // amount), total * loads[0] // sum(loads)))
    least = 1 if total - largest >= amount - 1 else 0
    holding, surplus = [largest] + [least] * (amount - 1), total - largest - least * (amount - 1)
    while surplus > 0:
        movable = [i for i in range(1, amount) if holding[i] < largest] or [i for i in range(1, amount) if holding[i] < limit]
        mass, left = sum([loads[i] for i in movable]), surplus
        for i in movable:
            extra = min(limit - holding[i], max(1, left * loads[i] // mass), surplus)
            holding[i] = holding[i] + extra
            surplus = surplus - extra
    return np.array(holding)


def bell_draw(key, dims, deviation, bound, cuts=(), kind=jnp.bfloat16):
    gain = block_scale(key, dims, cuts, -0.22, 0.18) if cuts else 1.0
    values = jax.random.normal(key, dims, jnp.float32) * deviation * gain
    return jnp.minimum(jnp.maximum(values, -bound), bound).astype(kind)


def setup_inputs(seed: int = 0) -> dict:
    keys = jax.random.split(jax.random.key(seed), 11)
    checkpoint_field = bell_draw(keys[0], (GX, GY, S * NODE_BLK), 1.0, 6.0, ((0, 8), (1, 16)), jnp.float32)
    checkpoint_memory = bell_draw(keys[1], (Q, GX, GY, S * NODE_BLK), 0.5, 3.0, ((1, 8), (2, 16)), jnp.float32)
    stiffness = bell_draw(keys[2], (GX, GY, NODE_BLK, NNZ * NODE_BLK), (NNZ * NODE_BLK) ** -0.5, 0.25, ((0, 8), (1, 16)))
    block_offsets = draw_block_offsets(jax.random.fold_in(keys[10], 71), 0)
    chargeability = jnp.clip(jnp.exp(math.log(0.5) - 2.3025851 * jax.random.uniform(keys[4], (GX, GY, NODE_BLK), jnp.float32) ** block_scale(keys[4], (GX, GY, NODE_BLK), ((0, 8), (1, 16)), -0.2, 0.2)), 0.05, 0.5)
    relaxation = jnp.clip(0.2 + 0.75 * jax.random.uniform(keys[5], (Q, GX, GY, NODE_BLK), jnp.float32) ** block_scale(keys[5], (Q, GX, GY, NODE_BLK), ((1, 8), (2, 16)), -0.2, 0.2), 0.2, 0.95)
    observed = bell_draw(keys[6], (R, G * S), 1.0, 6.0, ((0, 128),), jnp.float32)
    receiver_part_keys = jax.random.split(jax.random.fold_in(keys[7], 1), R // R_DEV)
    receiver_part_turns = jax.random.permutation(jax.random.fold_in(keys[7], 3), R // R_DEV)
    receiver_part = jax.vmap(lambda own, number: routed_block(jax.random.fold_in(keys[7], 2), own, number, R_DEV, DEVICES, 1, CAP, 2))(receiver_part_keys, receiver_part_turns).reshape((R, 1))
    receiver_node = set_ends(jax.random.randint(keys[8], (R,), 0, BX * BY * NODE_BLK), jax.random.fold_in(keys[8], 1), 0, (BX * BY * NODE_BLK) - 1).astype(jnp.int32)
    gate_step = set_ends(jax.random.randint(keys[9], (G,), 1, NT + 1), jax.random.fold_in(keys[9], 1), 1, NT).astype(jnp.int32)
    return {"checkpoint_field": checkpoint_field, "checkpoint_memory": checkpoint_memory, "stiffness": stiffness, "block_offsets": block_offsets, "chargeability": chargeability, "relaxation": relaxation, "observed": observed, "receiver_part": receiver_part, "receiver_node": receiver_node, "gate_step": gate_step}


OFFSET_PAIRS = ((-1, -1), (-1, 0), (-1, 1), (0, -1), (0, 0), (0, 1), (1, -1), (1, 0), (1, 1))


def apply_forward(current, stiffness, block_offsets):
    height, breadth, wide_dim = current.shape
    node_block = stiffness.shape[2]
    nonzeros = block_offsets.shape[2]
    sources = wide_dim // node_block
    padded = lax.optimization_barrier(jnp.pad(current.astype(jnp.bfloat16), ((1, 1), (1, 1), (0, 0))))

    def one_row(item):
        row_index, stiff_row, offset_row = item
        window = lax.dynamic_slice_in_dim(padded, row_index, 3, 0).astype(jnp.float32)
        shifted = jnp.stack([window[1 + shift_x, 1 + shift_y:1 + shift_y + breadth] for shift_x, shift_y in OFFSET_PAIRS])
        selector = (offset_row[:, :, None] == jnp.arange(9, dtype=jnp.int32)).astype(jnp.float32)
        picked = jnp.einsum("yko,oyw->ykw", selector, shifted, precision=lax.Precision.HIGHEST)
        picked = picked.reshape(breadth, nonzeros, sources, node_block).transpose(0, 2, 1, 3)
        picked = picked.reshape(breadth, sources, nonzeros * node_block)
        applied = jnp.einsum("yin,ysn->ysi", stiff_row.astype(jnp.float32), picked, precision=lax.Precision.HIGHEST)
        return applied.reshape(breadth, wide_dim)

    return lax.map(one_row, (jnp.arange(height, dtype=jnp.int32), stiffness, block_offsets))


def apply_adjoint(current, stiffness, block_offsets):
    height, breadth, wide_dim = current.shape
    node_block = stiffness.shape[2]
    nonzeros = block_offsets.shape[2]
    sources = wide_dim // node_block
    rounded = lax.optimization_barrier(current.astype(jnp.bfloat16)).astype(jnp.float32)
    rounded = rounded.reshape(height, breadth, sources, node_block)

    def one_row(total, item):
        row_index, stiff_row, offset_row, field_row = item
        spread = jnp.einsum("yin,ysi->ysn", stiff_row.astype(jnp.float32), field_row, precision=lax.Precision.HIGHEST)
        spread = spread.reshape(breadth, sources, nonzeros, node_block)
        selector = (offset_row[:, :, None] == jnp.arange(9, dtype=jnp.int32)).astype(jnp.float32)
        pieces = jnp.einsum("yko,yskj->oysj", selector, spread, precision=lax.Precision.HIGHEST)
        window = jnp.zeros((3, breadth + 2, sources, node_block), jnp.float32)
        for offset_id, (shift_x, shift_y) in enumerate(OFFSET_PAIRS):
            window = window.at[1 + shift_x, 1 + shift_y:1 + shift_y + breadth].add(pieces[offset_id])
        before = lax.dynamic_slice_in_dim(total, row_index, 3, 0)
        return lax.dynamic_update_slice_in_dim(total, before + window, row_index, 0), None

    total = jnp.zeros((height + 2, breadth + 2, sources, node_block), jnp.float32)
    total, _ = lax.scan(one_row, total, (jnp.arange(height, dtype=jnp.int32), stiffness, block_offsets, rounded))
    return total[1:height + 1, 1:breadth + 1].reshape(height, breadth, wide_dim)


def reference(checkpoint_field, checkpoint_memory, stiffness, block_offsets, chargeability, relaxation, observed, receiver_part, receiver_node, gate_step):
    height, breadth, wide_dim = checkpoint_field.shape
    node_block = stiffness.shape[2]
    sources = wide_dim // node_block
    terms = relaxation.shape[0]
    gates = gate_step.shape[0]
    charge = chargeability[:, :, None, :]
    relax_rate = relaxation[:, :, :, None, :]
    partition = receiver_part[:, 0]
    local_block = receiver_node // node_block
    row_of = (partition // N_PY) * BX + local_block // BY
    column_of = (partition % N_PY) * BY + local_block % BY
    within = receiver_node % node_block
    current = checkpoint_field.reshape(height, breadth, sources, node_block)
    memory = checkpoint_memory.reshape(terms, height, breadth, sources, node_block)
    history = []
    sampled = []
    for moment in range(NT):
        summed = jnp.sum(memory, axis=0)
        history.append(summed)
        applied = apply_forward(current.reshape(height, breadth, wide_dim), stiffness, block_offsets)
        following = applied.reshape(height, breadth, sources, node_block) - charge * summed
        memory = relax_rate * memory + (1.0 - relax_rate) * current
        current = following
        sampled.append(current[row_of, column_of, :, within])
    gate_value = jnp.zeros((observed.shape[0], gates, sources), jnp.float32)
    for moment in range(NT):
        gate_value = gate_value + jnp.where(gate_step[None, :, None] == moment + 1, sampled[moment][:, None, :], 0.0)
    residual = gate_value - observed.reshape(observed.shape[0], gates, sources)

    def inject(adjoint, moment):
        chosen = jnp.sum(jnp.where(gate_step[None, :, None] == moment, residual, 0.0), axis=1)
        return adjoint.at[row_of, column_of, :, within].add(chosen)

    adjoint = inject(jnp.zeros_like(current), NT)
    adjoint_memory = jnp.zeros_like(memory)
    gradient = jnp.zeros((height, breadth, node_block), jnp.float32)
    for moment in range(NT - 1, -1, -1):
        gradient = gradient - jnp.sum(adjoint * history[moment], axis=2)
        pulled = apply_adjoint(adjoint.reshape(height, breadth, wide_dim), stiffness, block_offsets)
        previous = pulled.reshape(height, breadth, sources, node_block) + jnp.sum((1.0 - relax_rate) * adjoint_memory, axis=0)
        adjoint_memory = relax_rate * adjoint_memory - charge * adjoint
        adjoint = previous
        if moment >= 1:
            adjoint = inject(adjoint, moment)
    return adjoint.reshape(height, breadth, wide_dim), gradient
```

```python
import jax
import jax.numpy as jnp
from jax import lax
from jax.experimental import pallas as pl
from jax.experimental.pallas import tpu as pltpu
from jax.sharding import PartitionSpec as P

ROWS, COLS = 4, 8
OWN = ROWS * COLS
CAP = 8
WIDE = COLS + 4
PLACES = (ROWS + 4) * WIDE
F32, BF16 = jnp.float32, jnp.bfloat16
VMEM_BYTES = 24 * 1024 * 1024


def place(row, col):
    return (row + 2) * WIDE + col + 2


def low_lanes(rows):
    return lax.broadcasted_iota(jnp.int32, (rows, 128), 1) < 64


def doubled(plain):
    turned = pltpu.roll(plain, 64, 1)
    low = low_lanes(8)
    return jnp.concatenate([jnp.where(low, plain, turned), jnp.where(low, turned, plain)], 0)


def packed(plain):
    return jnp.concatenate([plain[:, :64], plain[:, 64:]], 0)


def unpacked(rows):
    return jnp.concatenate([rows[:8], rows[8:]], 1)


def halves(plain):
    high = plain.astype(BF16).astype(F32)
    return jnp.concatenate([high, plain - high], 0).astype(BF16)


def joined(pair):
    pair = pair.astype(F32)
    return pair[:8] + pair[8:]


def sides(par_ref, axis, near, far):
    even = par_ref[axis] == 0
    return jnp.where(even, near, far), jnp.where(even, far, near)


def call(kernel, out, inputs, scalars=0, scratch=(), flops=0):
    smem = pl.BlockSpec(memory_space=pltpu.SMEM)
    vmem = pl.BlockSpec(memory_space=pltpu.VMEM)
    moved = sum(a.size * a.dtype.itemsize for a in inputs)
    return pl.pallas_call(
        kernel,
        out_shape=[jax.ShapeDtypeStruct(s, d) for s, d in out],
        in_specs=[smem] * scalars + [vmem] * (len(inputs) - scalars),
        out_specs=[vmem] * len(out),
        scratch_shapes=list(scratch),
        compiler_params=pltpu.CompilerParams(vmem_limit_bytes=VMEM_BYTES),
        cost_estimate=pl.CostEstimate(flops=flops, bytes_accessed=moved, transcendentals=0),
    )(*inputs)


PLAIN = ((OWN, 8, 128), F32)


def to_plain(native, scratch, out):
    for x in range(ROWS):
        for r in range(8):
            scratch[pl.ds(x * 64 + r * 8, 8), :] = native(x, r)
    for x in range(ROWS):
        for y in range(COLS):
            out[x * COLS + y] = scratch[pl.ds(x * 64 + y, 8, stride=8), :]


def lanes(r):
    return pl.ds(r * 128, 128)


def twice(rows):
    return jnp.concatenate([rows, rows], 1)


def px_message(par_ref, plain, addend, outs):
    bases = sides(par_ref, 0, 2, 0)
    edges = sides(par_ref, 0, 3, 0)
    for out, base, edge in zip(outs, bases, edges):
        for k in range(2):
            for p in range(4):
                at = (base + k) * COLS + 2 * p
                out[k * 4 + p] = jnp.concatenate([plain[at], plain[at + 1]], 0).astype(BF16)
        for y in range(COLS):
            out[8 + y] = halves(addend[edge * COLS + y])


def start_kernel(par, field, memory, charge, plain, addend, summed, m_even, m_odd, scratch):
    terms = memory.shape[0]
    to_plain(lambda x, r: field[x, :, lanes(r)], scratch, plain)

    def total(x, r):
        acc = memory[0, x, :, lanes(r)]
        for q in range(1, terms):
            acc = acc + memory[q, x, :, lanes(r)]
        return acc

    to_plain(total, scratch, summed)
    wide = [twice(charge[x]) for x in range(ROWS)]
    for x in range(ROWS):
        for r in range(8):
            at = pl.ds(x * 64 + r * 8, 8)
            scratch[at, :] = scratch[at, :] * (-wide[x])
    for x in range(ROWS):
        for y in range(COLS):
            addend[x * COLS + y] = scratch[pl.ds(x * 64 + y, 8, stride=8), :]
    px_message(par, plain, addend, (m_even, m_odd))


def decay_kernel(field, memory, charge, relaxation, sum1, sum2, sum3, coef, scratch):
    terms = memory.shape[0]
    for x in range(ROWS):
        rates = [twice(relaxation[q, x]) for q in range(terms)]
        w0 = w1 = w2 = 0.0
        for rate in rates:
            w0 = w0 + (1.0 - rate)
            w1 = w1 + rate * (1.0 - rate)
            w2 = w2 + rate * rate * (1.0 - rate)
        for j, value in enumerate((twice(charge[x]), w0, w1, w2)):
            coef[j, pl.ds(x * COLS, COLS), :] = value
    for power, out in ((1, sum1), (2, sum2), (3, sum3)):
        scale = []
        for x in range(ROWS):
            row = []
            for q in range(terms):
                rate = twice(relaxation[q, x])
                row.append(rate if power == 1 else rate * rate if power == 2 else rate * rate * rate)
            scale.append(row)

        def part(x, r):
            acc = coef[power, pl.ds(x * COLS, COLS), :] * field[x, :, lanes(r)]
            for q in range(terms):
                acc = acc + scale[x][q] * memory[q, x, :, lanes(r)]
            return acc

        to_plain(part, scratch, out)


def py_kernel(par, plain, addend, r_even, r_odd, n_even, n_odd):
    pairs = sides(par, 1, 3, 0)
    edges = sides(par, 1, 7, 0)
    for out, pair, edge in zip((n_even, n_odd), pairs, edges):
        for x in range(ROWS):
            at = x * COLS + 2 * pair
            out[x] = jnp.concatenate([plain[at], plain[at + 1]], 0).astype(BF16)
            out[8 + x] = halves(addend[x * COLS + edge])
        for k in range(2):
            out[4 + k] = r_even[k * 4 + pair]
            out[6 + k] = r_odd[k * 4 + pair]
        out[12] = r_even[8 + edge]
        out[13] = r_odd[8 + edge]


def outer_places(par):
    row_even, row_odd = sides(par, 0, ROWS, -1)
    col_even, col_odd = sides(par, 1, COLS, -1)
    listed = []
    for array, row in ((0, row_even), (1, row_odd)):
        listed += [(array, y, place(row, y)) for y in range(COLS)]
    rows = [0, 1, 2, 3, row_even, row_odd]
    for array, col in ((2, col_even), (3, col_odd)):
        listed += [(array, j, place(row, col)) for j, row in enumerate(rows)]
    return listed


def weight_of(blocks, item):
    own, outer = blocks
    if item < OWN:
        return own[item // COLS, item % COLS]
    item -= OWN
    for array, count in zip(outer, (COLS, COLS, ROWS + 2, ROWS + 2)):
        if item < count:
            return array[item]
        item -= count


def forward_pair(par, table, blocks, plain, received, addend, field, middle, store_first, store_second):
    low = low_lanes(16)
    r_even, r_odd, n_even, n_odd = received
    for block in range(OWN):
        field[place(block // COLS, block % COLS)] = doubled(plain[block]).astype(BF16)

    def spread(pair, first, second):
        both = pair.astype(F32)
        field[first] = doubled(both[:8]).astype(BF16)
        field[second] = doubled(both[8:]).astype(BF16)

    row_bases = sides(par, 0, ROWS, -2)
    col_bases = sides(par, 1, COLS, -2)
    for msg, base in zip((r_even, r_odd), row_bases):
        for k in range(2):
            for p in range(4):
                at = place(base + k, 2 * p)
                spread(msg[k * 4 + p], at, at + 1)
    rows = [0, 1, 2, 3, row_bases[0], row_bases[0] + 1, row_bases[1], row_bases[1] + 1]
    for msg, base in zip((n_even, n_odd), col_bases):
        for j, row in enumerate(rows):
            at = place(row, base)
            spread(msg[j], at, at + 1)

    def product(source, item):
        parts = []
        for m in range(4):
            one = source[table[item * 8 + 2 * m]]
            two = source[table[item * 8 + 2 * m + 1]]
            parts.append(jnp.where(low, one, two))
        picked = jnp.concatenate(parts, 1)
        out = lax.dot_general(
            picked, weight_of(blocks, item), (((1,), (1,)), ((), ())), preferred_element_type=F32
        )
        return unpacked(out)

    outer = outer_places(par)
    for number, (array, index, at) in enumerate(outer):
        got = product(field, OWN + number) + joined(received[array][8 + index])
        middle[at] = doubled(got).astype(BF16)
    for block in range(OWN):
        got = store_first(block, product(field, block))
        middle[place(block // COLS, block % COLS)] = doubled(got).astype(BF16)
    for block in range(OWN):
        store_second(block, product(middle, block))


def forward_one(
    par, table, own, a_even, a_odd, b_even, b_odd, plain, addend, r_even, r_odd, n_even, n_odd, sum1, sum2, sum3, coef,
    field1, field2, addend2, full2, full3, m_even, m_odd, field, middle,
):
    def row(j, block):
        return coef[j, pl.ds(block, 1), :]

    def first(block, out):
        got = out + addend[block]
        field1[block] = got
        full = sum2[block] + row(1, block) * got
        full2[block] = full
        addend2[block] = -row(0, block) * full
        return got

    def second(block, out):
        got = out - row(0, block) * sum1[block]
        field2[block] = got

    forward_pair(
        par, table, (own, (a_even, a_odd, b_even, b_odd)), plain, (r_even, r_odd, n_even, n_odd), addend,
        field, middle, first, second,
    )
    px_message(par, field2, addend2, (m_even, m_odd))
    for block in range(OWN):
        full3[block] = sum3[block] + row(2, block) * field1[block] + row(1, block) * field2[block]


def forward_two(
    par, table, own, a_even, a_odd, b_even, b_odd, plain, addend, r_even, r_odd, n_even, n_odd, full3, coef,
    field3, field4, field, middle,
):
    def first(block, out):
        got = out + addend[block]
        field3[block] = got
        return got

    def second(block, out):
        field4[block] = out - coef[0, pl.ds(block, 1), :] * full3[block]

    forward_pair(
        par, table, (own, (a_even, a_odd, b_even, b_odd)), plain, (r_even, r_odd, n_even, n_odd), addend,
        field, middle, first, second,
    )


def adjoint_pair(par, table, blocks, start, add_first, add_second, outs, middle, last):
    first_out, second_out, m_even, m_odd = outs
    low = low_lanes(16)
    zero = jnp.zeros((16, 128), F32)
    for at in range(PLACES):
        middle[at] = zero
        last[at] = zero

    def push(target, item, rows):
        out = lax.dot_general(
            rows, weight_of(blocks, item), (((1,), (0,)), ((), ())), preferred_element_type=F32
        )
        spots = [table[item * 8 + k] for k in range(8)]
        sums = []
        for k in range(8):
            part = out[:, (k // 2) * 128 : (k // 2 + 1) * 128]
            part = jnp.where(low, part, 0.0) if k % 2 == 0 else jnp.where(low, 0.0, part)
            sums.append(target[spots[k]] + part)
        for k in range(8):
            target[spots[k]] = sums[k]

    def both(target, at):
        value = target[at]
        return value + pltpu.roll(value, 64, 1)

    def plain_of(value):
        return jnp.where(low_lanes(8), value[:8], value[8:])

    for block in range(OWN):
        push(middle, block, packed(start(block)).astype(BF16))
    rows_at = sides(par, 0, ROWS, -1)
    for number, (array, index, at) in enumerate(outer_places(par)):
        value = both(middle, at)
        push(last, OWN + number, value[:, :64].astype(BF16))
    for out, row in zip((m_even, m_odd), rows_at):
        for j in range(COLS + 2):
            out[j] = plain_of(both(middle, place(row, j - 1)))
    for x in range(ROWS):
        for j in range(COLS + 2):
            value = plain_of(both(middle, place(x, j - 1)))
            if 1 <= j <= COLS:
                block = x * COLS + j - 1
                value = value + add_first(block)
                push(last, block, packed(value).astype(BF16))
            first_out[x * (COLS + 2) + j] = value
    for out, base in zip((m_even, m_odd), sides(par, 0, ROWS, -2)):
        for k in range(2):
            for j in range(WIDE):
                out[COLS + 2 + k * WIDE + j] = plain_of(both(last, place(base + k, j - 2)))
    for x in range(ROWS):
        for j in range(WIDE):
            value = plain_of(both(last, place(x, j - 2)))
            if 2 <= j < COLS + 2:
                value = value + add_second(x * COLS + j - 2)
            second_out[x * WIDE + j] = value


def adjoint_py_kernel(par, first, second, r_even, r_odd, first_own, second_own, n_even, n_odd, one, two):
    one[...] = first[...]
    two[...] = second[...]
    for msg, row, base in zip((r_even, r_odd), sides(par, 0, 3, 0), sides(par, 0, 2, 0)):
        for j in range(COLS + 2):
            one[row * (COLS + 2) + j] += msg[j]
        for k in range(2):
            for j in range(WIDE):
                two[(base + k) * WIDE + j] += msg[COLS + 2 + k * WIDE + j]
    for out, col, base in zip((n_even, n_odd), sides(par, 1, COLS + 1, 0), sides(par, 1, COLS + 2, 0)):
        for x in range(ROWS):
            out[x] = one[x * (COLS + 2) + col]
            for k in range(2):
                out[ROWS + 2 * x + k] = two[x * WIDE + base + k]
    for x in range(ROWS):
        for y in range(COLS):
            first_own[x * COLS + y] = one[x * (COLS + 2) + 1 + y]
            second_own[x * COLS + y] = two[x * WIDE + 2 + y]


def settle(par, first_own, second_own, n_even, n_odd, first, second):
    first[...] = first_own[...]
    second[...] = second_own[...]
    for msg, col, base in zip((n_even, n_odd), sides(par, 1, 7, 0), sides(par, 1, 6, 0)):
        for x in range(ROWS):
            first[x * COLS + col] += msg[x]
            for k in range(2):
                second[x * COLS + base + k] += msg[ROWS + 2 * x + k]


def injected(tally, moment, counted, field, spread, block):
    return tally[moment] * counted[block] * field[block] - spread[moment - 1, block]


def adjoint_one(
    par, table, tally, own, a_even, a_odd, b_even, b_odd, field2, field3, field4, counted, spread, coef,
    adjoint4, first_out, second_out, m_even, m_odd, middle, last,
):
    def start(block):
        value = injected(tally, 4, counted, field4, spread, block)
        adjoint4[block] = value
        return value

    def add_first(block):
        return injected(tally, 3, counted, field3, spread, block)

    def add_second(block):
        memory = coef[0, pl.ds(block, 1), :] * coef[1, pl.ds(block, 1), :] * adjoint4[block]
        return injected(tally, 2, counted, field2, spread, block) - memory

    adjoint_pair(
        par, table, (own, (a_even, a_odd, b_even, b_odd)), start, add_first, add_second,
        (first_out, second_out, m_even, m_odd), middle, last,
    )


def adjoint_two(
    par, table, tally, own, a_even, a_odd, b_even, b_odd, first_own, second_own, n_even, n_odd, adjoint4, field1, counted,
    spread, coef, adjoint3, adjoint2, first_out, second_out, m_even, m_odd, middle, last,
):
    settle(par, first_own, second_own, n_even, n_odd, adjoint3, adjoint2)

    def row(j, block):
        return coef[j, pl.ds(block, 1), :]

    def add_first(block):
        memory = row(2, block) * adjoint4[block] + row(1, block) * adjoint3[block]
        return injected(tally, 1, counted, field1, spread, block) - row(0, block) * memory

    def add_second(block):
        memory = row(3, block) * adjoint4[block] + row(2, block) * adjoint3[block] + row(1, block) * adjoint2[block]
        return -row(0, block) * memory

    adjoint_pair(
        par, table, (own, (a_even, a_odd, b_even, b_odd)), lambda block: adjoint2[block], add_first, add_second,
        (first_out, second_out, m_even, m_odd), middle, last,
    )


def finish_kernel(
    par, first_own, second_own, n_even, n_odd, adjoint4, adjoint3, adjoint2, sum0, sum1, sum2, sum3,
    result, gradient, adjoint1, adjoint0, scratch,
):
    settle(par, first_own, second_own, n_even, n_odd, adjoint1, adjoint0)
    for x in range(ROWS):
        parts = []
        for y in range(COLS):
            block = x * COLS + y
            scratch[pl.ds(x * 64 + y * 8, 8), :] = adjoint0[block]
            value = (
                adjoint4[block] * sum3[block] + adjoint3[block] * sum2[block]
                + adjoint2[block] * sum1[block] + adjoint1[block] * sum0[block]
            )
            parts.append(jnp.sum(value, axis=0, keepdims=True))
        rows = jnp.concatenate(parts, 0)
        gradient[x] = -(rows[:, :64] + rows[:, 64:])
        for r in range(8):
            result[x, :, lanes(r)] = scratch[pl.ds(x * 64 + r, 8, stride=8), :]


def split(value):
    high = value.astype(BF16)
    return high, (value - high.astype(F32)).astype(BF16)


def owner_kernel(steps, observed, part, node, out):
    owned = observed.shape[0]
    slots = out.shape[0]
    devices = slots // CAP
    row = lax.broadcasted_iota(jnp.int32, (128, 128), 0)
    col = lax.broadcasted_iota(jnp.int32, (128, 128), 1)
    gate = row // 16
    source = row % 16
    step = jnp.zeros((128, 128), jnp.int32)
    for g in range(8):
        step = jnp.where(gate == g, steps[g], step)
    wanted = 2 * (col % 8) + (col // 8) % 2
    chosen = ((step == col // 16 + 1) & (source == wanted) & (col < 64)).astype(F32).astype(BF16)
    high, low = split(observed[...])
    dot = lambda a, b: lax.dot_general(a, b, (((1,), (0,)), ((), ())), preferred_element_type=F32)
    sums = dot(high, chosen) + dot(low, chosen)
    dest = part[...]
    member = (dest == lax.broadcasted_iota(jnp.int32, (owned, devices), 1)).astype(F32)
    earlier = (
        lax.broadcasted_iota(jnp.int32, (owned, owned), 0) > lax.broadcasted_iota(jnp.int32, (owned, owned), 1)
    ).astype(F32).astype(BF16)
    ahead = dot(earlier, member.astype(BF16))
    rank = jnp.sum(ahead * member, axis=1, keepdims=True).astype(jnp.int32)
    position = dest * CAP + rank
    where = (position == lax.broadcasted_iota(jnp.int32, (owned, slots), 1)).astype(F32).astype(BF16)
    lane = lax.broadcasted_iota(jnp.int32, (owned, 128), 1)
    which = node[...]
    block = (which // 64).astype(F32)
    inner = (which % 64).astype(F32)
    marks = jnp.where(lane == 64, block, jnp.where(lane == 65, inner, jnp.where(lane == 66, 1.0, 0.0)))
    high, low = split(jnp.where(lane < 64, sums, marks))
    turned = lambda a, b: lax.dot_general(a, b, (((0,), (0,)), ((), ())), preferred_element_type=F32)
    out[...] = turned(where, high) + turned(where, low)


def holder_kernel(slots, spread, counted):
    values = slots[...]
    count = values.shape[0]
    lane = lax.broadcasted_iota(jnp.int32, (count, 128), 1)
    pick = lambda at: jnp.sum(jnp.where(lane == at, values, 0.0), axis=1, keepdims=True)
    place_of = jnp.where(pick(66) > 0.5, pick(64) * 64.0 + pick(65), -1.0).astype(jnp.int32)
    high, low = split(values.T)
    both = jnp.concatenate([high, low], 0)
    low8 = low_lanes(8)
    for chunk in range(OWN * 64 // 256):
        spots = lax.broadcasted_iota(jnp.int32, (count, 256), 1) + chunk * 256
        hot = (place_of == spots).astype(F32).astype(BF16)
        out = lax.dot_general(both, hot, (((1,), (0,)), ((), ())), preferred_element_type=F32)
        out = out[:128] + out[128:]
        for j in range(2):
            first = chunk * 4 + 2 * j
            for n in range(4):
                even = out[n * 16 : n * 16 + 8, j * 128 : (j + 1) * 128]
                odd = out[n * 16 + 8 : n * 16 + 16, j * 128 : (j + 1) * 128]
                spread[n, first] = jnp.where(low8, even, pltpu.roll(odd, 64, 1))
                spread[n, first + 1] = jnp.where(low8, pltpu.roll(even, 64, 1), odd)
            many = jnp.broadcast_to(out[66:67, j * 128 : (j + 1) * 128], (8, 128))
            other = pltpu.roll(many, 64, 1)
            counted[first] = jnp.where(low8, many, other)
            counted[first + 1] = jnp.where(low8, other, many)


def swap_even(axis):
    return [(i, i ^ 1) for i in range(lax.axis_size(axis))]


def swap_odd(axis):
    inner = range(1, lax.axis_size(axis) - 1, 2)
    return [(i, i + 1) for i in inner] + [(i + 1, i) for i in inner]


def exchange(axis, for_even, for_odd):
    return lax.ppermute(for_even, axis, swap_even(axis)), lax.ppermute(for_odd, axis, swap_odd(axis))


def edge(array, par, dim, last):
    at = jnp.where(par == 0, last, 0)
    even = lax.dynamic_index_in_dim(array, at, dim, keepdims=False)
    return even, lax.dynamic_index_in_dim(array, last - at, dim, keepdims=False)


def with_corners(array, outer, par):
    sides_own = edge(array, par, 1, COLS - 1)
    ends = [edge(one, par, 0, COLS - 1) for one in outer]
    return tuple(
        jnp.concatenate([own, ends[0][k][None], ends[1][k][None]], 0) for k, own in enumerate(sides_own)
    )


def target_table(offsets, outer, par):
    row_even = jnp.where(par[0] == 0, ROWS, -1)
    row_odd = ROWS - 1 - row_even
    col_even = jnp.where(par[1] == 0, COLS, -1)
    col_odd = COLS - 1 - col_even
    along = jnp.arange(COLS, dtype=jnp.int32)
    down = jnp.concatenate([jnp.arange(ROWS, dtype=jnp.int32), jnp.stack([row_even, row_odd]).astype(jnp.int32)])
    own = place(jnp.arange(ROWS, dtype=jnp.int32)[:, None], along[None, :]).reshape(-1)
    spots = jnp.concatenate(
        [own, place(row_even, along), place(row_odd, along), place(down, col_even), place(down, col_odd)]
    )
    codes = jnp.concatenate([offsets.reshape(OWN, -1)] + list(outer), 0)
    shift = (codes // 3 - 1) * WIDE + codes % 3 - 1
    return (spots[:, None] + shift).reshape(-1).astype(jnp.int32)


def body(
    checkpoint_field,
    checkpoint_memory,
    stiffness,
    block_offsets,
    chargeability,
    relaxation,
    observed,
    receiver_part,
    receiver_node,
    gate_step,
):
    devices = lax.axis_size(("px", "py"))
    slots = devices * CAP
    par = jnp.stack([lax.axis_index("px") % 2, lax.axis_index("py") % 2]).astype(jnp.int32)
    column = ((256, 128), F32)
    places = pltpu.VMEM((PLACES, 16, 128), BF16)
    sums = pltpu.VMEM((PLACES, 16, 128), F32)
    px_shape = ((16, 16, 128), BF16)
    py_shape = ((14, 16, 128), BF16)
    plain, addend, sum0, m_even, m_odd = call(
        start_kernel, [PLAIN, PLAIN, PLAIN, px_shape, px_shape],
        [par, checkpoint_field, checkpoint_memory, chargeability], 1, [pltpu.VMEM(*column)],
    )
    r_even, r_odd = exchange("px", m_even, m_odd)
    a_even, a_odd = exchange("px", *edge(stiffness, par[0], 0, ROWS - 1))
    o_even, o_odd = exchange("px", *edge(block_offsets, par[0], 0, ROWS - 1))
    n_even, n_odd = call(
        py_kernel, [py_shape, py_shape], [par, plain, addend, r_even, r_odd], 1
    )
    n_even, n_odd = exchange("py", n_even, n_odd)
    b_even, b_odd = exchange("py", *with_corners(stiffness, (a_even, a_odd), par[1]))
    c_even, c_odd = exchange("py", *with_corners(block_offsets, (o_even, o_odd), par[1]))
    table = target_table(block_offsets, (o_even, o_odd, c_even, c_odd), par)
    (sent,) = call(
        owner_kernel, [((slots, 128), F32)],
        [gate_step, observed, receiver_part, receiver_node[:, None]], 1,
    )
    held = lax.all_to_all(
        sent.reshape(devices, CAP, 128), ("px", "py"), split_axis=0, concat_axis=0, tiled=True
    ).reshape(slots, 128)
    tally = jnp.sum(gate_step[None, :] == jnp.arange(5, dtype=jnp.int32)[:, None], axis=1).astype(F32)
    sum1, sum2, sum3, coef = call(
        decay_kernel, [PLAIN, PLAIN, PLAIN, ((4, OWN, 128), F32)],
        [checkpoint_field, checkpoint_memory, chargeability, relaxation], 0, [pltpu.VMEM(*column)],
    )
    spread, counted = call(holder_kernel, [((4, OWN, 8, 128), F32), PLAIN], [held])
    weights = [stiffness, a_even, a_odd, b_even, b_odd]
    field1, field2, addend2, sum2, sum3, m_even, m_odd = call(
        forward_one, [PLAIN] * 5 + [px_shape, px_shape],
        [par, table] + weights + [plain, addend, r_even, r_odd, n_even, n_odd, sum1, sum2, sum3, coef],
        2, [places, places],
    )
    r_even, r_odd = exchange("px", m_even, m_odd)
    n_even, n_odd = call(py_kernel, [py_shape, py_shape], [par, field2, addend2, r_even, r_odd], 1)
    n_even, n_odd = exchange("py", n_even, n_odd)
    field3, field4 = call(
        forward_two, [PLAIN, PLAIN],
        [par, table] + weights + [field2, addend2, r_even, r_odd, n_even, n_odd, sum3, coef],
        2, [places, places],
    )
    pair_out = [
        ((ROWS * (COLS + 2), 8, 128), F32), ((ROWS * WIDE, 8, 128), F32),
        ((COLS + 2 + 2 * WIDE, 8, 128), F32), ((COLS + 2 + 2 * WIDE, 8, 128), F32),
    ]

    def gathered(first, second, m_even, m_odd):
        r_even, r_odd = exchange("px", m_even, m_odd)
        own_first, own_second, n_even, n_odd = call(
            adjoint_py_kernel, [PLAIN, PLAIN, ((12, 8, 128), F32), ((12, 8, 128), F32)],
            [par, first, second, r_even, r_odd], 1,
            [pltpu.VMEM(first.shape, F32), pltpu.VMEM(second.shape, F32)],
        )
        n_even, n_odd = exchange("py", n_even, n_odd)
        return [own_first, own_second, n_even, n_odd]

    adjoint4, *rest = call(
        adjoint_one, [PLAIN] + pair_out,
        [par, table, tally] + weights + [field2, field3, field4, counted, spread, coef], 3, [sums, sums],
    )
    adjoint3, adjoint2, *rest = call(
        adjoint_two, [PLAIN, PLAIN] + pair_out,
        [par, table, tally] + weights + gathered(*rest) + [adjoint4, field1, counted, spread, coef], 3, [sums, sums],
    )
    field_out, gradient = call(
        finish_kernel, [(checkpoint_field.shape, F32), (chargeability.shape, F32)],
        [par] + gathered(*rest) + [adjoint4, adjoint3, adjoint2, sum0, sum1, sum2, sum3], 1,
        [pltpu.VMEM(*PLAIN), pltpu.VMEM(*PLAIN), pltpu.VMEM(*column)],
    )
    return field_out, gradient


def solution(mesh):
    in_specs = (
        P("px", "py", None),
        P(None, "px", "py", None),
        P("px", "py", None, None),
        P("px", "py", None),
        P("px", "py", None),
        P(None, "px", "py", None),
        P(("px", "py"), None),
        P(("px", "py"), None),
        P(("px", "py")),
        P(),
    )
    out_specs = (P("px", "py", None), P("px", "py", None))
    return jax.shard_map(body, mesh=mesh, in_specs=in_specs, out_specs=out_specs, check_vma=False)
```

```python
import jax
import jax.numpy as jnp
from jax import lax
from jax.experimental import pallas as pl
from jax.experimental.pallas import tpu as pltpu
from jax.sharding import PartitionSpec as P

ROWS, COLS = 4, 8
OWN = ROWS * COLS
CAP = 8
WIDE = COLS + 4
PLACES = (ROWS + 4) * WIDE
F32, BF16 = jnp.float32, jnp.bfloat16
VMEM_BYTES = 16 * 1024 * 1024
NODE, WIDTH = 64, 512
FIELD, ADDEND, SUM0, SUM1, SUM2, SUM3, COEF = (i * OWN for i in range(7))
PX_BASE, PY_BASE = COLS * NODE, (ROWS + 2) * NODE


def place(row, col):
    return (row + 2) * WIDE + col + 2


def low_lanes(rows):
    return lax.broadcasted_iota(jnp.int32, (rows, 128), 1) < 64


def doubled(plain):
    turned = pltpu.roll(plain, 64, 1)
    low = low_lanes(8)
    return jnp.concatenate([jnp.where(low, plain, turned), jnp.where(low, turned, plain)], 0)


def packed(plain):
    return jnp.concatenate([plain[:, :64], plain[:, 64:]], 0)


def unpacked(rows):
    return jnp.concatenate([rows[:8], rows[8:]], 1)


def halves(plain):
    high = plain.astype(BF16).astype(F32)
    return jnp.concatenate([high, plain - high], 0).astype(BF16)


def joined(pair):
    pair = pair.astype(F32)
    return pair[:8] + pair[8:]


def sides(par_ref, axis, near, far):
    even = par_ref[axis] == 0
    return jnp.where(even, near, far), jnp.where(even, far, near)


class Flow:
    def __init__(self, sems):
        self.sems, self.used, self.coming, self.going = sems, 0, {}, []

    def copy(self, source, target):
        made = pltpu.make_async_copy(source, target, self.sems.at[self.used])
        self.used += 1
        made.start()
        return made

    def wait(self, *refs):
        for ref in refs:
            for made in self.coming.pop(id(ref), ()):
                made.wait()

    def send(self, source, target):
        self.going.append(self.copy(source, target))

    def finish(self):
        for key in list(self.coming):
            for made in self.coming.pop(key):
                made.wait()
        for made in self.going:
            made.wait()


def call(kernel, outs, inputs, scratch=(), copies=0):
    spaces = {"s": pltpu.SMEM, "v": pltpu.VMEM, "h": pltpu.HBM, "b": pltpu.HBM}
    arrays = [array for array, _ in inputs]
    fetched = [i for i, (_, kind) in enumerate(inputs) if kind == "h"]
    total = len(fetched) + copies

    def wrapped(*refs):
        refs = list(refs)
        buffers = refs[len(inputs) + len(outs) + len(scratch) :]
        flow = Flow(buffers[-1])
        for buffer, i in zip(buffers, fetched):
            flow.coming[id(buffer)] = [flow.copy(refs[i], buffer)]
            refs[i] = buffer
        kernel(flow, *refs[: len(inputs) + len(outs) + len(scratch)])
        flow.finish()

    buffers = [pltpu.VMEM(arrays[i].shape, arrays[i].dtype) for i in fetched]
    return pl.pallas_call(
        wrapped,
        out_shape=[jax.ShapeDtypeStruct(shape, dtype) for shape, dtype, _ in outs],
        in_specs=[pl.BlockSpec(memory_space=spaces[kind]) for _, kind in inputs],
        out_specs=[pl.BlockSpec(memory_space=spaces[kind]) for _, _, kind in outs],
        scratch_shapes=list(scratch) + buffers + [pltpu.SemaphoreType.DMA((max(total, 1),))],
        compiler_params=pltpu.CompilerParams(vmem_limit_bytes=VMEM_BYTES),
    )(*arrays)


PLAIN = ((OWN, 8, 128), F32, "v")


class Tiles:
    def __init__(self, ref, base=None):
        self.ref, self.base = ref, base

    def at(self, t):
        if self.base is None:
            return (t,)
        return pl.ds(self.base + 16 * (t // 4), 16), pl.ds(128 * (t % 4), 128)

    def __getitem__(self, t):
        return self.ref[self.at(t)]

    def __setitem__(self, t, value):
        self.ref[self.at(t)] = value


def to_plain(native, scratch, out):
    for x in range(ROWS):
        for r in range(8):
            scratch[pl.ds(x * 64 + r * 8, 8), :] = native(x, r)
    for x in range(ROWS):
        for y in range(COLS):
            out[x * COLS + y] = scratch[pl.ds(x * 64 + y, 8, stride=8), :]


def lanes(r):
    return pl.ds(r * 128, 128)


def twice(rows):
    return jnp.concatenate([rows, rows], 1)


def px_message(par, plain, addend, outs):
    bases = sides(par, 0, 2, 0)
    edges = sides(par, 0, 3, 0)
    for out, base, edge in zip(outs, bases, edges):
        for k in range(2):
            for p in range(4):
                at = (base + k) * COLS + 2 * p
                out[k * 4 + p] = jnp.concatenate([plain(at), plain(at + 1)], 0).astype(BF16)
        for y in range(COLS):
            out[8 + y] = halves(addend(edge * COLS + y))


def py_message(par, plain, addend, outs):
    pairs = sides(par, 1, 3, 0)
    edges = sides(par, 1, 7, 0)
    for out, pair, edge in zip(outs, pairs, edges):
        for x in range(ROWS):
            at = x * COLS + 2 * pair
            out[x] = jnp.concatenate([plain(at), plain(at + 1)], 0).astype(BF16)
            out[8 + x] = halves(addend(x * COLS + edge))


def picked_tile(tiles, choice, low, high):
    return jnp.where(choice == 0, tiles[low].astype(F32), tiles[high].astype(F32)).astype(BF16)


def py_fill(par, r_even, r_odd, outs):
    edges = sides(par, 1, 7, 0)
    for out, edge in zip(outs, edges):
        for k in range(2):
            out[4 + k] = picked_tile(r_even, edge, k * 4, k * 4 + 3)
            out[6 + k] = picked_tile(r_odd, edge, k * 4, k * 4 + 3)
        out[12] = picked_tile(r_even, edge, 8, 15)
        out[13] = picked_tile(r_odd, edge, 8, 15)


def shift_lines(offsets):
    row = lax.broadcasted_iota(jnp.int32, (8, 128), 0)
    lane = lax.broadcasted_iota(jnp.int32, (8, 128), 1)
    repeat = ((lane % 8 == row) & (lane < 64)).astype(F32).astype(BF16)
    lines = jnp.zeros((8, 128), F32)
    for x in range(ROWS):
        codes = offsets[x].astype(F32).astype(BF16)
        wide = lax.dot_general(codes, repeat, (((1,), (0,)), ((), ())), preferred_element_type=F32)
        line = jnp.sum(jnp.where(lane // 8 == row, wide, 0.0), axis=0, keepdims=True)
        lines = jnp.where(row == x, line, lines)
    above = (lines > 2.5).astype(F32) + (lines > 5.5).astype(F32)
    return 9.0 * above + lines - 13.0


def start_kernel(
    flow, par, field, memory, charge, offsets, stiffness, m_even, m_odd, n_even, n_odd, lines, plain, addend, scratch
):
    for out, edge in zip((m_even, m_odd), sides(par, 0, ROWS - 1, 0)):
        for y in range(COLS):
            flow.send(stiffness.at[edge, y], out.at[pl.ds(y * NODE, NODE), :])
    for out, edge in zip((n_even, n_odd), sides(par, 1, COLS - 1, 0)):
        for x in range(ROWS):
            flow.send(stiffness.at[x, edge], out.at[pl.ds(x * NODE, NODE), :])
    flow.wait(offsets)
    found = shift_lines(offsets)
    lines[...] = found
    px_tiles = [Tiles(m_even, PX_BASE), Tiles(m_odd, PX_BASE)]
    py_tiles = [Tiles(n_even, PY_BASE), Tiles(n_odd, PY_BASE)]
    for out, edge in zip(px_tiles, sides(par, 0, ROWS - 1, 0)):
        line = jnp.where(edge == 0, found[0:1], found[ROWS - 1 : ROWS])
        out[16] = jnp.broadcast_to(line, (16, 128)).astype(BF16)
    for out in py_tiles:
        out[14] = jnp.concatenate([found, jnp.zeros((8, 128), F32)], 0).astype(BF16)
    flow.wait(field, memory, charge)
    terms = memory.shape[0]
    to_plain(lambda x, r: field[x, :, lanes(r)], scratch, plain)

    def total(x, r):
        acc = memory[0, x, :, lanes(r)]
        for q in range(1, terms):
            acc = acc + memory[q, x, :, lanes(r)]
        return acc * -twice(charge[x])

    to_plain(total, scratch, addend)
    get, add = (lambda at: plain[at]), (lambda at: addend[at])
    px_message(par, get, add, px_tiles)
    py_message(par, get, add, py_tiles)


def first_py_kernel(flow, par, r_even, r_odd, in_even, in_odd, n_even, n_odd):
    n_even[...] = in_even[...]
    n_odd[...] = in_odd[...]
    tiles = [Tiles(r_even, PX_BASE), Tiles(r_odd, PX_BASE)]
    outs = [Tiles(n_even, PY_BASE), Tiles(n_odd, PY_BASE)]
    py_fill(par, tiles[0], tiles[1], outs)
    row = lax.broadcasted_iota(jnp.int32, (16, 128), 0)
    for out, source, edge in zip((n_even, n_odd), (in_even, in_odd), sides(par, 1, COLS - 1, 0)):
        for k, got in enumerate((r_even, r_odd)):
            out[pl.ds((ROWS + k) * NODE, NODE), :] = got[pl.ds(edge * NODE, NODE), :]
    for out, source in zip(outs, (Tiles(in_even, PY_BASE), Tiles(in_odd, PY_BASE))):
        even, odd = tiles[0][16].astype(F32), tiles[1][16].astype(F32)
        own = source[14].astype(F32)
        out[14] = jnp.where(row == ROWS, even, jnp.where(row == ROWS + 1, odd, own)).astype(BF16)


def second_py_kernel(flow, par, r_even, r_odd, in_even, in_odd, n_even, n_odd):
    n_even[...] = in_even[...]
    n_odd[...] = in_odd[...]
    py_fill(par, Tiles(r_even), Tiles(r_odd), (Tiles(n_even), Tiles(n_odd)))


def decay_kernel(flow, after, field, memory, charge, relaxation, out, full, scratch):
    terms = memory.shape[0]
    flow.wait(field, memory, charge, relaxation)
    wide = [twice(charge[x]) for x in range(ROWS)]
    rates = [[twice(relaxation[q, x]) for q in range(terms)] for x in range(ROWS)]
    coefs = []
    for x in range(ROWS):
        w0 = w1 = w2 = 0.0
        for rate in rates[x]:
            w0 = w0 + (1.0 - rate)
            w1 = w1 + rate * (1.0 - rate)
            w2 = w2 + rate * rate * (1.0 - rate)
        coefs.append((wide[x], w0, w1, w2))
        for j in range(4):
            full[COEF + j * ROWS + x] = coefs[x][j]

    def region(base):
        return full.at[pl.ds(base, OWN)]

    def total(x, r):
        acc = memory[0, x, :, lanes(r)]
        for q in range(1, terms):
            acc = acc + memory[q, x, :, lanes(r)]
        return acc

    to_plain(lambda x, r: field[x, :, lanes(r)], scratch, region(FIELD))
    to_plain(total, scratch, region(SUM0))
    to_plain(lambda x, r: total(x, r) * -wide[x], scratch, region(ADDEND))
    for power, base in ((1, SUM1), (2, SUM2), (3, SUM3)):
        scale = [[rate if power == 1 else rate * rate if power == 2 else rate * rate * rate for rate in row] for row in rates]

        def part(x, r):
            acc = coefs[x][power] * field[x, :, lanes(r)]
            for q in range(terms):
                acc = acc + scale[x][q] * memory[q, x, :, lanes(r)]
            return acc

        to_plain(part, scratch, region(base))
    flow.send(full, out)


class Coefs:
    def __init__(self, ref):
        self.ref = ref

    def __call__(self, j, block):
        return self.ref[j * ROWS + block // COLS, pl.ds(block % COLS, 1), :]


def outer_places(par):
    row_even, row_odd = sides(par, 0, ROWS, -1)
    col_even, col_odd = sides(par, 1, COLS, -1)
    listed = []
    for array, row in ((0, row_even), (1, row_odd)):
        listed += [(array, y, place(row, y)) for y in range(COLS)]
    rows = [0, 1, 2, 3, row_even, row_odd]
    for array, col in ((2, col_even), (3, col_odd)):
        listed += [(array, j, place(row, col)) for j, row in enumerate(rows)]
    return listed


def weight_of(blocks, item):
    own, r_even, r_odd, n_even, n_odd = blocks
    if item < OWN:
        return own[item // COLS, item % COLS]
    item -= OWN
    for array, count in ((r_even, COLS), (r_odd, COLS), (n_even, ROWS + 2), (n_odd, ROWS + 2)):
        if item < count:
            return array[pl.ds(item * NODE, NODE), :]
        item -= count


def targets_of(table, par):
    columns = sides(par, 1, 0, COLS - 1)

    def target(item, k):
        if item < OWN + 2 * COLS:
            return table[item // COLS, (item % COLS) * 8 + k]
        item -= OWN + 2 * COLS
        side, j = item // (ROWS + 2), item % (ROWS + 2)
        return table[8 * (side + 1) + j, columns[side] * 8 + k]

    return target


def table_lines(par, lines, r_even, r_odd, n_even, n_odd):
    row = lax.broadcasted_iota(jnp.int32, (8, 128), 0)
    lane = lax.broadcasted_iota(jnp.int32, (8, 128), 1)
    row_even, row_odd = sides(par, 0, ROWS, -1)
    line = jnp.where(row == ROWS, row_even, jnp.where(row == ROWS + 1, row_odd, row))
    even = Tiles(r_even, PX_BASE)[16].astype(F32)[:8]
    odd = Tiles(r_odd, PX_BASE)[16].astype(F32)[:8]
    first = jnp.where(row == ROWS, even, jnp.where(row == ROWS + 1, odd, lines))
    parts = [first.astype(jnp.int32) + place(line, lane // 8)]
    for msg, col in zip((n_even, n_odd), sides(par, 1, COLS, -1)):
        parts.append(Tiles(msg, PY_BASE)[14].astype(F32)[:8].astype(jnp.int32) + place(line, col))
    return jnp.concatenate(parts, 0)


def forward_pair(par, target, ready, blocks, plain, received, field, middle, store_first, store_second):
    low = low_lanes(16)
    r_even, r_odd, n_even, n_odd = received

    def spread(pair, first, second):
        both = pair.astype(F32)
        field[first] = doubled(both[:8]).astype(BF16)
        field[second] = doubled(both[8:]).astype(BF16)

    row_bases = sides(par, 0, ROWS, -2)
    col_bases = sides(par, 1, COLS, -2)
    for msg, base in zip((r_even, r_odd), row_bases):
        for k in range(2):
            for p in range(4):
                at = place(base + k, 2 * p)
                spread(msg[k * 4 + p], at, at + 1)
    rows = [0, 1, 2, 3, row_bases[0], row_bases[0] + 1, row_bases[1], row_bases[1] + 1]
    for msg, base in zip((n_even, n_odd), col_bases):
        for j, row in enumerate(rows):
            at = place(row, base)
            spread(msg[j], at, at + 1)
    ready()
    for block in range(OWN):
        field[place(block // COLS, block % COLS)] = doubled(plain(block)).astype(BF16)

    def product(source, item):
        parts = []
        for m in range(4):
            one = source[target(item, 2 * m)]
            two = source[target(item, 2 * m + 1)]
            parts.append(jnp.where(low, one, two))
        picked = jnp.concatenate(parts, 1)
        out = lax.dot_general(
            picked, weight_of(blocks, item), (((1,), (1,)), ((), ())), preferred_element_type=F32
        )
        return unpacked(out)

    for number, (array, index, at) in enumerate(outer_places(par)):
        got = product(field, OWN + number) + joined(received[array][8 + index])
        middle[at] = doubled(got).astype(BF16)
    for block in range(OWN):
        got = store_first(block, product(field, block))
        middle[place(block // COLS, block % COLS)] = doubled(got).astype(BF16)
    for block in range(OWN):
        store_second(block, product(middle, block))


def forward_one(
    flow, par, lines, own, r_even, r_odd, n_even, n_odd, known, past, now, m_even, m_odd, p_even, p_odd, table_out,
    field, middle, table, codes, older,
):
    table_out[...] = table_lines(par, lines[...], r_even, r_odd, n_even, n_odd)
    looked = flow.copy(table_out, table)
    coef = Coefs(known.at[pl.ds(COEF, 4 * ROWS)])

    def ready():
        looked.wait()
        flow.wait(known)

    def first(block, out):
        got = out + known[ADDEND + block]
        older[block] = got
        full = known[SUM2 + block] + coef(1, block) * got
        older[OWN + block] = full
        now[OWN + block] = -coef(0, block) * full
        if block == OWN - 1:
            flow.send(older, past)
        return got

    def second(block, out):
        now[block] = out - coef(0, block) * known[SUM1 + block]

    received = (Tiles(r_even, PX_BASE), Tiles(r_odd, PX_BASE), Tiles(n_even, PY_BASE), Tiles(n_odd, PY_BASE))
    forward_pair(
        par, targets_of(table, par), ready, (own, r_even, r_odd, n_even, n_odd), lambda block: known[FIELD + block],
        received, field, middle, first, second,
    )
    get, add = (lambda at: now[at]), (lambda at: now[OWN + at])
    px_message(par, get, add, (Tiles(m_even), Tiles(m_odd)))
    py_message(par, get, add, (Tiles(p_even), Tiles(p_odd)))
    for block in range(OWN):
        now[2 * OWN + block] = known[SUM3 + block] + coef(2, block) * older[block] + coef(1, block) * now[block]


def turn_kernel(
    flow, par, table, tally, own, r_even, r_odd, n_even, n_odd, e_even, e_odd, s_even, s_odd, now, coefs, spread, counted,
    adjoint4, first_out, second_out, m_even, m_odd, field, middle, sums_one, sums_two, field3, field4, start_out,
):
    blocks = (own, r_even, r_odd, n_even, n_odd)
    target = targets_of(table, par)
    coef = Coefs(coefs)

    def first(block, out):
        got = out + now[OWN + block]
        field3[block] = got
        return got

    def second(block, out):
        field4[block] = out - coef(0, block) * now[2 * OWN + block]

    received = (Tiles(e_even), Tiles(e_odd), Tiles(s_even), Tiles(s_odd))
    clear(sums_one, sums_two)
    forward_pair(
        par, target, lambda: flow.wait(coefs), blocks, lambda block: now[block], received, field, middle, first, second
    )
    flow.wait(spread, counted)

    def start(block):
        value = injected(tally, 4, counted, field4[block], spread, block)
        start_out[block] = value
        if block == OWN - 1:
            flow.send(start_out, adjoint4)
        return value

    def add_first(block):
        return injected(tally, 3, counted, field3[block], spread, block)

    def add_second(block):
        memory = coef(0, block) * coef(1, block) * start_out[block]
        return injected(tally, 2, counted, now[block], spread, block) - memory

    adjoint_pair(
        par, target, blocks, start, add_first, add_second, (first_out, second_out, m_even, m_odd), sums_one, sums_two
    )


def clear(*refs):
    for ref in refs:
        zero = jnp.zeros(ref.shape[1:], F32)
        for at in range(ref.shape[0]):
            ref[at] = zero


def adjoint_pair(par, target, blocks, start, add_first, add_second, outs, middle, last):
    first_out, second_out, m_even, m_odd = outs
    low = low_lanes(16)

    def push(sums_ref, item, rows):
        out = lax.dot_general(
            rows, weight_of(blocks, item), (((1,), (0,)), ((), ())), preferred_element_type=F32
        )
        spots = [target(item, k) for k in range(8)]
        sums = []
        for k in range(8):
            part = out[:, (k // 2) * 128 : (k // 2 + 1) * 128]
            part = jnp.where(low, part, 0.0) if k % 2 == 0 else jnp.where(low, 0.0, part)
            sums.append(sums_ref[spots[k]] + part)
        for k in range(8):
            sums_ref[spots[k]] = sums[k]

    def both(sums_ref, at):
        value = sums_ref[at]
        return value + pltpu.roll(value, 64, 1)

    def plain_of(value):
        return jnp.where(low_lanes(8), value[:8], value[8:])

    for block in range(OWN):
        push(middle, block, packed(start(block)).astype(BF16))
    rows_at = sides(par, 0, ROWS, -1)
    for number, (array, index, at) in enumerate(outer_places(par)):
        value = both(middle, at)
        push(last, OWN + number, value[:, :64].astype(BF16))
    for out, row in zip((m_even, m_odd), rows_at):
        for j in range(COLS + 2):
            out[j] = plain_of(both(middle, place(row, j - 1)))
    for x in range(ROWS):
        for j in range(COLS + 2):
            value = plain_of(both(middle, place(x, j - 1)))
            if 1 <= j <= COLS:
                block = x * COLS + j - 1
                value = value + add_first(block)
                push(last, block, packed(value).astype(BF16))
            first_out[x * (COLS + 2) + j] = value
    for out, base in zip((m_even, m_odd), sides(par, 0, ROWS, -2)):
        for k in range(2):
            for j in range(WIDE):
                out[COLS + 2 + k * WIDE + j] = plain_of(both(last, place(base + k, j - 2)))
    for x in range(ROWS):
        for j in range(WIDE):
            value = plain_of(both(last, place(x, j - 2)))
            if 2 <= j < COLS + 2:
                value = value + add_second(x * COLS + j - 2)
            second_out[x * WIDE + j] = value


def adjoint_py_kernel(flow, par, first, second, r_even, r_odd, first_own, second_own, n_even, n_odd, one, two):
    one[...] = first[...]
    two[...] = second[...]
    for msg, row, base in zip((r_even, r_odd), sides(par, 0, 3, 0), sides(par, 0, 2, 0)):
        for j in range(COLS + 2):
            one[row * (COLS + 2) + j] += msg[j]
        for k in range(2):
            for j in range(WIDE):
                two[(base + k) * WIDE + j] += msg[COLS + 2 + k * WIDE + j]
    for out, col, base in zip((n_even, n_odd), sides(par, 1, COLS + 1, 0), sides(par, 1, COLS + 2, 0)):
        for x in range(ROWS):
            out[x] = one[x * (COLS + 2) + col]
            for k in range(2):
                out[ROWS + 2 * x + k] = two[x * WIDE + base + k]
    for x in range(ROWS):
        for y in range(COLS):
            first_own[x * COLS + y] = one[x * (COLS + 2) + 1 + y]
            second_own[x * COLS + y] = two[x * WIDE + 2 + y]


def settle(par, first_own, second_own, n_even, n_odd, first, second):
    first[...] = first_own[...]
    second[...] = second_own[...]
    for msg, col, base in zip((n_even, n_odd), sides(par, 1, 7, 0), sides(par, 1, 6, 0)):
        for x in range(ROWS):
            first[x * COLS + col] += msg[x]
            for k in range(2):
                second[x * COLS + base + k] += msg[ROWS + 2 * x + k]


def injected(tally, moment, counted, field, spread, block):
    return tally[moment] * counted[block] * field - spread[moment - 1, block]


def adjoint_two(
    flow, par, table, tally, own, r_even, r_odd, n_even, n_odd, first_own, second_own, e_even, e_odd, adjoint4, past, coefs,
    spread, counted, later, first_out, second_out, m_even, m_odd, sums_one, sums_two, adjoint3, adjoint2,
):
    clear(sums_one, sums_two)
    settle(par, first_own, second_own, e_even, e_odd, adjoint3, adjoint2)
    flow.send(adjoint3, later.at[pl.ds(0, OWN)])
    flow.send(adjoint2, later.at[pl.ds(OWN, OWN)])
    coef = Coefs(coefs)

    def add_first(block):
        if block == 0:
            flow.wait(adjoint4, past, coefs, spread, counted)
        memory = coef(2, block) * adjoint4[block] + coef(1, block) * adjoint3[block]
        return injected(tally, 1, counted, past[block], spread, block) - coef(0, block) * memory

    def add_second(block):
        memory = coef(3, block) * adjoint4[block] + coef(2, block) * adjoint3[block] + coef(1, block) * adjoint2[block]
        return -coef(0, block) * memory

    adjoint_pair(
        par, targets_of(table, par), (own, r_even, r_odd, n_even, n_odd), lambda block: adjoint2[block], add_first,
        add_second, (first_out, second_out, m_even, m_odd), sums_one, sums_two,
    )


def gradient_kernel(flow, after, adjoint4, later, known, past, now, out):
    flow.wait(adjoint4, later, known, past, now)
    for block in range(OWN):
        out[block] = (
            adjoint4[block] * now[2 * OWN + block] + later[block] * past[OWN + block]
            + later[OWN + block] * known[SUM1 + block]
        )
        out[OWN + block] = known[SUM0 + block]


def finish_kernel(
    flow, par, first_own, second_own, n_even, n_odd, before, result, gradient, adjoint1, adjoint0, scratch
):
    settle(par, first_own, second_own, n_even, n_odd, adjoint1, adjoint0)
    for x in range(ROWS):
        parts = []
        for y in range(COLS):
            block = x * COLS + y
            scratch[pl.ds(x * 64 + y * 8, 8), :] = adjoint0[block]
            value = before[block] + adjoint1[block] * before[OWN + block]
            parts.append(jnp.sum(value, axis=0, keepdims=True))
        rows = jnp.concatenate(parts, 0)
        gradient[x] = -(rows[:, :64] + rows[:, 64:])
        for r in range(8):
            result[x, :, lanes(r)] = scratch[pl.ds(x * 64 + r, 8, stride=8), :]


def split(value):
    high = value.astype(BF16)
    return high, (value - high.astype(F32)).astype(BF16)


def owner_kernel(flow, steps, after, observed, part, node, out, slots_of):
    flow.wait(observed, part, node)
    owned = observed.shape[0]
    slots = out.shape[0]
    devices = slots // CAP
    row = lax.broadcasted_iota(jnp.int32, (128, 128), 0)
    col = lax.broadcasted_iota(jnp.int32, (128, 128), 1)
    gate = row // 16
    source = row % 16
    step = jnp.zeros((128, 128), jnp.int32)
    for g in range(8):
        step = jnp.where(gate == g, steps[g], step)
    wanted = 2 * (col % 8) + (col // 8) % 2
    chosen = ((step == col // 16 + 1) & (source == wanted) & (col < 64)).astype(F32).astype(BF16)
    high, low = split(observed[...])
    dot = lambda a, b: lax.dot_general(a, b, (((1,), (0,)), ((), ())), preferred_element_type=F32)
    sums = dot(high, chosen) + dot(low, chosen)
    dest = part[...]
    member = (dest == lax.broadcasted_iota(jnp.int32, (devices, owned), 0)).astype(F32)
    earlier = (
        lax.broadcasted_iota(jnp.int32, (owned, owned), 0) < lax.broadcasted_iota(jnp.int32, (owned, owned), 1)
    ).astype(F32).astype(BF16)
    ahead = dot(member.astype(BF16), earlier)
    rank = jnp.sum(ahead * member, axis=0, keepdims=True).astype(jnp.int32)
    position = dest * CAP + rank
    where = (position == lax.broadcasted_iota(jnp.int32, (slots, owned), 0)).astype(F32).astype(BF16)
    line = lax.broadcasted_iota(jnp.int32, (128, owned), 0)
    which = node[...]
    block = lax.shift_right_logical(which, 6)
    inner = which - block * 64
    marks = jnp.where(line == 64, block, jnp.where(line == 65, inner, jnp.where(line == 66, 1, 0)))
    high, low = split(sums)
    turned = lambda a, b: lax.dot_general(a, b, (((1,), (1,)), ((), ())), preferred_element_type=F32)
    slots_of[...] = dot(where, high) + dot(where, low) + turned(where, marks.astype(F32).astype(BF16))
    flow.send(slots_of, out)


def holder_kernel(flow, slots, spread_out, counted_out, spread, counted):
    flow.wait(slots)
    values = slots[...]
    count = values.shape[0]
    lane = lax.broadcasted_iota(jnp.int32, (count, 128), 1)
    pick = lambda at: jnp.sum(jnp.where(lane == at, values, 0.0), axis=1, keepdims=True)
    place_of = jnp.where(pick(66) > 0.5, pick(64) * 64.0 + pick(65), -1.0).astype(jnp.int32)
    high, low = split(values.T)
    both = jnp.concatenate([high, low], 0)
    low8 = low_lanes(8)
    for chunk in range(OWN * 64 // 256):
        spots = lax.broadcasted_iota(jnp.int32, (count, 256), 1) + chunk * 256
        hot = (place_of == spots).astype(F32).astype(BF16)
        out = lax.dot_general(both, hot, (((1,), (0,)), ((), ())), preferred_element_type=F32)
        out = out[:128] + out[128:]
        for j in range(2):
            first = chunk * 4 + 2 * j
            for n in range(4):
                even = out[n * 16 : n * 16 + 8, j * 128 : (j + 1) * 128]
                odd = out[n * 16 + 8 : n * 16 + 16, j * 128 : (j + 1) * 128]
                spread[n, first] = jnp.where(low8, even, pltpu.roll(odd, 64, 1))
                spread[n, first + 1] = jnp.where(low8, pltpu.roll(even, 64, 1), odd)
            many = jnp.broadcast_to(out[66:67, j * 128 : (j + 1) * 128], (8, 128))
            other = pltpu.roll(many, 64, 1)
            counted[first] = jnp.where(low8, many, other)
            counted[first + 1] = jnp.where(low8, other, many)
    flow.send(spread, spread_out)
    flow.send(counted, counted_out)


def swap_even(axis):
    return [(i, i ^ 1) for i in range(lax.axis_size(axis))]


def swap_odd(axis):
    inner = range(1, lax.axis_size(axis) - 1, 2)
    return [(i, i + 1) for i in inner] + [(i + 1, i) for i in inner]


def exchange(axis, for_even, for_odd):
    return lax.ppermute(for_even, axis, swap_even(axis)), lax.ppermute(for_odd, axis, swap_odd(axis))


def body(
    checkpoint_field,
    checkpoint_memory,
    stiffness,
    block_offsets,
    chargeability,
    relaxation,
    observed,
    receiver_part,
    receiver_node,
    gate_step,
):
    devices = lax.axis_size(("px", "py"))
    slots = devices * CAP
    par = jnp.stack([lax.axis_index("px") % 2, lax.axis_index("py") % 2]).astype(jnp.int32)
    turn = pltpu.VMEM((256, 128), F32)
    places = pltpu.VMEM((PLACES, 16, 128), BF16)
    sums = pltpu.VMEM((PLACES, 16, 128), F32)
    blocks = pltpu.VMEM((OWN, 8, 128), F32)
    px_first = ((PX_BASE + 80, WIDTH), BF16, "v")
    py_first = ((PY_BASE + 64, WIDTH), BF16, "v")
    px_shape = ((16, 16, 128), BF16, "v")
    py_shape = ((14, 16, 128), BF16, "v")
    m_even, m_odd, p_even, p_odd, lines = call(
        start_kernel, [px_first, px_first, py_first, py_first, ((8, 128), F32, "v")],
        [
            (par, "s"), (checkpoint_field, "h"), (checkpoint_memory, "h"), (chargeability, "h"), (block_offsets, "h"),
            (stiffness, "b"),
        ],
        [blocks, blocks, turn], copies=2 * COLS + 2 * ROWS,
    )
    r_even, r_odd = exchange("px", m_even, m_odd)
    (known,) = call(
        decay_kernel, [((COEF + 4 * ROWS, 8, 128), F32, "h")],
        [(lines, "v"), (checkpoint_field, "h"), (checkpoint_memory, "h"), (chargeability, "h"), (relaxation, "h")],
        [pltpu.VMEM((COEF + 4 * ROWS, 8, 128), F32), turn], copies=1,
    )
    (sent,) = call(
        owner_kernel, [((slots, 128), F32, "h")],
        [
            (gate_step, "s"), (r_even, "v"), (observed, "h"), (receiver_part.reshape(1, -1), "h"),
            (receiver_node.reshape(1, -1), "h"),
        ],
        [pltpu.VMEM((slots, 128), F32)], copies=1,
    )
    held = lax.all_to_all(
        sent.reshape(devices, CAP, 128), ("px", "py"), split_axis=0, concat_axis=0, tiled=True
    ).reshape(slots, 128)
    n_even, n_odd = call(
        first_py_kernel, [py_first, py_first],
        [(par, "s"), (r_even, "v"), (r_odd, "v"), (p_even, "v"), (p_odd, "v")],
    )
    n_even, n_odd = exchange("py", n_even, n_odd)
    tally = jnp.sum(gate_step[None, :] == jnp.arange(5, dtype=jnp.int32)[:, None], axis=1).astype(F32)
    weights = [(a, "v") for a in (stiffness, r_even, r_odd, n_even, n_odd)]
    past, now, m_even, m_odd, p_even, p_odd, table = call(
        forward_one,
        [
            ((2 * OWN, 8, 128), F32, "h"), ((3 * OWN, 8, 128), F32, "v"), px_shape, px_shape, py_shape, py_shape,
            ((24, 128), jnp.int32, "v"),
        ],
        [(par, "s"), (lines, "v")] + weights + [(known, "h")],
        [places, places, pltpu.SMEM((24, 128), jnp.int32), pltpu.VMEM((8, 128), F32), pltpu.VMEM((2 * OWN, 8, 128), F32)],
        copies=2,
    )
    r_even, r_odd = exchange("px", m_even, m_odd)
    n_even, n_odd = call(
        second_py_kernel, [py_shape, py_shape],
        [(par, "s"), (r_even, "v"), (r_odd, "v"), (p_even, "v"), (p_odd, "v")],
    )
    n_even, n_odd = exchange("py", n_even, n_odd)
    spread, counted = call(
        holder_kernel, [((4, OWN, 8, 128), F32, "h"), ((OWN, 8, 128), F32, "h")], [(held, "h")],
        [pltpu.VMEM((4, OWN, 8, 128), F32), blocks], copies=2,
    )
    coefs = known[COEF:]
    pair_out = [
        ((ROWS * (COLS + 2), 8, 128), F32, "v"), ((ROWS * WIDE, 8, 128), F32, "v"),
        ((COLS + 2 + 2 * WIDE, 8, 128), F32, "v"), ((COLS + 2 + 2 * WIDE, 8, 128), F32, "v"),
    ]
    adjoint4, *rest = call(
        turn_kernel, [((OWN, 8, 128), F32, "h")] + pair_out,
        [(par, "s"), (table, "s"), (tally, "s")] + weights
        + [(r_even, "v"), (r_odd, "v"), (n_even, "v"), (n_odd, "v"), (now, "v"), (coefs, "h"), (spread, "h"), (counted, "h")],
        [places, places, sums, sums, blocks, blocks, blocks], copies=1,
    )

    def gathered(first, second, m_even, m_odd):
        r_even, r_odd = exchange("px", m_even, m_odd)
        own_first, own_second, n_even, n_odd = call(
            adjoint_py_kernel, [PLAIN, PLAIN, ((12, 8, 128), F32, "v"), ((12, 8, 128), F32, "v")],
            [(par, "s"), (first, "v"), (second, "v"), (r_even, "v"), (r_odd, "v")],
            [pltpu.VMEM(first.shape, F32), pltpu.VMEM(second.shape, F32)],
        )
        n_even, n_odd = exchange("py", n_even, n_odd)
        return [(a, "v") for a in (own_first, own_second, n_even, n_odd)]

    later, *rest = call(
        adjoint_two, [((2 * OWN, 8, 128), F32, "h")] + pair_out,
        [(par, "s"), (table, "s"), (tally, "s")] + weights + gathered(*rest)
        + [(adjoint4, "h"), (past, "h"), (coefs, "h"), (spread, "h"), (counted, "h")],
        [sums, sums, blocks, blocks], copies=2,
    )
    (before,) = call(
        gradient_kernel, [((2 * OWN, 8, 128), F32, "v")],
        [(rest[2], "v"), (adjoint4, "h"), (later, "h"), (known, "h"), (past, "h"), (now, "h")],
    )
    field_out, gradient = call(
        finish_kernel, [(checkpoint_field.shape, F32, "v"), (chargeability.shape, F32, "v")],
        [(par, "s")] + gathered(*rest) + [(before, "v")], [blocks, blocks, turn],
    )
    return field_out, gradient


def solution(mesh):
    in_specs = (
        P("px", "py", None),
        P(None, "px", "py", None),
        P("px", "py", None, None),
        P("px", "py", None),
        P("px", "py", None),
        P(None, "px", "py", None),
        P(("px", "py"), None),
        P(("px", "py"), None),
        P(("px", "py")),
        P(),
    )
    out_specs = (P("px", "py", None), P("px", "py", None))
    return jax.shard_map(body, mesh=mesh, in_specs=in_specs, out_specs=out_specs, check_vma=False)
```

```python
import jax
import jax.numpy as jnp
from jax import lax
from jax.experimental import pallas as pl
from jax.experimental.pallas import tpu as pltpu
from jax.sharding import PartitionSpec as P

ROWS, COLS = 4, 8
OWN = ROWS * COLS
CAP = 8
WIDE = COLS + 4
PLACES = (ROWS + 4) * WIDE
F32, BF16 = jnp.float32, jnp.bfloat16
VMEM_BYTES, VMEM_MOST = 16 * 1024 * 1024, 63 * 1000 * 1000
NODE, WIDTH = 64, 512
FIELD, ADDEND, SUM0, SUM1, SUM2, SUM3, COEF = (i * OWN for i in range(7))
PX_BASE, PY_BASE = COLS * NODE, 2 * NODE
KNOWN, ROOM = COEF + 4 * ROWS, 12288


def place(row, col):
    return (row + 2) * WIDE + col + 2


def low_lanes(rows):
    return lax.broadcasted_iota(jnp.int32, (rows, 128), 1) < 64


def doubled(plain):
    turned = pltpu.roll(plain, 64, 1)
    low = low_lanes(8)
    return jnp.concatenate([jnp.where(low, plain, turned), jnp.where(low, turned, plain)], 0)


def packed(plain):
    return jnp.concatenate([plain[:, :64], plain[:, 64:]], 0)


def unpacked(rows):
    return jnp.concatenate([rows[:8], rows[8:]], 1)


def halves(plain):
    high = plain.astype(BF16).astype(F32)
    return jnp.concatenate([high, plain - high], 0).astype(BF16)


def joined(pair):
    pair = pair.astype(F32)
    return pair[:8] + pair[8:]


def parity():
    return lax.axis_index("px") % 2, lax.axis_index("py") % 2


def sides(par_ref, axis, near, far):
    even = par_ref[axis] == 0
    return jnp.where(even, near, far), jnp.where(even, far, near)


class Flow:
    def __init__(self, sems):
        self.sems, self.used, self.coming, self.going = sems, 0, {}, []

    def copy(self, source, target):
        made = pltpu.make_async_copy(source, target, self.sems.at[self.used])
        self.used += 1
        made.start()
        return made

    def wait(self, *refs):
        for ref in refs:
            for made in self.coming.pop(id(ref), ()):
                made.wait()

    def fetch(self, source, target):
        self.coming[id(target)] = [self.copy(source, target)]

    def send(self, source, target):
        self.going.append(self.copy(source, target))

    def finish(self):
        for key in list(self.coming):
            for made in self.coming.pop(key):
                made.wait()
        for made in self.going:
            made.wait()


def call(kernel, outs, inputs, scratch=(), copies=0, vmem=VMEM_BYTES):
    spaces = {"s": pltpu.SMEM, "v": pltpu.VMEM, "h": pltpu.HBM, "b": pltpu.HBM}
    arrays = [array for array, _ in inputs]
    fetched = [i for i, (_, kind) in enumerate(inputs) if kind == "h"]
    total = len(fetched) + copies

    def wrapped(*refs):
        refs = list(refs)
        buffers = refs[len(inputs) + len(outs) + len(scratch) :]
        flow = Flow(buffers[-1])
        for buffer, i in zip(buffers, fetched):
            flow.coming[id(buffer)] = [flow.copy(refs[i], buffer)]
            refs[i] = buffer
        kernel(flow, *refs[: len(inputs) + len(outs) + len(scratch)])
        flow.finish()

    buffers = [pltpu.VMEM(arrays[i].shape, arrays[i].dtype) for i in fetched]
    return pl.pallas_call(
        wrapped,
        out_shape=[jax.ShapeDtypeStruct(shape, dtype) for shape, dtype, _ in outs],
        in_specs=[pl.BlockSpec(memory_space=spaces[kind]) for _, kind in inputs],
        out_specs=[pl.BlockSpec(memory_space=spaces[kind]) for _, _, kind in outs],
        scratch_shapes=list(scratch) + buffers + [pltpu.SemaphoreType.DMA((max(total, 1),))],
        compiler_params=pltpu.CompilerParams(vmem_limit_bytes=vmem),
    )(*arrays)


PLAIN = ((OWN, 8, 128), F32, "v")


class Tiles:
    def __init__(self, ref, base=None):
        self.ref, self.base = ref, base

    def at(self, t):
        if self.base is None:
            return (t,)
        return pl.ds(self.base + 16 * (t // 4), 16), pl.ds(128 * (t % 4), 128)

    def __getitem__(self, t):
        return self.ref[self.at(t)]

    def __setitem__(self, t, value):
        self.ref[self.at(t)] = value


def to_plain(native, scratch, out):
    for x in range(ROWS):
        for r in range(8):
            scratch[pl.ds(x * 64 + r * 8, 8), :] = native(x, r)
    for x in range(ROWS):
        for y in range(COLS):
            out[x * COLS + y] = scratch[pl.ds(x * 64 + y, 8, stride=8), :]


def lanes(r):
    return pl.ds(r * 128, 128)


def twice(rows):
    return jnp.concatenate([rows, rows], 1)


def px_message(par, plain, addend, outs):
    bases = sides(par, 0, 2, 0)
    edges = sides(par, 0, 3, 0)
    for out, base, edge in zip(outs, bases, edges):
        for k in range(2):
            for p in range(4):
                at = (base + k) * COLS + 2 * p
                out[k * 4 + p] = jnp.concatenate([plain(at), plain(at + 1)], 0).astype(BF16)
        for y in range(COLS):
            out[8 + y] = halves(addend(edge * COLS + y))


def py_message(par, plain, addend, outs):
    pairs = sides(par, 1, 3, 0)
    edges = sides(par, 1, 7, 0)
    for out, pair, edge in zip(outs, pairs, edges):
        for x in range(ROWS):
            at = x * COLS + 2 * pair
            out[x] = jnp.concatenate([plain(at), plain(at + 1)], 0).astype(BF16)
            out[8 + x] = halves(addend(x * COLS + edge))


def picked_tile(tiles, choice, low, high):
    return jnp.where(choice == 0, tiles[low].astype(F32), tiles[high].astype(F32)).astype(BF16)


def py_fill(par, r_even, r_odd, outs):
    edges = sides(par, 1, 7, 0)
    for out, edge in zip(outs, edges):
        for k in range(2):
            out[4 + k] = picked_tile(r_even, edge, k * 4, k * 4 + 3)
            out[6 + k] = picked_tile(r_odd, edge, k * 4, k * 4 + 3)
        out[12] = picked_tile(r_even, edge, 8, 15)
        out[13] = picked_tile(r_odd, edge, 8, 15)


def shift_lines(offsets):
    row = lax.broadcasted_iota(jnp.int32, (8, 128), 0)
    lane = lax.broadcasted_iota(jnp.int32, (8, 128), 1)
    repeat = ((lane % 8 == row) & (lane < 64)).astype(F32).astype(BF16)
    lines = jnp.zeros((8, 128), F32)
    for x in range(ROWS):
        codes = offsets[x].astype(F32).astype(BF16)
        wide = lax.dot_general(codes, repeat, (((1,), (0,)), ((), ())), preferred_element_type=F32)
        line = jnp.sum(jnp.where(lane // 8 == row, wide, 0.0), axis=0, keepdims=True)
        lines = jnp.where(row == x, line, lines)
    above = (lines > 2.5).astype(F32) + (lines > 5.5).astype(F32)
    return 9.0 * above + lines - 13.0


def start_kernel(
    flow, steps, observed, part, node, offsets, field, memory, charge, stiffness,
    m_even_out, m_odd_out, both_out, d_even_out, d_odd_out, lines, sent,
    plain, addend, scratch, slots_of, m_even, m_odd, both, d_even, d_odd,
):
    par = parity()
    for out, edge in zip((m_even, m_odd), sides(par, 0, ROWS - 1, 0)):
        flow.coming[id(out)] = [
            flow.copy(stiffness.at[edge, y], out.at[pl.ds(y * NODE, NODE), :]) for y in range(COLS)
        ]
    for out, edge in zip((d_even, d_odd), sides(par, 1, COLS - 1, 0)):
        flow.coming[id(out)] = [flow.copy(stiffness.at[x, edge], out.at[x]) for x in range(ROWS)]
    flow.wait(steps, observed, part, node)
    owner_slots(steps, observed, part, node, slots_of)
    flow.send(slots_of, sent)
    flow.wait(offsets)
    found = shift_lines(offsets)
    lines[...] = found
    px_tiles = [Tiles(m_even, PX_BASE), Tiles(m_odd, PX_BASE)]
    py_tiles = [Tiles(both.at[0], PY_BASE), Tiles(both.at[1], PY_BASE)]
    flow.wait(m_even, m_odd, d_even, d_odd)
    for source, out in ((m_even, m_even_out), (m_odd, m_odd_out)):
        flow.send(source.at[pl.ds(0, PX_BASE), :], out.at[pl.ds(0, PX_BASE), :])
    flow.send(d_even, d_even_out)
    flow.send(d_odd, d_odd_out)
    for out, edge in zip(px_tiles, sides(par, 0, ROWS - 1, 0)):
        line = jnp.where(edge == 0, found[0:1], found[ROWS - 1 : ROWS])
        out[16] = jnp.broadcast_to(line, (16, 128)).astype(BF16)
    for out in py_tiles:
        out[14] = jnp.concatenate([found, jnp.zeros((8, 128), F32)], 0).astype(BF16)
    flow.wait(field, memory, charge)
    terms = memory.shape[0]
    to_plain(lambda x, r: field[x, :, lanes(r)], scratch, plain)

    def total(x, r):
        acc = memory[0, x, :, lanes(r)]
        for q in range(1, terms):
            acc = acc + memory[q, x, :, lanes(r)]
        return acc * -twice(charge[x])

    to_plain(total, scratch, addend)
    get, add = (lambda at: plain[at]), (lambda at: addend[at])
    px_message(par, get, add, px_tiles)
    for source, out in ((m_even, m_even_out), (m_odd, m_odd_out)):
        flow.send(source.at[pl.ds(PX_BASE, 80), :], out.at[pl.ds(PX_BASE, 80), :])
    py_message(par, get, add, py_tiles)
    flow.send(both.at[:, pl.ds(PY_BASE, 64), :], both_out.at[:, pl.ds(PY_BASE, 64), :])


def first_py_kernel(flow, r_even, r_odd, given, n_even, n_odd):
    par = parity()
    n_even[...] = given[0]
    n_odd[...] = given[1]
    tiles = [Tiles(r_even, PX_BASE), Tiles(r_odd, PX_BASE)]
    outs = [Tiles(n_even, PY_BASE), Tiles(n_odd, PY_BASE)]
    py_fill(par, tiles[0], tiles[1], outs)
    row = lax.broadcasted_iota(jnp.int32, (16, 128), 0)
    for out, edge in zip((n_even, n_odd), sides(par, 1, COLS - 1, 0)):
        for k, got in enumerate((r_even, r_odd)):
            out[pl.ds(k * NODE, NODE), :] = got[pl.ds(edge * NODE, NODE), :]
    for out in outs:
        even, odd = tiles[0][16].astype(F32), tiles[1][16].astype(F32)
        own = out[14].astype(F32)
        out[14] = jnp.where(row == ROWS, even, jnp.where(row == ROWS + 1, odd, own)).astype(BF16)


def second_py_kernel(flow, r_even, r_odd, in_even, in_odd, n_even, n_odd):
    par = parity()
    n_even[...] = in_even[...]
    n_odd[...] = in_odd[...]
    py_fill(par, Tiles(r_even), Tiles(r_odd), (Tiles(n_even), Tiles(n_odd)))


def decay_kernel(flow, after, field, memory, charge, relaxation, out, full, scratch):
    terms = memory.shape[0]
    flow.wait(field, memory, charge, relaxation)
    wide = [twice(charge[x]) for x in range(ROWS)]
    rates = [[twice(relaxation[q, x]) for q in range(terms)] for x in range(ROWS)]
    coefs = []
    for x in range(ROWS):
        w0 = w1 = w2 = 0.0
        for rate in rates[x]:
            w0 = w0 + (1.0 - rate)
            w1 = w1 + rate * (1.0 - rate)
            w2 = w2 + rate * rate * (1.0 - rate)
        coefs.append((wide[x], w0, w1, w2))
        for j in range(4):
            full[COEF + j * ROWS + x] = coefs[x][j]

    def region(base):
        return full.at[pl.ds(base, OWN)]

    def total(x, r):
        acc = memory[0, x, :, lanes(r)]
        for q in range(1, terms):
            acc = acc + memory[q, x, :, lanes(r)]
        return acc

    to_plain(lambda x, r: field[x, :, lanes(r)], scratch, region(FIELD))
    to_plain(total, scratch, region(SUM0))
    to_plain(lambda x, r: total(x, r) * -wide[x], scratch, region(ADDEND))
    for power, base in ((1, SUM1), (2, SUM2), (3, SUM3)):
        scale = [[rate if power == 1 else rate * rate if power == 2 else rate * rate * rate for rate in row] for row in rates]

        def part(x, r):
            acc = coefs[x][power] * field[x, :, lanes(r)]
            for q in range(terms):
                acc = acc + scale[x][q] * memory[q, x, :, lanes(r)]
            return acc

        to_plain(part, scratch, region(base))
    flow.send(full, out.at[pl.ds(0, KNOWN)])


class Coefs:
    def __init__(self, ref):
        self.ref = ref

    def __call__(self, j, block):
        return self.ref[j * ROWS + block // COLS, pl.ds(block % COLS, 1), :]


def outer_places(par):
    row_even, row_odd = sides(par, 0, ROWS, -1)
    col_even, col_odd = sides(par, 1, COLS, -1)
    listed = []
    for array, row in ((0, row_even), (1, row_odd)):
        listed += [(array, y, place(row, y)) for y in range(COLS)]
    rows = [0, 1, 2, 3, row_even, row_odd]
    for array, col in ((2, col_even), (3, col_odd)):
        listed += [(array, j, place(row, col)) for j, row in enumerate(rows)]
    return listed


def weight_of(blocks, item):
    own, r_even, r_odd, n_even, n_odd, d_even, d_odd = blocks
    if item < OWN:
        return own[item // COLS, item % COLS]
    item -= OWN
    if item < 2 * COLS:
        return (r_even, r_odd)[item // COLS][pl.ds(item % COLS * NODE, NODE), :]
    side, j = (item - 2 * COLS) // (ROWS + 2), (item - 2 * COLS) % (ROWS + 2)
    if j < ROWS:
        return (d_even, d_odd)[side][j]
    return (n_even, n_odd)[side][pl.ds((j - ROWS) * NODE, NODE), :]


def targets_of(table, par):
    columns = sides(par, 1, 0, COLS - 1)

    def target(item, k):
        if item < OWN + 2 * COLS:
            return table[item // COLS, (item % COLS) * 8 + k]
        item -= OWN + 2 * COLS
        side, j = item // (ROWS + 2), item % (ROWS + 2)
        return table[8 + j, columns[side] * 8 + k + 64 * side]

    return target


def table_lines(par, lines, r_even, r_odd, n_even, n_odd):
    row = lax.broadcasted_iota(jnp.int32, (8, 128), 0)
    lane = lax.broadcasted_iota(jnp.int32, (8, 128), 1)
    row_even, row_odd = sides(par, 0, ROWS, -1)
    line = jnp.where(row == ROWS, row_even, jnp.where(row == ROWS + 1, row_odd, row))
    even = Tiles(r_even, PX_BASE)[16].astype(F32)[:8]
    odd = Tiles(r_odd, PX_BASE)[16].astype(F32)[:8]
    first = jnp.where(row == ROWS, even, jnp.where(row == ROWS + 1, odd, lines))
    parts = [first.astype(jnp.int32) + place(line, lane // 8)]
    ends = []
    for msg, col in zip((n_even, n_odd), sides(par, 1, COLS, -1)):
        ends.append(Tiles(msg, PY_BASE)[14].astype(F32)[:8].astype(jnp.int32) + place(line, col))
    parts.append(jnp.where(lane < 64, ends[0], pltpu.roll(ends[1], 64, 1)))
    return jnp.concatenate(parts, 0)


def forward_pair(par, target, ready, blocks, plain, received, field, middle, store_first, store_second):
    low = low_lanes(16)
    r_even, r_odd, n_even, n_odd = received

    def spread(pair, first, second):
        both = pair.astype(F32)
        field[first] = doubled(both[:8]).astype(BF16)
        field[second] = doubled(both[8:]).astype(BF16)

    row_bases = sides(par, 0, ROWS, -2)
    col_bases = sides(par, 1, COLS, -2)
    for msg, base in zip((r_even, r_odd), row_bases):
        for k in range(2):
            for p in range(4):
                at = place(base + k, 2 * p)
                spread(msg[k * 4 + p], at, at + 1)
    rows = [0, 1, 2, 3, row_bases[0], row_bases[0] + 1, row_bases[1], row_bases[1] + 1]
    for msg, base in zip((n_even, n_odd), col_bases):
        for j, row in enumerate(rows):
            at = place(row, base)
            spread(msg[j], at, at + 1)
    ready()
    for block in range(OWN):
        field[place(block // COLS, block % COLS)] = doubled(plain(block)).astype(BF16)

    def product(source, item):
        parts = []
        for m in range(4):
            one = source[target(item, 2 * m)]
            two = source[target(item, 2 * m + 1)]
            parts.append(jnp.where(low, one, two))
        picked = jnp.concatenate(parts, 1)
        out = lax.dot_general(
            picked, weight_of(blocks, item), (((1,), (1,)), ((), ())), preferred_element_type=F32
        )
        return unpacked(out)

    for number, (array, index, at) in enumerate(outer_places(par)):
        got = product(field, OWN + number) + joined(received[array][8 + index])
        middle[at] = doubled(got).astype(BF16)
    for block in range(OWN):
        got = store_first(block, product(field, block))
        middle[place(block // COLS, block % COLS)] = doubled(got).astype(BF16)
    for block in range(OWN):
        store_second(block, product(middle, block))


def forward_one(
    flow, lines, own, r_even, r_odd, n_even, n_odd, d_even, d_odd, stored, past, now, m_even, m_odd, p_even, p_odd, table_out,
    field, middle, table, known,
):
    par = parity()
    begun = flow.copy(stored.at[pl.ds(0, 2 * OWN)], known.at[pl.ds(0, 2 * OWN)])
    rest = flow.copy(stored.at[pl.ds(2 * OWN, KNOWN - 2 * OWN)], known.at[pl.ds(2 * OWN, KNOWN - 2 * OWN)])
    table_out[...] = table_lines(par, lines[...], r_even, r_odd, n_even, n_odd)
    looked = flow.copy(table_out, table)
    coef = Coefs(known.at[pl.ds(COEF, 4 * ROWS)])

    def ready():
        looked.wait()
        begun.wait()

    def first(block, out):
        if block == 0:
            rest.wait()
        got = out + known[ADDEND + block]
        past[block] = got
        full = known[SUM2 + block] + coef(1, block) * got
        past[OWN + block] = full
        now[OWN + block] = -coef(0, block) * full
        return got

    def second(block, out):
        now[block] = out - coef(0, block) * known[SUM1 + block]

    received = (Tiles(r_even, PX_BASE), Tiles(r_odd, PX_BASE), Tiles(n_even, PY_BASE), Tiles(n_odd, PY_BASE))
    forward_pair(
        par, targets_of(table, par), ready, (own, r_even, r_odd, n_even, n_odd, d_even, d_odd), lambda block: known[FIELD + block],
        received, field, middle, first, second,
    )
    get, add = (lambda at: now[at]), (lambda at: now[OWN + at])
    px_message(par, get, add, (Tiles(m_even), Tiles(m_odd)))
    py_message(par, get, add, (Tiles(p_even), Tiles(p_odd)))
    for block in range(OWN):
        now[2 * OWN + block] = known[SUM3 + block] + coef(2, block) * past[block] + coef(1, block) * now[block]


def turn_kernel(
    flow, table, own, r_even, r_odd, n_even, n_odd, d_even, d_odd, e_even, e_odd, s_even, s_odd, now, stored, spread, counted,
    adjoint4, first_out, second_out, m_even, m_odd, field, middle, sums_one, sums_two, field3, field4, coefs,
):
    par = parity()
    flow.fetch(stored.at[pl.ds(COEF, 4 * ROWS)], coefs)
    blocks = (own, r_even, r_odd, n_even, n_odd, d_even, d_odd)
    target = targets_of(table, par)
    coef = Coefs(coefs)

    def first(block, out):
        got = out + now[OWN + block]
        field3[block] = got
        return got

    def second(block, out):
        if block == 0:
            flow.wait(coefs)
        field4[block] = out - coef(0, block) * now[2 * OWN + block]

    received = (Tiles(e_even), Tiles(e_odd), Tiles(s_even), Tiles(s_odd))
    clear(sums_one, sums_two)
    forward_pair(
        par, target, lambda: None, blocks, lambda block: now[block], received, field, middle, first, second
    )
    def start(block):
        value = injected(4, counted, field4[block], spread, block)
        adjoint4[block] = value
        return value

    def add_first(block):
        return injected(3, counted, field3[block], spread, block)

    def add_second(block):
        memory = coef(0, block) * coef(1, block) * adjoint4[block]
        return injected(2, counted, now[block], spread, block) - memory

    adjoint_pair(
        par, target, blocks, start, add_first, add_second, (first_out, second_out, m_even, m_odd), sums_one, sums_two
    )


def clear(*refs):
    for ref in refs:
        zero = jnp.zeros(ref.shape[1:], F32)
        for at in range(ref.shape[0]):
            ref[at] = zero


def adjoint_pair(par, target, blocks, start, add_first, add_second, outs, middle, last):
    first_out, second_out, m_even, m_odd = outs
    low = low_lanes(16)

    def push(sums_ref, item, rows):
        out = lax.dot_general(
            rows, weight_of(blocks, item), (((1,), (0,)), ((), ())), preferred_element_type=F32
        )
        spots = [target(item, k) for k in range(8)]
        sums = []
        for k in range(8):
            part = out[:, (k // 2) * 128 : (k // 2 + 1) * 128]
            part = jnp.where(low, part, 0.0) if k % 2 == 0 else jnp.where(low, 0.0, part)
            sums.append(sums_ref[spots[k]] + part)
        for k in range(8):
            sums_ref[spots[k]] = sums[k]

    def both(sums_ref, at):
        value = sums_ref[at]
        return value + pltpu.roll(value, 64, 1)

    def plain_of(value):
        return jnp.where(low_lanes(8), value[:8], value[8:])

    for block in range(OWN):
        push(middle, block, packed(start(block)).astype(BF16))
    rows_at = sides(par, 0, ROWS, -1)
    for number, (array, index, at) in enumerate(outer_places(par)):
        value = both(middle, at)
        push(last, OWN + number, value[:, :64].astype(BF16))
    for out, row in zip((m_even, m_odd), rows_at):
        for j in range(0, COLS + 2, 2):
            out[j // 2] = paired(plain_of(both(middle, place(row, j + i - 1))) for i in range(2))
    for x in range(ROWS):
        for j in range(COLS + 2):
            value = plain_of(both(middle, place(x, j - 1)))
            if 1 <= j <= COLS:
                block = x * COLS + j - 1
                value = value + add_first(block)
                push(last, block, packed(value).astype(BF16))
            first_out[x * (COLS + 2) + j] = value
    for out, base in zip((m_even, m_odd), sides(par, 0, ROWS, -2)):
        for k in range(2):
            for j in range(0, WIDE, 2):
                at = COLS // 2 + 1 + (k * WIDE + j) // 2
                out[at] = paired(plain_of(both(last, place(base + k, j + i - 2))) for i in range(2))
    for x in range(ROWS):
        for j in range(WIDE):
            value = plain_of(both(last, place(x, j - 2)))
            if 2 <= j < COLS + 2:
                value = value + add_second(x * COLS + j - 2)
            second_out[x * WIDE + j] = value


def paired(blocks):
    return jnp.concatenate(list(blocks), 0).astype(BF16)


def add_pair(target, at, pair):
    both = pair.astype(F32)
    target[at] += both[:8]
    target[at + 1] += both[8:]


def adjoint_py_kernel(flow, first, second, r_even, r_odd, first_own, second_own, n_even, n_odd, one, two):
    par = parity()
    one[...] = first[...]
    two[...] = second[...]
    for msg, row, base in zip((r_even, r_odd), sides(par, 0, 3, 0), sides(par, 0, 2, 0)):
        for j in range(0, COLS + 2, 2):
            add_pair(one, row * (COLS + 2) + j, msg[j // 2])
        for k in range(2):
            for j in range(0, WIDE, 2):
                add_pair(two, (base + k) * WIDE + j, msg[COLS // 2 + 1 + (k * WIDE + j) // 2])
    for out, col, base in zip((n_even, n_odd), sides(par, 1, COLS + 1, 0), sides(par, 1, COLS + 2, 0)):
        for x in range(ROWS):
            out[2 + x] = paired(two[x * WIDE + base + k] for k in range(2))
        for h in range(2):
            out[h] = paired(one[(2 * h + i) * (COLS + 2) + col] for i in range(2))
    for x in range(ROWS):
        for y in range(COLS):
            first_own[x * COLS + y] = one[x * (COLS + 2) + 1 + y]
            second_own[x * COLS + y] = two[x * WIDE + 2 + y]


def settle(par, first_own, second_own, n_even, n_odd, first, second):
    first[...] = first_own[...]
    second[...] = second_own[...]
    for msg, col, base in zip((n_even, n_odd), sides(par, 1, 7, 0), sides(par, 1, 6, 0)):
        for x in range(ROWS):
            add_pair(second, x * COLS + base, msg[2 + x])
        for h in range(2):
            both = msg[h].astype(F32)
            first[2 * h * COLS + col] += both[:8]
            first[(2 * h + 1) * COLS + col] += both[8:]


def injected(moment, counted, field, spread, block):
    return counted[moment - 1, block] * field - spread[moment - 1, block]


def adjoint_two(
    flow, table, own, r_even, r_odd, n_even, n_odd, d_even, d_odd, first_own, second_own, e_even, e_odd, adjoint4, past, stored,
    spread, counted, later, first_out, second_out, m_even, m_odd, sums_one, sums_two, coefs,
):
    par = parity()
    flow.fetch(stored.at[pl.ds(COEF, 4 * ROWS)], coefs)
    clear(sums_one, sums_two)
    adjoint3, adjoint2 = later.at[pl.ds(0, OWN)], later.at[pl.ds(OWN, OWN)]
    settle(par, first_own, second_own, e_even, e_odd, adjoint3, adjoint2)
    coef = Coefs(coefs)

    def add_first(block):
        if block == 0:
            flow.wait(coefs)
        memory = coef(2, block) * adjoint4[block] + coef(1, block) * adjoint3[block]
        return injected(1, counted, past[block], spread, block) - coef(0, block) * memory

    def add_second(block):
        memory = coef(3, block) * adjoint4[block] + coef(2, block) * adjoint3[block] + coef(1, block) * adjoint2[block]
        return -coef(0, block) * memory

    adjoint_pair(
        par, targets_of(table, par), (own, r_even, r_odd, n_even, n_odd, d_even, d_odd), lambda block: adjoint2[block], add_first,
        add_second, (first_out, second_out, m_even, m_odd), sums_one, sums_two,
    )


def gradient_kernel(flow, after, adjoint4, later, stored, past, now, out, known):
    flow.fetch(stored.at[pl.ds(0, KNOWN)], known)
    flow.wait(known)
    for block in range(OWN):
        out[block] = (
            adjoint4[block] * now[2 * OWN + block] + later[block] * past[OWN + block]
            + later[OWN + block] * known[SUM1 + block]
        )
        out[OWN + block] = known[SUM0 + block]


def finish_kernel(
    flow, first_own, second_own, n_even, n_odd, before, result, gradient, adjoint1, adjoint0, scratch
):
    par = parity()
    settle(par, first_own, second_own, n_even, n_odd, adjoint1, adjoint0)
    for x in range(ROWS):
        parts = []
        for y in range(COLS):
            block = x * COLS + y
            scratch[pl.ds(x * 64 + y * 8, 8), :] = adjoint0[block]
            value = before[block] + adjoint1[block] * before[OWN + block]
            parts.append(jnp.sum(value, axis=0, keepdims=True))
        rows = jnp.concatenate(parts, 0)
        gradient[x] = -(rows[:, :64] + rows[:, 64:])
        for r in range(8):
            result[x, :, lanes(r)] = scratch[pl.ds(x * 64 + r, 8, stride=8), :]


def split(value):
    high = value.astype(BF16)
    return high, (value - high.astype(F32)).astype(BF16)


def owner_slots(steps, observed, part, node, slots_of):
    owned = observed.shape[0]
    slots = slots_of.shape[0]
    devices = slots // CAP
    row = lax.broadcasted_iota(jnp.int32, (128, 128), 0)
    col = lax.broadcasted_iota(jnp.int32, (128, 128), 1)
    gate = row // 16
    source = row % 16
    step = jnp.zeros((128, 128), jnp.int32)
    for g in range(8):
        step = jnp.where(gate == g, jnp.broadcast_to(steps[0:1, g : g + 1], (128, 128)), step)
    wanted = 2 * (col % 8) + (col // 8) % 2
    chosen = ((step == col // 16 + 1) & (source == wanted) & (col < 64)).astype(F32).astype(BF16)
    high, low = split(observed[...])
    dot = lambda a, b: lax.dot_general(a, b, (((1,), (0,)), ((), ())), preferred_element_type=F32)
    sums = dot(high, chosen) + dot(low, chosen)
    dest = part[...]
    member = (dest == lax.broadcasted_iota(jnp.int32, (devices, owned), 0)).astype(F32)
    earlier = (
        lax.broadcasted_iota(jnp.int32, (owned, owned), 0) < lax.broadcasted_iota(jnp.int32, (owned, owned), 1)
    ).astype(F32).astype(BF16)
    ahead = dot(member.astype(BF16), earlier)
    rank = jnp.sum(ahead * member, axis=0, keepdims=True).astype(jnp.int32)
    position = dest * CAP + rank
    where = (position == lax.broadcasted_iota(jnp.int32, (slots, owned), 0)).astype(F32).astype(BF16)
    line = lax.broadcasted_iota(jnp.int32, (128, owned), 0)
    which = node[...]
    block = lax.shift_right_logical(which, 6)
    inner = which - block * 64
    marks = jnp.where(line == 64, block, jnp.where(line == 65, inner, jnp.where(line == 66, 1, 0)))
    high, low = split(sums)
    turned = lambda a, b: lax.dot_general(a, b, (((1,), (1,)), ((), ())), preferred_element_type=F32)
    slots_of[...] = dot(where, high) + dot(where, low) + turned(where, marks.astype(F32).astype(BF16))


def holder_kernel(flow, steps, slots, after, spread, counted):
    flow.wait(slots)
    tally = []
    for n in range(4):
        total = jnp.zeros((), F32)
        for g in range(8):
            total = total + jnp.where(steps[g] == n + 1, 1.0, 0.0)
        tally.append(total)
    values = slots[...]
    count = values.shape[0]
    lane = lax.broadcasted_iota(jnp.int32, (count, 128), 1)
    pick = lambda at: jnp.sum(jnp.where(lane == at, values, 0.0), axis=1, keepdims=True)
    place_of = jnp.where(pick(66) > 0.5, pick(64) * 64.0 + pick(65), -1.0).astype(jnp.int32)
    high, low = split(values.T)
    both = jnp.concatenate([high, low], 0)
    low8 = low_lanes(8)
    for chunk in range(OWN * 64 // 256):
        spots = lax.broadcasted_iota(jnp.int32, (count, 256), 1) + chunk * 256
        hot = (place_of == spots).astype(F32).astype(BF16)
        out = lax.dot_general(both, hot, (((1,), (0,)), ((), ())), preferred_element_type=F32)
        out = out[:128] + out[128:]
        for j in range(2):
            first = chunk * 4 + 2 * j
            for n in range(4):
                even = out[n * 16 : n * 16 + 8, j * 128 : (j + 1) * 128]
                odd = out[n * 16 + 8 : n * 16 + 16, j * 128 : (j + 1) * 128]
                spread[n, first] = jnp.where(low8, even, pltpu.roll(odd, 64, 1))
                spread[n, first + 1] = jnp.where(low8, pltpu.roll(even, 64, 1), odd)
            many = jnp.broadcast_to(out[66:67, j * 128 : (j + 1) * 128], (8, 128))
            other = pltpu.roll(many, 64, 1)
            for n in range(4):
                counted[n, first] = jnp.where(low8, many, other) * tally[n]
                counted[n, first + 1] = jnp.where(low8, other, many) * tally[n]


def swap_even(axis):
    return [(i, i ^ 1) for i in range(lax.axis_size(axis))]


def swap_odd(axis):
    inner = range(1, lax.axis_size(axis) - 1, 2)
    return [(i, i + 1) for i in inner] + [(i + 1, i) for i in inner]


def exchange(axis, for_even, for_odd):
    return lax.ppermute(for_even, axis, swap_even(axis)), lax.ppermute(for_odd, axis, swap_odd(axis))


def body(
    checkpoint_field,
    checkpoint_memory,
    stiffness,
    block_offsets,
    chargeability,
    relaxation,
    observed,
    receiver_part,
    receiver_node,
    gate_step,
):
    devices = lax.axis_size(("px", "py"))
    slots = devices * CAP
    turn = pltpu.VMEM((256, 128), F32)
    lookup = pltpu.SMEM((16, 128), jnp.int32)
    places = pltpu.VMEM((PLACES, 16, 128), BF16)
    sums = pltpu.VMEM((PLACES, 16, 128), F32)
    blocks = pltpu.VMEM((OWN, 8, 128), F32)
    px_first = ((PX_BASE + 80, WIDTH), BF16, "v")
    py_first = ((PY_BASE + 64, WIDTH), BF16, "v")
    px_shape = ((16, 16, 128), BF16, "v")
    py_shape = ((14, 16, 128), BF16, "v")
    down = ((ROWS, NODE, WIDTH), BF16, "v")
    two = (2,) + py_first[0]
    m_even, m_odd, both, d_even, d_odd, lines, sent = call(
        start_kernel,
        [
            px_first[:2] + ("h",), px_first[:2] + ("h",), (two, BF16, "h"), down[:2] + ("h",), down[:2] + ("h",),
            ((8, 128), F32, "v"), ((slots, 128), F32, "h"),
        ],
        [
            (gate_step.reshape(1, -1), "h"), (observed, "h"), (receiver_part.reshape(1, -1), "h"),
            (receiver_node.reshape(1, -1), "h"), (block_offsets, "h"), (checkpoint_field, "h"),
            (checkpoint_memory, "h"), (chargeability, "h"), (stiffness, "b"),
        ],
        [blocks, blocks, turn, pltpu.VMEM((slots, 128), F32)]
        + [pltpu.VMEM(shape, BF16) for shape in (px_first[0], px_first[0], two, down[0], down[0])],
        copies=2 * COLS + 2 * ROWS + 8, vmem=65 * 1000 * 1000,
    )
    r_even, r_odd = exchange("px", m_even, m_odd)
    d_even, d_odd = exchange("py", d_even, d_odd)
    sent, r_even = lax.optimization_barrier((sent, r_even))
    held = lax.all_to_all(
        sent.reshape(devices, CAP, 128), ("px", "py"), split_axis=0, concat_axis=0, tiled=True
    ).reshape(slots, 128)
    n_even, n_odd = call(
        first_py_kernel, [py_first, py_first],
        [(r_even, "v"), (r_odd, "v"), (both, "v")],
    )
    (known,) = call(
        decay_kernel, [((ROOM, 8, 128), F32, "h")],
        [(n_even, "v"), (checkpoint_field, "h"), (checkpoint_memory, "h"), (chargeability, "h"), (relaxation, "h")],
        [pltpu.VMEM((KNOWN, 8, 128), F32), turn], copies=1, vmem=VMEM_MOST,
    )
    n_even, n_odd = exchange("py", n_even, n_odd)
    held, n_even = lax.optimization_barrier((held, n_even))
    weights = [(a, "v") for a in (stiffness, r_even, r_odd, n_even, n_odd, d_even, d_odd)]
    past, now, m_even, m_odd, p_even, p_odd, table = call(
        forward_one,
        [
            ((2 * OWN, 8, 128), F32, "v"), ((3 * OWN, 8, 128), F32, "v"), px_shape, px_shape, py_shape, py_shape,
            ((16, 128), jnp.int32, "v"),
        ],
        [(lines, "v")] + weights + [(known, "b")],
        [places, places, lookup, pltpu.VMEM((KNOWN, 8, 128), F32)], copies=3,
    )
    r_even, r_odd = exchange("px", m_even, m_odd)
    n_even, n_odd = call(
        second_py_kernel, [py_shape, py_shape],
        [(r_even, "v"), (r_odd, "v"), (p_even, "v"), (p_odd, "v")],
    )
    n_even, n_odd = exchange("py", n_even, n_odd)
    spread, counted = call(
        holder_kernel, [((4, OWN, 8, 128), F32, "v"), ((4, OWN, 8, 128), F32, "v")],
        [(gate_step, "s"), (held, "h"), (m_even, "v")],
    )
    coefs = pltpu.VMEM((4 * ROWS, 8, 128), F32)
    rim = ((COLS // 2 + 1 + WIDE, 16, 128), BF16, "v")
    rim_py = ((6, 16, 128), BF16, "v")
    pair_out = [
        ((ROWS * (COLS + 2), 8, 128), F32, "v"), ((ROWS * WIDE, 8, 128), F32, "v"),
        rim, rim,
    ]
    adjoint4, *rest = call(
        turn_kernel, [PLAIN] + pair_out,
        [(table, "s")] + weights
        + [(r_even, "v"), (r_odd, "v"), (n_even, "v"), (n_odd, "v"), (now, "v"), (known, "b"), (spread, "v"), (counted, "v")],
        [places, places, sums, sums, blocks, blocks, coefs], copies=1,
    )

    def gathered(first, second, m_even, m_odd):
        r_even, r_odd = exchange("px", m_even, m_odd)
        own_first, own_second, n_even, n_odd = call(
            adjoint_py_kernel, [PLAIN, PLAIN, rim_py, rim_py],
            [(first, "v"), (second, "v"), (r_even, "v"), (r_odd, "v")],
            [pltpu.VMEM(first.shape, F32), pltpu.VMEM(second.shape, F32)],
        )
        n_even, n_odd = exchange("py", n_even, n_odd)
        return [(a, "v") for a in (own_first, own_second, n_even, n_odd)]

    later, *rest = call(
        adjoint_two, [((2 * OWN, 8, 128), F32, "v")] + pair_out,
        [(table, "s")] + weights + gathered(*rest)
        + [(adjoint4, "v"), (past, "v"), (known, "b"), (spread, "v"), (counted, "v")],
        [sums, sums, coefs], copies=1,
    )
    (before,) = call(
        gradient_kernel, [((2 * OWN, 8, 128), F32, "v")],
        [(a, "b" if a is known else "v") for a in (rest[2], adjoint4, later, known, past, now)],
        [pltpu.VMEM((KNOWN, 8, 128), F32)], copies=1,
    )
    field_out, gradient = call(
        finish_kernel, [(checkpoint_field.shape, F32, "v"), (chargeability.shape, F32, "v")],
        [] + gathered(*rest) + [(before, "v")], [blocks, blocks, turn],
    )
    return field_out, gradient


def solution(mesh):
    in_specs = (
        P("px", "py", None),
        P(None, "px", "py", None),
        P("px", "py", None, None),
        P("px", "py", None),
        P("px", "py", None),
        P(None, "px", "py", None),
        P(("px", "py"), None),
        P(("px", "py"), None),
        P(("px", "py")),
        P(),
    )
    out_specs = (P("px", "py", None), P("px", "py", None))
    return jax.shard_map(body, mesh=mesh, in_specs=in_specs, out_specs=out_specs, check_vma=False)
```

```python
import jax
import jax.numpy as jnp
from jax import lax
from jax.experimental import pallas as pl
from jax.experimental.pallas import tpu as pltpu
from jax.sharding import PartitionSpec as P

ROWS, COLS = 4, 8
OWN = ROWS * COLS
CAP = 8
WIDE = COLS + 4
PLACES = (ROWS + 4) * WIDE
F32, BF16 = jnp.float32, jnp.bfloat16
VMEM_BYTES, VMEM_MOST = 16 * 1024 * 1024, 63 * 1000 * 1000
NODE, WIDTH = 64, 512
FIELD, ADDEND, SUM0, SUM1, SUM2, SUM3, COEF = (i * OWN for i in range(7))
PX_BASE, PY_BASE = COLS * NODE, 2 * NODE
KNOWN, ROOM = COEF + 4 * ROWS, 12288


def place(row, col):
    return (row + 2) * WIDE + col + 2


def low_lanes(rows):
    return lax.broadcasted_iota(jnp.int32, (rows, 128), 1) < 64


def doubled(plain):
    turned = pltpu.roll(plain, 64, 1)
    low = low_lanes(8)
    return jnp.concatenate([jnp.where(low, plain, turned), jnp.where(low, turned, plain)], 0)


def packed(plain):
    return jnp.concatenate([plain[:, :64], plain[:, 64:]], 0)


def unpacked(rows):
    return jnp.concatenate([rows[:8], rows[8:]], 1)


def halves(plain):
    high = plain.astype(BF16).astype(F32)
    return jnp.concatenate([high, plain - high], 0).astype(BF16)


def joined(pair):
    pair = pair.astype(F32)
    return pair[:8] + pair[8:]


def parity():
    return lax.axis_index("px") % 2, lax.axis_index("py") % 2


def sides(par_ref, axis, near, far):
    even = par_ref[axis] == 0
    return jnp.where(even, near, far), jnp.where(even, far, near)


class Flow:
    def __init__(self, sems):
        self.sems, self.used, self.coming, self.going = sems, 0, {}, []

    def copy(self, source, target):
        made = pltpu.make_async_copy(source, target, self.sems.at[self.used])
        self.used += 1
        made.start()
        return made

    def wait(self, *refs):
        for ref in refs:
            for made in self.coming.pop(id(ref), ()):
                made.wait()

    def fetch(self, source, target):
        self.coming[id(target)] = [self.copy(source, target)]

    def send(self, source, target):
        self.going.append(self.copy(source, target))

    def finish(self):
        for key in list(self.coming):
            for made in self.coming.pop(key):
                made.wait()
        for made in self.going:
            made.wait()


def call(kernel, outs, inputs, scratch=(), copies=0, vmem=VMEM_BYTES):
    spaces = {"s": pltpu.SMEM, "v": pltpu.VMEM, "h": pltpu.HBM, "b": pltpu.HBM}
    arrays = [array for array, _ in inputs]
    fetched = [i for i, (_, kind) in enumerate(inputs) if kind == "h"]
    total = len(fetched) + copies

    def wrapped(*refs):
        refs = list(refs)
        buffers = refs[len(inputs) + len(outs) + len(scratch) :]
        flow = Flow(buffers[-1])
        for buffer, i in zip(buffers, fetched):
            flow.coming[id(buffer)] = [flow.copy(refs[i], buffer)]
            refs[i] = buffer
        kernel(flow, *refs[: len(inputs) + len(outs) + len(scratch)])
        flow.finish()

    buffers = [pltpu.VMEM(arrays[i].shape, arrays[i].dtype) for i in fetched]
    return pl.pallas_call(
        wrapped,
        out_shape=[jax.ShapeDtypeStruct(shape, dtype) for shape, dtype, _ in outs],
        in_specs=[pl.BlockSpec(memory_space=spaces[kind]) for _, kind in inputs],
        out_specs=[pl.BlockSpec(memory_space=spaces[kind]) for _, _, kind in outs],
        scratch_shapes=list(scratch) + buffers + [pltpu.SemaphoreType.DMA((max(total, 1),))],
        compiler_params=pltpu.CompilerParams(vmem_limit_bytes=vmem),
    )(*arrays)


PLAIN = ((OWN, 8, 128), F32, "v")


class Tiles:
    def __init__(self, ref, base=None):
        self.ref, self.base = ref, base

    def at(self, t):
        if self.base is None:
            return (t,)
        return pl.ds(self.base + 16 * (t // 4), 16), pl.ds(128 * (t % 4), 128)

    def __getitem__(self, t):
        return self.ref[self.at(t)]

    def __setitem__(self, t, value):
        self.ref[self.at(t)] = value


def to_plain(native, scratch, out):
    for x in range(ROWS):
        for r in range(8):
            scratch[pl.ds(x * 64 + r * 8, 8), :] = native(x, r)
    for x in range(ROWS):
        for y in range(COLS):
            out[x * COLS + y] = scratch[pl.ds(x * 64 + y, 8, stride=8), :]


def lanes(r):
    return pl.ds(r * 128, 128)


def twice(rows):
    return jnp.concatenate([rows, rows], 1)


def px_message(par, plain, addend, outs):
    bases = sides(par, 0, 2, 0)
    edges = sides(par, 0, 3, 0)
    for out, base, edge in zip(outs, bases, edges):
        for k in range(2):
            for p in range(4):
                at = (base + k) * COLS + 2 * p
                out[k * 4 + p] = jnp.concatenate([plain(at), plain(at + 1)], 0).astype(BF16)
        for y in range(COLS):
            out[8 + y] = halves(addend(edge * COLS + y))


def py_message(par, plain, addend, outs):
    pairs = sides(par, 1, 3, 0)
    edges = sides(par, 1, 7, 0)
    for out, pair, edge in zip(outs, pairs, edges):
        for x in range(ROWS):
            at = x * COLS + 2 * pair
            out[x] = jnp.concatenate([plain(at), plain(at + 1)], 0).astype(BF16)
            out[8 + x] = halves(addend(x * COLS + edge))


def picked_tile(tiles, choice, low, high):
    return jnp.where(choice == 0, tiles[low].astype(F32), tiles[high].astype(F32)).astype(BF16)


def py_fill(par, r_even, r_odd, outs):
    edges = sides(par, 1, 7, 0)
    for out, edge in zip(outs, edges):
        for k in range(2):
            out[4 + k] = picked_tile(r_even, edge, k * 4, k * 4 + 3)
            out[6 + k] = picked_tile(r_odd, edge, k * 4, k * 4 + 3)
        out[12] = picked_tile(r_even, edge, 8, 15)
        out[13] = picked_tile(r_odd, edge, 8, 15)


def shift_lines(offsets):
    row = lax.broadcasted_iota(jnp.int32, (8, 128), 0)
    lane = lax.broadcasted_iota(jnp.int32, (8, 128), 1)
    repeat = ((lane % 8 == row) & (lane < 64)).astype(F32).astype(BF16)
    lines = jnp.zeros((8, 128), F32)
    for x in range(ROWS):
        codes = offsets[x].astype(F32).astype(BF16)
        wide = lax.dot_general(codes, repeat, (((1,), (0,)), ((), ())), preferred_element_type=F32)
        line = jnp.sum(jnp.where(lane // 8 == row, wide, 0.0), axis=0, keepdims=True)
        lines = jnp.where(row == x, line, lines)
    above = (lines > 2.5).astype(F32) + (lines > 5.5).astype(F32)
    return 9.0 * above + lines - 13.0


def start_kernel(
    flow, steps, observed, part, node, offsets, field, memory, charge, stiffness,
    m_even_out, m_odd_out, both_out, d_even_out, d_odd_out, lines, sent,
    plain, addend, scratch, slots_of, m_even, m_odd, both, d_even, d_odd,
):
    par = parity()
    for out, edge in zip((m_even, m_odd), sides(par, 0, ROWS - 1, 0)):
        flow.coming[id(out)] = [
            flow.copy(stiffness.at[edge, y], out.at[pl.ds(y * NODE, NODE), :]) for y in range(COLS)
        ]
    for out, edge in zip((d_even, d_odd), sides(par, 1, COLS - 1, 0)):
        flow.coming[id(out)] = [flow.copy(stiffness.at[x, edge], out.at[x]) for x in range(ROWS)]
    flow.wait(steps, observed, part, node)
    owner_slots(steps, observed, part, node, slots_of)
    flow.send(slots_of, sent)
    flow.wait(offsets)
    found = shift_lines(offsets)
    lines[...] = found
    px_tiles = [Tiles(m_even, PX_BASE), Tiles(m_odd, PX_BASE)]
    py_tiles = [Tiles(both.at[0], PY_BASE), Tiles(both.at[1], PY_BASE)]
    flow.wait(m_even, m_odd, d_even, d_odd)
    for source, out in ((m_even, m_even_out), (m_odd, m_odd_out)):
        flow.send(source.at[pl.ds(0, PX_BASE), :], out.at[pl.ds(0, PX_BASE), :])
    flow.send(d_even, d_even_out)
    flow.send(d_odd, d_odd_out)
    for out, edge in zip(px_tiles, sides(par, 0, ROWS - 1, 0)):
        line = jnp.where(edge == 0, found[0:1], found[ROWS - 1 : ROWS])
        out[16] = jnp.broadcast_to(line, (16, 128)).astype(BF16)
    for out in py_tiles:
        out[14] = jnp.concatenate([found, jnp.zeros((8, 128), F32)], 0).astype(BF16)
    flow.wait(field, memory, charge)
    terms = memory.shape[0]
    to_plain(lambda x, r: field[x, :, lanes(r)], scratch, plain)

    def total(x, r):
        acc = memory[0, x, :, lanes(r)]
        for q in range(1, terms):
            acc = acc + memory[q, x, :, lanes(r)]
        return acc * -twice(charge[x])

    to_plain(total, scratch, addend)
    get, add = (lambda at: plain[at]), (lambda at: addend[at])
    px_message(par, get, add, px_tiles)
    for source, out in ((m_even, m_even_out), (m_odd, m_odd_out)):
        flow.send(source.at[pl.ds(PX_BASE, 80), :], out.at[pl.ds(PX_BASE, 80), :])
    py_message(par, get, add, py_tiles)
    flow.send(both.at[:, pl.ds(PY_BASE, 64), :], both_out.at[:, pl.ds(PY_BASE, 64), :])


def first_py_kernel(flow, r_even, r_odd, given, n_even, n_odd):
    par = parity()
    n_even[...] = given[0]
    n_odd[...] = given[1]
    tiles = [Tiles(r_even, PX_BASE), Tiles(r_odd, PX_BASE)]
    outs = [Tiles(n_even, PY_BASE), Tiles(n_odd, PY_BASE)]
    py_fill(par, tiles[0], tiles[1], outs)
    row = lax.broadcasted_iota(jnp.int32, (16, 128), 0)
    for out, edge in zip((n_even, n_odd), sides(par, 1, COLS - 1, 0)):
        for k, got in enumerate((r_even, r_odd)):
            out[pl.ds(k * NODE, NODE), :] = got[pl.ds(edge * NODE, NODE), :]
    for out in outs:
        even, odd = tiles[0][16].astype(F32), tiles[1][16].astype(F32)
        own = out[14].astype(F32)
        out[14] = jnp.where(row == ROWS, even, jnp.where(row == ROWS + 1, odd, own)).astype(BF16)


def second_py_kernel(flow, r_even, r_odd, in_even, in_odd, n_even, n_odd):
    par = parity()
    n_even[...] = in_even[...]
    n_odd[...] = in_odd[...]
    py_fill(par, Tiles(r_even), Tiles(r_odd), (Tiles(n_even), Tiles(n_odd)))


def decay_kernel(flow, after, field, memory, charge, relaxation, out, full, scratch):
    terms = memory.shape[0]
    flow.wait(field, memory, charge, relaxation)
    wide = [twice(charge[x]) for x in range(ROWS)]
    rates = [[twice(relaxation[q, x]) for q in range(terms)] for x in range(ROWS)]
    coefs = []
    for x in range(ROWS):
        w0 = w1 = w2 = 0.0
        for rate in rates[x]:
            w0 = w0 + (1.0 - rate)
            w1 = w1 + rate * (1.0 - rate)
            w2 = w2 + rate * rate * (1.0 - rate)
        coefs.append((wide[x], w0, w1, w2))
        for j in range(4):
            full[COEF + j * ROWS + x] = coefs[x][j]

    def region(base):
        return full.at[pl.ds(base, OWN)]

    def total(x, r):
        acc = memory[0, x, :, lanes(r)]
        for q in range(1, terms):
            acc = acc + memory[q, x, :, lanes(r)]
        return acc

    to_plain(lambda x, r: field[x, :, lanes(r)], scratch, region(FIELD))
    to_plain(total, scratch, region(SUM0))
    to_plain(lambda x, r: total(x, r) * -wide[x], scratch, region(ADDEND))
    for power, base in ((1, SUM1), (2, SUM2), (3, SUM3)):
        scale = [[rate if power == 1 else rate * rate if power == 2 else rate * rate * rate for rate in row] for row in rates]

        def part(x, r):
            acc = coefs[x][power] * field[x, :, lanes(r)]
            for q in range(terms):
                acc = acc + scale[x][q] * memory[q, x, :, lanes(r)]
            return acc

        to_plain(part, scratch, region(base))
    flow.send(full, out.at[pl.ds(0, KNOWN)])


class Coefs:
    def __init__(self, ref):
        self.ref = ref

    def __call__(self, j, block):
        return self.ref[j * ROWS + block // COLS, pl.ds(block % COLS, 1), :]


def outer_places(par):
    row_even, row_odd = sides(par, 0, ROWS, -1)
    col_even, col_odd = sides(par, 1, COLS, -1)
    listed = []
    for array, row in ((0, row_even), (1, row_odd)):
        listed += [(array, y, place(row, y)) for y in range(COLS)]
    rows = [0, 1, 2, 3, row_even, row_odd]
    for array, col in ((2, col_even), (3, col_odd)):
        listed += [(array, j, place(row, col)) for j, row in enumerate(rows)]
    return listed


def weight_of(blocks, item):
    own, r_even, r_odd, n_even, n_odd, d_even, d_odd = blocks
    if item < OWN:
        return own[item // COLS, item % COLS]
    item -= OWN
    if item < 2 * COLS:
        return (r_even, r_odd)[item // COLS][pl.ds(item % COLS * NODE, NODE), :]
    side, j = (item - 2 * COLS) // (ROWS + 2), (item - 2 * COLS) % (ROWS + 2)
    if j < ROWS:
        return (d_even, d_odd)[side][j]
    return (n_even, n_odd)[side][pl.ds((j - ROWS) * NODE, NODE), :]


def targets_of(table, par):
    columns = sides(par, 1, 0, COLS - 1)

    def target(item, k):
        if item < OWN + 2 * COLS:
            return table[item // COLS, (item % COLS) * 8 + k]
        item -= OWN + 2 * COLS
        side, j = item // (ROWS + 2), item % (ROWS + 2)
        return table[8 + j, columns[side] * 8 + k + 64 * side]

    return target


def table_lines(par, lines, r_even, r_odd, n_even, n_odd):
    row = lax.broadcasted_iota(jnp.int32, (8, 128), 0)
    lane = lax.broadcasted_iota(jnp.int32, (8, 128), 1)
    row_even, row_odd = sides(par, 0, ROWS, -1)
    line = jnp.where(row == ROWS, row_even, jnp.where(row == ROWS + 1, row_odd, row))
    even = Tiles(r_even, PX_BASE)[16].astype(F32)[:8]
    odd = Tiles(r_odd, PX_BASE)[16].astype(F32)[:8]
    first = jnp.where(row == ROWS, even, jnp.where(row == ROWS + 1, odd, lines))
    parts = [first.astype(jnp.int32) + place(line, lane // 8)]
    ends = []
    for msg, col in zip((n_even, n_odd), sides(par, 1, COLS, -1)):
        ends.append(Tiles(msg, PY_BASE)[14].astype(F32)[:8].astype(jnp.int32) + place(line, col))
    parts.append(jnp.where(lane < 64, ends[0], pltpu.roll(ends[1], 64, 1)))
    return jnp.concatenate(parts, 0)


def forward_pair(par, target, ready, blocks, plain, received, field, middle, store_first, store_second):
    low = low_lanes(16)
    r_even, r_odd, n_even, n_odd = received

    def spread(pair, first, second):
        both = pair.astype(F32)
        field[first] = doubled(both[:8]).astype(BF16)
        field[second] = doubled(both[8:]).astype(BF16)

    row_bases = sides(par, 0, ROWS, -2)
    col_bases = sides(par, 1, COLS, -2)
    for msg, base in zip((r_even, r_odd), row_bases):
        for k in range(2):
            for p in range(4):
                at = place(base + k, 2 * p)
                spread(msg[k * 4 + p], at, at + 1)
    rows = [0, 1, 2, 3, row_bases[0], row_bases[0] + 1, row_bases[1], row_bases[1] + 1]
    for msg, base in zip((n_even, n_odd), col_bases):
        for j, row in enumerate(rows):
            at = place(row, base)
            spread(msg[j], at, at + 1)
    ready()
    for block in range(OWN):
        field[place(block // COLS, block % COLS)] = doubled(plain(block)).astype(BF16)

    def product(source, item):
        parts = []
        for m in range(4):
            one = source[target(item, 2 * m)]
            two = source[target(item, 2 * m + 1)]
            parts.append(jnp.where(low, one, two))
        picked = jnp.concatenate(parts, 1)
        out = lax.dot_general(
            picked, weight_of(blocks, item), (((1,), (1,)), ((), ())), preferred_element_type=F32
        )
        return unpacked(out)

    for number, (array, index, at) in enumerate(outer_places(par)):
        got = product(field, OWN + number) + joined(received[array][8 + index])
        middle[at] = doubled(got).astype(BF16)
    for block in range(OWN):
        got = store_first(block, product(field, block))
        middle[place(block // COLS, block % COLS)] = doubled(got).astype(BF16)
    for block in range(OWN):
        store_second(block, product(middle, block))


def forward_one(
    flow, lines, own, r_even, r_odd, n_even, n_odd, d_even, d_odd, stored, past, now, m_even, m_odd, p_even, p_odd, table_out,
    coefs_out, n_odd_out, d_even_out, d_odd_out,
    field, middle, table, known,
):
    par = parity()
    begun = flow.copy(stored.at[pl.ds(0, 2 * OWN)], known.at[pl.ds(0, 2 * OWN)])
    rest = flow.copy(stored.at[pl.ds(2 * OWN, KNOWN - 2 * OWN)], known.at[pl.ds(2 * OWN, KNOWN - 2 * OWN)])
    table_out[...] = table_lines(par, lines[...], r_even, r_odd, n_even, n_odd)
    looked = flow.copy(table_out, table)
    coef = Coefs(known.at[pl.ds(COEF, 4 * ROWS)])

    def ready():
        looked.wait()
        begun.wait()

    def first(block, out):
        if block == 0:
            rest.wait()
        got = out + known[ADDEND + block]
        past[block] = got
        full = known[SUM2 + block] + coef(1, block) * got
        past[OWN + block] = full
        now[OWN + block] = -coef(0, block) * full
        return got

    def second(block, out):
        now[block] = out - coef(0, block) * known[SUM1 + block]

    received = (Tiles(r_even, PX_BASE), Tiles(r_odd, PX_BASE), Tiles(n_even, PY_BASE), Tiles(n_odd, PY_BASE))
    forward_pair(
        par, targets_of(table, par), ready, (own, r_even, r_odd, n_even, n_odd, d_even, d_odd), lambda block: known[FIELD + block],
        received, field, middle, first, second,
    )
    get, add = (lambda at: now[at]), (lambda at: now[OWN + at])
    px_message(par, get, add, (Tiles(m_even), Tiles(m_odd)))
    coefs_out[...] = known[COEF:KNOWN]
    n_odd_out[...] = n_odd[...]
    d_even_out[...] = d_even[...]
    d_odd_out[...] = d_odd[...]
    py_message(par, get, add, (Tiles(p_even), Tiles(p_odd)))
    for block in range(OWN):
        now[2 * OWN + block] = known[SUM3 + block] + coef(2, block) * past[block] + coef(1, block) * now[block]


def turn_kernel(
    flow, table, own, r_even, r_odd, n_even, n_odd, d_even, d_odd, e_even, e_odd, s_even, s_odd, now, coefs, spread, counted,
    adjoint4, first_out, second_out, m_even, m_odd, field, middle, sums_one, sums_two, field3, field4,
):
    par = parity()
    blocks = (own, r_even, r_odd, n_even, n_odd, d_even, d_odd)
    target = targets_of(table, par)
    coef = Coefs(coefs)

    def first(block, out):
        got = out + now[OWN + block]
        field3[block] = got
        return got

    def second(block, out):
        field4[block] = out - coef(0, block) * now[2 * OWN + block]

    received = (Tiles(e_even), Tiles(e_odd), Tiles(s_even), Tiles(s_odd))
    clear(sums_one, sums_two)
    forward_pair(
        par, target, lambda: None, blocks, lambda block: now[block], received, field, middle, first, second
    )
    def start(block):
        value = injected(4, counted, field4[block], spread, block)
        adjoint4[block] = value
        return value

    def add_first(block):
        return injected(3, counted, field3[block], spread, block)

    def add_second(block):
        memory = coef(0, block) * coef(1, block) * adjoint4[block]
        return injected(2, counted, now[block], spread, block) - memory

    adjoint_pair(
        par, target, blocks, start, add_first, add_second, (first_out, second_out, m_even, m_odd), sums_one, sums_two
    )


def clear(*refs):
    for ref in refs:
        zero = jnp.zeros(ref.shape[1:], F32)
        for at in range(ref.shape[0]):
            ref[at] = zero


def adjoint_pair(par, target, blocks, start, add_first, add_second, outs, middle, last):
    first_out, second_out, m_even, m_odd = outs
    low = low_lanes(16)

    def push(sums_ref, item, rows):
        out = lax.dot_general(
            rows, weight_of(blocks, item), (((1,), (0,)), ((), ())), preferred_element_type=F32
        )
        spots = [target(item, k) for k in range(8)]
        sums = []
        for k in range(8):
            part = out[:, (k // 2) * 128 : (k // 2 + 1) * 128]
            part = jnp.where(low, part, 0.0) if k % 2 == 0 else jnp.where(low, 0.0, part)
            sums.append(sums_ref[spots[k]] + part)
        for k in range(8):
            sums_ref[spots[k]] = sums[k]

    def both(sums_ref, at):
        value = sums_ref[at]
        return value + pltpu.roll(value, 64, 1)

    def plain_of(value):
        return jnp.where(low_lanes(8), value[:8], value[8:])

    for block in range(OWN):
        push(middle, block, packed(start(block)).astype(BF16))
    rows_at = sides(par, 0, ROWS, -1)
    for number, (array, index, at) in enumerate(outer_places(par)):
        value = both(middle, at)
        push(last, OWN + number, value[:, :64].astype(BF16))
    for out, row in zip((m_even, m_odd), rows_at):
        for j in range(0, COLS + 2, 2):
            out[j // 2] = paired(plain_of(both(middle, place(row, j + i - 1))) for i in range(2))
    for x in range(ROWS):
        for j in range(COLS + 2):
            value = plain_of(both(middle, place(x, j - 1)))
            if 1 <= j <= COLS:
                block = x * COLS + j - 1
                value = value + add_first(block)
                push(last, block, packed(value).astype(BF16))
            first_out[x * (COLS + 2) + j] = value
    for out, base in zip((m_even, m_odd), sides(par, 0, ROWS, -2)):
        for k in range(2):
            for j in range(0, WIDE, 2):
                at = COLS // 2 + 1 + (k * WIDE + j) // 2
                out[at] = paired(plain_of(both(last, place(base + k, j + i - 2))) for i in range(2))
    for x in range(ROWS):
        for j in range(WIDE):
            value = plain_of(both(last, place(x, j - 2)))
            if 2 <= j < COLS + 2:
                value = value + add_second(x * COLS + j - 2)
            second_out[x * WIDE + j] = value


def paired(blocks):
    return jnp.concatenate(list(blocks), 0).astype(BF16)


def add_pair(target, at, pair):
    both = pair.astype(F32)
    target[at] += both[:8]
    target[at + 1] += both[8:]


def adjoint_py_kernel(flow, first, second, r_even, r_odd, first_own, second_own, n_even, n_odd, one, two):
    par = parity()
    one[...] = first[...]
    two[...] = second[...]
    for msg, row, base in zip((r_even, r_odd), sides(par, 0, 3, 0), sides(par, 0, 2, 0)):
        for j in range(0, COLS + 2, 2):
            add_pair(one, row * (COLS + 2) + j, msg[j // 2])
        for k in range(2):
            for j in range(0, WIDE, 2):
                add_pair(two, (base + k) * WIDE + j, msg[COLS // 2 + 1 + (k * WIDE + j) // 2])
    for out, col, base in zip((n_even, n_odd), sides(par, 1, COLS + 1, 0), sides(par, 1, COLS + 2, 0)):
        for x in range(ROWS):
            out[2 + x] = paired(two[x * WIDE + base + k] for k in range(2))
        for h in range(2):
            out[h] = paired(one[(2 * h + i) * (COLS + 2) + col] for i in range(2))
    for x in range(ROWS):
        for y in range(COLS):
            first_own[x * COLS + y] = one[x * (COLS + 2) + 1 + y]
            second_own[x * COLS + y] = two[x * WIDE + 2 + y]


def settle(par, first_own, second_own, n_even, n_odd, first, second):
    first[...] = first_own[...]
    second[...] = second_own[...]
    for msg, col, base in zip((n_even, n_odd), sides(par, 1, 7, 0), sides(par, 1, 6, 0)):
        for x in range(ROWS):
            add_pair(second, x * COLS + base, msg[2 + x])
        for h in range(2):
            both = msg[h].astype(F32)
            first[2 * h * COLS + col] += both[:8]
            first[(2 * h + 1) * COLS + col] += both[8:]


def injected(moment, counted, field, spread, block):
    return counted[moment - 1, block] * field - spread[moment - 1, block]


def adjoint_two(
    flow, table, own, r_even, r_odd, n_even, n_odd, d_even, d_odd, first_own, second_own, e_even, e_odd, adjoint4, past, coefs,
    spread, counted, later, first_out, second_out, m_even, m_odd, sums_one, sums_two,
):
    par = parity()
    clear(sums_one, sums_two)
    adjoint3, adjoint2 = later.at[pl.ds(0, OWN)], later.at[pl.ds(OWN, OWN)]
    settle(par, first_own, second_own, e_even, e_odd, adjoint3, adjoint2)
    coef = Coefs(coefs)

    def add_first(block):
        memory = coef(2, block) * adjoint4[block] + coef(1, block) * adjoint3[block]
        return injected(1, counted, past[block], spread, block) - coef(0, block) * memory

    def add_second(block):
        memory = coef(3, block) * adjoint4[block] + coef(2, block) * adjoint3[block] + coef(1, block) * adjoint2[block]
        return -coef(0, block) * memory

    adjoint_pair(
        par, targets_of(table, par), (own, r_even, r_odd, n_even, n_odd, d_even, d_odd), lambda block: adjoint2[block], add_first,
        add_second, (first_out, second_out, m_even, m_odd), sums_one, sums_two,
    )


def gradient_kernel(flow, after, adjoint4, later, stored, past, now, out, known):
    flow.fetch(stored.at[pl.ds(0, KNOWN)], known)
    flow.wait(known)
    for block in range(OWN):
        out[block] = (
            adjoint4[block] * now[2 * OWN + block] + later[block] * past[OWN + block]
            + later[OWN + block] * known[SUM1 + block]
        )
        out[OWN + block] = known[SUM0 + block]


def finish_kernel(
    flow, first_own, second_own, n_even, n_odd, before, result, gradient, adjoint1, adjoint0, scratch
):
    par = parity()
    settle(par, first_own, second_own, n_even, n_odd, adjoint1, adjoint0)
    for x in range(ROWS):
        parts = []
        for y in range(COLS):
            block = x * COLS + y
            scratch[pl.ds(x * 64 + y * 8, 8), :] = adjoint0[block]
            value = before[block] + adjoint1[block] * before[OWN + block]
            parts.append(jnp.sum(value, axis=0, keepdims=True))
        rows = jnp.concatenate(parts, 0)
        gradient[x] = -(rows[:, :64] + rows[:, 64:])
        for r in range(8):
            result[x, :, lanes(r)] = scratch[pl.ds(x * 64 + r, 8, stride=8), :]


def split(value):
    high = value.astype(BF16)
    return high, (value - high.astype(F32)).astype(BF16)


def owner_slots(steps, observed, part, node, slots_of):
    owned = observed.shape[0]
    slots = slots_of.shape[0]
    devices = slots // CAP
    row = lax.broadcasted_iota(jnp.int32, (128, 128), 0)
    col = lax.broadcasted_iota(jnp.int32, (128, 128), 1)
    gate = row // 16
    source = row % 16
    step = jnp.zeros((128, 128), jnp.int32)
    for g in range(8):
        step = jnp.where(gate == g, jnp.broadcast_to(steps[0:1, g : g + 1], (128, 128)), step)
    wanted = 2 * (col % 8) + (col // 8) % 2
    chosen = ((step == col // 16 + 1) & (source == wanted) & (col < 64)).astype(F32).astype(BF16)
    high, low = split(observed[...])
    dot = lambda a, b: lax.dot_general(a, b, (((1,), (0,)), ((), ())), preferred_element_type=F32)
    sums = dot(high, chosen) + dot(low, chosen)
    dest = part[...]
    member = (dest == lax.broadcasted_iota(jnp.int32, (devices, owned), 0)).astype(F32)
    earlier = (
        lax.broadcasted_iota(jnp.int32, (owned, owned), 0) < lax.broadcasted_iota(jnp.int32, (owned, owned), 1)
    ).astype(F32).astype(BF16)
    ahead = dot(member.astype(BF16), earlier)
    rank = jnp.sum(ahead * member, axis=0, keepdims=True).astype(jnp.int32)
    position = dest * CAP + rank
    where = (position == lax.broadcasted_iota(jnp.int32, (slots, owned), 0)).astype(F32).astype(BF16)
    line = lax.broadcasted_iota(jnp.int32, (128, owned), 0)
    which = node[...]
    block = lax.shift_right_logical(which, 6)
    inner = which - block * 64
    marks = jnp.where(line == 64, block, jnp.where(line == 65, inner, jnp.where(line == 66, 1, 0)))
    high, low = split(sums)
    turned = lambda a, b: lax.dot_general(a, b, (((1,), (1,)), ((), ())), preferred_element_type=F32)
    slots_of[...] = dot(where, high) + dot(where, low) + turned(where, marks.astype(F32).astype(BF16))


def holder_kernel(flow, steps, slots, after, spread, counted):
    flow.wait(slots)
    tally = []
    for n in range(4):
        total = jnp.zeros((), F32)
        for g in range(8):
            total = total + jnp.where(steps[g] == n + 1, 1.0, 0.0)
        tally.append(total)
    values = slots[...]
    count = values.shape[0]
    lane = lax.broadcasted_iota(jnp.int32, (count, 128), 1)
    pick = lambda at: jnp.sum(jnp.where(lane == at, values, 0.0), axis=1, keepdims=True)
    place_of = jnp.where(pick(66) > 0.5, pick(64) * 64.0 + pick(65), -1.0).astype(jnp.int32)
    high, low = split(values.T)
    both = jnp.concatenate([high, low], 0)
    low8 = low_lanes(8)
    for chunk in range(OWN * 64 // 256):
        spots = lax.broadcasted_iota(jnp.int32, (count, 256), 1) + chunk * 256
        hot = (place_of == spots).astype(F32).astype(BF16)
        out = lax.dot_general(both, hot, (((1,), (0,)), ((), ())), preferred_element_type=F32)
        out = out[:128] + out[128:]
        for j in range(2):
            first = chunk * 4 + 2 * j
            for n in range(4):
                even = out[n * 16 : n * 16 + 8, j * 128 : (j + 1) * 128]
                odd = out[n * 16 + 8 : n * 16 + 16, j * 128 : (j + 1) * 128]
                spread[n, first] = jnp.where(low8, even, pltpu.roll(odd, 64, 1))
                spread[n, first + 1] = jnp.where(low8, pltpu.roll(even, 64, 1), odd)
            many = jnp.broadcast_to(out[66:67, j * 128 : (j + 1) * 128], (8, 128))
            other = pltpu.roll(many, 64, 1)
            for n in range(4):
                counted[n, first] = jnp.where(low8, many, other) * tally[n]
                counted[n, first + 1] = jnp.where(low8, other, many) * tally[n]


def swap_even(axis):
    return [(i, i ^ 1) for i in range(lax.axis_size(axis))]


def swap_odd(axis):
    inner = range(1, lax.axis_size(axis) - 1, 2)
    return [(i, i + 1) for i in inner] + [(i + 1, i) for i in inner]


def exchange(axis, for_even, for_odd):
    return lax.ppermute(for_even, axis, swap_even(axis)), lax.ppermute(for_odd, axis, swap_odd(axis))


def body(
    checkpoint_field,
    checkpoint_memory,
    stiffness,
    block_offsets,
    chargeability,
    relaxation,
    observed,
    receiver_part,
    receiver_node,
    gate_step,
):
    devices = lax.axis_size(("px", "py"))
    slots = devices * CAP
    turn = pltpu.VMEM((256, 128), F32)
    lookup = pltpu.SMEM((16, 128), jnp.int32)
    places = pltpu.VMEM((PLACES, 16, 128), BF16)
    sums = pltpu.VMEM((PLACES, 16, 128), F32)
    blocks = pltpu.VMEM((OWN, 8, 128), F32)
    px_first = ((PX_BASE + 80, WIDTH), BF16, "v")
    py_first = ((PY_BASE + 64, WIDTH), BF16, "v")
    px_shape = ((16, 16, 128), BF16, "v")
    py_shape = ((14, 16, 128), BF16, "v")
    down = ((ROWS, NODE, WIDTH), BF16, "v")
    two = (2,) + py_first[0]
    m_even, m_odd, both, d_even, d_odd, lines, sent = call(
        start_kernel,
        [
            px_first[:2] + ("h",), px_first[:2] + ("h",), (two, BF16, "h"), down[:2] + ("h",), down[:2] + ("h",),
            ((8, 128), F32, "v"), ((slots, 128), F32, "h"),
        ],
        [
            (gate_step.reshape(1, -1), "h"), (observed, "h"), (receiver_part.reshape(1, -1), "h"),
            (receiver_node.reshape(1, -1), "h"), (block_offsets, "h"), (checkpoint_field, "h"),
            (checkpoint_memory, "h"), (chargeability, "h"), (stiffness, "b"),
        ],
        [blocks, blocks, turn, pltpu.VMEM((slots, 128), F32)]
        + [pltpu.VMEM(shape, BF16) for shape in (px_first[0], px_first[0], two, down[0], down[0])],
        copies=2 * COLS + 2 * ROWS + 8, vmem=65 * 1000 * 1000,
    )
    r_even, r_odd = exchange("px", m_even, m_odd)
    d_even, d_odd = exchange("py", d_even, d_odd)
    sent, r_even = lax.optimization_barrier((sent, r_even))
    held = lax.all_to_all(
        sent.reshape(devices, CAP, 128), ("px", "py"), split_axis=0, concat_axis=0, tiled=True
    ).reshape(slots, 128)
    n_even, n_odd = call(
        first_py_kernel, [py_first, py_first],
        [(r_even, "v"), (r_odd, "v"), (both, "v")],
    )
    (known,) = call(
        decay_kernel, [((ROOM, 8, 128), F32, "h")],
        [(n_even, "v"), (checkpoint_field, "h"), (checkpoint_memory, "h"), (chargeability, "h"), (relaxation, "h")],
        [pltpu.VMEM((KNOWN, 8, 128), F32), turn], copies=1, vmem=VMEM_MOST,
    )
    n_even, n_odd = exchange("py", n_even, n_odd)
    held, n_even = lax.optimization_barrier((held, n_even))
    weights = [(a, "v") for a in (stiffness, r_even, r_odd, n_even, n_odd, d_even, d_odd)]
    past, now, m_even, m_odd, p_even, p_odd, table, coefs, *late = call(
        forward_one,
        [
            ((2 * OWN, 8, 128), F32, "v"), ((3 * OWN, 8, 128), F32, "v"), px_shape, px_shape, py_shape, py_shape,
            ((16, 128), jnp.int32, "v"), ((4 * ROWS, 8, 128), F32, "v"), py_first, down, down,
        ],
        [(lines, "v")] + weights + [(known, "b")],
        [places, places, lookup, pltpu.VMEM((KNOWN, 8, 128), F32)], copies=3,
    )
    weights = weights[:4] + [(a, "v") for a in late]
    r_even, r_odd = exchange("px", m_even, m_odd)
    n_even, n_odd = call(
        second_py_kernel, [py_shape, py_shape],
        [(r_even, "v"), (r_odd, "v"), (p_even, "v"), (p_odd, "v")],
    )
    n_even, n_odd = exchange("py", n_even, n_odd)
    spread, counted = call(
        holder_kernel, [((4, OWN, 8, 128), F32, "v"), ((4, OWN, 8, 128), F32, "v")],
        [(gate_step, "s"), (held, "h"), (m_even, "v")],
    )
    rim = ((COLS // 2 + 1 + WIDE, 16, 128), BF16, "v")
    rim_py = ((6, 16, 128), BF16, "v")
    pair_out = [
        ((ROWS * (COLS + 2), 8, 128), F32, "v"), ((ROWS * WIDE, 8, 128), F32, "v"),
        rim, rim,
    ]
    adjoint4, *rest = call(
        turn_kernel, [PLAIN] + pair_out,
        [(table, "s")] + weights
        + [(r_even, "v"), (r_odd, "v"), (n_even, "v"), (n_odd, "v"), (now, "v"), (coefs, "v"), (spread, "v"), (counted, "v")],
        [places, places, sums, sums, blocks, blocks],
    )

    def gathered(first, second, m_even, m_odd):
        r_even, r_odd = exchange("px", m_even, m_odd)
        own_first, own_second, n_even, n_odd = call(
            adjoint_py_kernel, [PLAIN, PLAIN, rim_py, rim_py],
            [(first, "v"), (second, "v"), (r_even, "v"), (r_odd, "v")],
            [pltpu.VMEM(first.shape, F32), pltpu.VMEM(second.shape, F32)],
        )
        n_even, n_odd = exchange("py", n_even, n_odd)
        return [(a, "v") for a in (own_first, own_second, n_even, n_odd)]

    later, *rest = call(
        adjoint_two, [((2 * OWN, 8, 128), F32, "v")] + pair_out,
        [(table, "s")] + weights + gathered(*rest)
        + [(adjoint4, "v"), (past, "v"), (coefs, "v"), (spread, "v"), (counted, "v")],
        [sums, sums],
    )
    (before,) = call(
        gradient_kernel, [((2 * OWN, 8, 128), F32, "v")],
        [(a, "b" if a is known else "v") for a in (rest[2], adjoint4, later, known, past, now)],
        [pltpu.VMEM((KNOWN, 8, 128), F32)], copies=1,
    )
    field_out, gradient = call(
        finish_kernel, [(checkpoint_field.shape, F32, "v"), (chargeability.shape, F32, "v")],
        [] + gathered(*rest) + [(before, "v")], [blocks, blocks, turn],
    )
    return field_out, gradient


def solution(mesh):
    in_specs = (
        P("px", "py", None),
        P(None, "px", "py", None),
        P("px", "py", None, None),
        P("px", "py", None),
        P("px", "py", None),
        P(None, "px", "py", None),
        P(("px", "py"), None),
        P(("px", "py"), None),
        P(("px", "py")),
        P(),
    )
    out_specs = (P("px", "py", None), P("px", "py", None))
    return jax.shard_map(body, mesh=mesh, in_specs=in_specs, out_specs=out_specs, check_vma=False)
```

```python
import jax
import jax.numpy as jnp
from jax import lax
from jax.experimental import pallas as pl
from jax.experimental.pallas import tpu as pltpu
from jax.sharding import PartitionSpec as P

ROWS, COLS = 4, 8
OWN = ROWS * COLS
CAP = 8
WIDE = COLS + 4
PLACES = (ROWS + 4) * WIDE
F32, BF16 = jnp.float32, jnp.bfloat16
VMEM_BYTES, VMEM_MOST = 16 * 1024 * 1024, 63 * 1000 * 1000
NODE, WIDTH = 64, 512
FIELD, ADDEND, SUM0, SUM1, SUM2, SUM3, COEF = (i * OWN for i in range(7))
PX_BASE, PY_BASE = COLS * NODE, 2 * NODE
KNOWN, ROOM, PAGES = COEF + 4 * ROWS, 12288, 96


def place(row, col):
    return (row + 2) * WIDE + col + 2


def low_lanes(rows):
    return lax.broadcasted_iota(jnp.int32, (rows, 128), 1) < 64


def doubled(plain):
    turned = pltpu.roll(plain, 64, 1)
    low = low_lanes(8)
    return jnp.concatenate([jnp.where(low, plain, turned), jnp.where(low, turned, plain)], 0)


def packed(plain):
    return jnp.concatenate([plain[:, :64], plain[:, 64:]], 0)


def unpacked(rows):
    return jnp.concatenate([rows[:8], rows[8:]], 1)


def halves(plain):
    high = plain.astype(BF16).astype(F32)
    return jnp.concatenate([high, plain - high], 0).astype(BF16)


def joined(pair):
    pair = pair.astype(F32)
    return pair[:8] + pair[8:]


def parity():
    return lax.axis_index("px") % 2, lax.axis_index("py") % 2


def sides(par_ref, axis, near, far):
    even = par_ref[axis] == 0
    return jnp.where(even, near, far), jnp.where(even, far, near)


class Flow:
    def __init__(self, sems):
        self.sems, self.used, self.coming, self.going = sems, 0, {}, []

    def copy(self, source, target):
        made = pltpu.make_async_copy(source, target, self.sems.at[self.used])
        self.used += 1
        made.start()
        return made

    def wait(self, *refs):
        for ref in refs:
            for made in self.coming.pop(id(ref), ()):
                made.wait()

    def fetch(self, source, target):
        self.coming[id(target)] = [self.copy(source, target)]

    def send(self, source, target):
        self.going.append(self.copy(source, target))

    def finish(self):
        for key in list(self.coming):
            for made in self.coming.pop(key):
                made.wait()
        for made in self.going:
            made.wait()


def call(kernel, outs, inputs, scratch=(), copies=0, vmem=VMEM_BYTES):
    spaces = {"s": pltpu.SMEM, "v": pltpu.VMEM, "h": pltpu.HBM, "b": pltpu.HBM}
    arrays = [array for array, _ in inputs]
    fetched = [i for i, (_, kind) in enumerate(inputs) if kind == "h"]
    total = len(fetched) + copies

    def wrapped(*refs):
        refs = list(refs)
        buffers = refs[len(inputs) + len(outs) + len(scratch) :]
        flow = Flow(buffers[-1])
        for buffer, i in zip(buffers, fetched):
            flow.coming[id(buffer)] = [flow.copy(refs[i], buffer)]
            refs[i] = buffer
        kernel(flow, *refs[: len(inputs) + len(outs) + len(scratch)])
        flow.finish()

    buffers = [pltpu.VMEM(arrays[i].shape, arrays[i].dtype) for i in fetched]
    return pl.pallas_call(
        wrapped,
        out_shape=[jax.ShapeDtypeStruct(shape, dtype) for shape, dtype, _ in outs],
        in_specs=[pl.BlockSpec(memory_space=spaces[kind]) for _, kind in inputs],
        out_specs=[pl.BlockSpec(memory_space=spaces[kind]) for _, _, kind in outs],
        scratch_shapes=list(scratch) + buffers + [pltpu.SemaphoreType.DMA((max(total, 1),))],
        compiler_params=pltpu.CompilerParams(vmem_limit_bytes=vmem),
    )(*arrays)


PLAIN = ((OWN, 8, 128), F32, "v")


class Tiles:
    def __init__(self, ref, base=None):
        self.ref, self.base = ref, base

    def at(self, t):
        if self.base is None:
            return (t,)
        return pl.ds(self.base + 16 * (t // 4), 16), pl.ds(128 * (t % 4), 128)

    def __getitem__(self, t):
        return self.ref[self.at(t)]

    def __setitem__(self, t, value):
        self.ref[self.at(t)] = value


def to_plain(native, scratch, out):
    for x in range(ROWS):
        for r in range(8):
            scratch[pl.ds(x * 64 + r * 8, 8), :] = native(x, r)
    for x in range(ROWS):
        for y in range(COLS):
            out[x * COLS + y] = scratch[pl.ds(x * 64 + y, 8, stride=8), :]


def lanes(r):
    return pl.ds(r * 128, 128)


def twice(rows):
    return jnp.concatenate([rows, rows], 1)


def px_message(par, plain, addend, outs):
    bases = sides(par, 0, 2, 0)
    edges = sides(par, 0, 3, 0)
    for out, base, edge in zip(outs, bases, edges):
        for k in range(2):
            for p in range(4):
                at = (base + k) * COLS + 2 * p
                out[k * 4 + p] = jnp.concatenate([plain(at), plain(at + 1)], 0).astype(BF16)
        for y in range(COLS):
            out[8 + y] = halves(addend(edge * COLS + y))


def py_message(par, plain, addend, outs):
    pairs = sides(par, 1, 3, 0)
    edges = sides(par, 1, 7, 0)
    for out, pair, edge in zip(outs, pairs, edges):
        for x in range(ROWS):
            at = x * COLS + 2 * pair
            out[x] = jnp.concatenate([plain(at), plain(at + 1)], 0).astype(BF16)
            out[8 + x] = halves(addend(x * COLS + edge))


def picked_tile(tiles, choice, low, high):
    return jnp.where(choice == 0, tiles[low].astype(F32), tiles[high].astype(F32)).astype(BF16)


def py_fill(par, r_even, r_odd, outs):
    edges = sides(par, 1, 7, 0)
    for out, edge in zip(outs, edges):
        for k in range(2):
            out[4 + k] = picked_tile(r_even, edge, k * 4, k * 4 + 3)
            out[6 + k] = picked_tile(r_odd, edge, k * 4, k * 4 + 3)
        out[12] = picked_tile(r_even, edge, 8, 15)
        out[13] = picked_tile(r_odd, edge, 8, 15)


def shift_lines(offsets):
    row = lax.broadcasted_iota(jnp.int32, (8, 128), 0)
    lane = lax.broadcasted_iota(jnp.int32, (8, 128), 1)
    repeat = ((lane % 8 == row) & (lane < 64)).astype(F32).astype(BF16)
    lines = jnp.zeros((8, 128), F32)
    for x in range(ROWS):
        codes = offsets[x].astype(F32).astype(BF16)
        wide = lax.dot_general(codes, repeat, (((1,), (0,)), ((), ())), preferred_element_type=F32)
        line = jnp.sum(jnp.where(lane // 8 == row, wide, 0.0), axis=0, keepdims=True)
        lines = jnp.where(row == x, line, lines)
    above = (lines > 2.5).astype(F32) + (lines > 5.5).astype(F32)
    return 9.0 * above + lines - 13.0


def start_kernel(
    flow, steps, observed, part, node, offsets, field, memory, charge, stiffness,
    m_even_out, m_odd_out, both_out, d_even_out, d_odd_out, lines, sent,
    plain, addend, scratch, slots_of, m_even, m_odd, both, d_even, d_odd,
):
    par = parity()
    for out, edge in zip((m_even, m_odd), sides(par, 0, ROWS - 1, 0)):
        flow.coming[id(out)] = [
            flow.copy(stiffness.at[edge, y], out.at[pl.ds(y * NODE, NODE), :]) for y in range(COLS)
        ]
    for out, edge in zip((d_even, d_odd), sides(par, 1, COLS - 1, 0)):
        flow.coming[id(out)] = [flow.copy(stiffness.at[x, edge], out.at[x]) for x in range(ROWS)]
    flow.wait(steps, observed, part, node)
    owner_slots(steps, observed, part, node, slots_of)
    flow.send(slots_of, sent)
    flow.wait(offsets)
    found = shift_lines(offsets)
    lines[...] = found
    px_tiles = [Tiles(m_even, PX_BASE), Tiles(m_odd, PX_BASE)]
    py_tiles = [Tiles(both.at[0], PY_BASE), Tiles(both.at[1], PY_BASE)]
    flow.wait(m_even, m_odd, d_even, d_odd)
    for source, out in ((m_even, m_even_out), (m_odd, m_odd_out)):
        flow.send(source.at[pl.ds(0, PX_BASE), :], out.at[pl.ds(0, PX_BASE), :])
    flow.send(d_even, d_even_out)
    flow.send(d_odd, d_odd_out)
    for out, edge in zip(px_tiles, sides(par, 0, ROWS - 1, 0)):
        line = jnp.where(edge == 0, found[0:1], found[ROWS - 1 : ROWS])
        out[16] = jnp.broadcast_to(line, (16, 128)).astype(BF16)
    for out in py_tiles:
        out[14] = jnp.concatenate([found, jnp.zeros((8, 128), F32)], 0).astype(BF16)
    flow.wait(field, memory, charge)
    terms = memory.shape[0]
    to_plain(lambda x, r: field[x, :, lanes(r)], scratch, plain)

    def total(x, r):
        acc = memory[0, x, :, lanes(r)]
        for q in range(1, terms):
            acc = acc + memory[q, x, :, lanes(r)]
        return acc * -twice(charge[x])

    to_plain(total, scratch, addend)
    get, add = (lambda at: plain[at]), (lambda at: addend[at])
    px_message(par, get, add, px_tiles)
    for source, out in ((m_even, m_even_out), (m_odd, m_odd_out)):
        flow.send(source.at[pl.ds(PX_BASE, 80), :], out.at[pl.ds(PX_BASE, 80), :])
    py_message(par, get, add, py_tiles)
    flow.send(both.at[:, pl.ds(PY_BASE, 64), :], both_out.at[pl.ds(0, 2), pl.ds(PY_BASE, 64), :])


def first_py_kernel(flow, r_even, r_odd, given, n_even, n_odd):
    par = parity()
    part = pl.ds(PY_BASE, 64)
    own = [flow.copy(given.at[i, part, :], out.at[part, :]) for i, out in enumerate((n_even, n_odd))]
    tiles = [Tiles(r_even, PX_BASE), Tiles(r_odd, PX_BASE)]
    outs = [Tiles(n_even, PY_BASE), Tiles(n_odd, PY_BASE)]
    row = lax.broadcasted_iota(jnp.int32, (16, 128), 0)
    for out, edge in zip((n_even, n_odd), sides(par, 1, COLS - 1, 0)):
        for k, got in enumerate((r_even, r_odd)):
            out[pl.ds(k * NODE, NODE), :] = got[pl.ds(edge * NODE, NODE), :]
    for copied in own:
        copied.wait()
    py_fill(par, tiles[0], tiles[1], outs)
    for out in outs:
        even, odd = tiles[0][16].astype(F32), tiles[1][16].astype(F32)
        own = out[14].astype(F32)
        out[14] = jnp.where(row == ROWS, even, jnp.where(row == ROWS + 1, odd, own)).astype(BF16)


def second_py_kernel(flow, r_even, r_odd, in_even, in_odd, n_even, n_odd):
    par = parity()
    n_even[...] = in_even[...]
    n_odd[...] = in_odd[...]
    py_fill(par, Tiles(r_even), Tiles(r_odd), (Tiles(n_even), Tiles(n_odd)))


def decay_kernel(flow, after, field, memory, charge, relaxation, out, full, scratch):
    terms = memory.shape[0]
    flow.wait(field, memory, charge, relaxation)
    wide = [twice(charge[x]) for x in range(ROWS)]
    rates = [[twice(relaxation[q, x]) for q in range(terms)] for x in range(ROWS)]
    coefs = []
    for x in range(ROWS):
        w0 = w1 = w2 = 0.0
        for rate in rates[x]:
            w0 = w0 + (1.0 - rate)
            w1 = w1 + rate * (1.0 - rate)
            w2 = w2 + rate * rate * (1.0 - rate)
        coefs.append((wide[x], w0, w1, w2))
        for j in range(4):
            full[COEF + j * ROWS + x] = coefs[x][j]

    def region(base):
        return full.at[pl.ds(base, OWN)]

    def total(x, r):
        acc = memory[0, x, :, lanes(r)]
        for q in range(1, terms):
            acc = acc + memory[q, x, :, lanes(r)]
        return acc

    to_plain(lambda x, r: field[x, :, lanes(r)], scratch, region(FIELD))
    to_plain(total, scratch, region(SUM0))
    to_plain(lambda x, r: total(x, r) * -wide[x], scratch, region(ADDEND))
    for power, base in ((1, SUM1), (2, SUM2), (3, SUM3)):
        scale = [[rate if power == 1 else rate * rate if power == 2 else rate * rate * rate for rate in row] for row in rates]

        def part(x, r):
            acc = coefs[x][power] * field[x, :, lanes(r)]
            for q in range(terms):
                acc = acc + scale[x][q] * memory[q, x, :, lanes(r)]
            return acc

        to_plain(part, scratch, region(base))
    flow.send(full, out.at[pl.ds(0, KNOWN)])


class Coefs:
    def __init__(self, ref):
        self.ref = ref

    def __call__(self, j, block):
        return self.ref[j * ROWS + block // COLS, pl.ds(block % COLS, 1), :]


def outer_places(par):
    row_even, row_odd = sides(par, 0, ROWS, -1)
    col_even, col_odd = sides(par, 1, COLS, -1)
    listed = []
    for array, row in ((0, row_even), (1, row_odd)):
        listed += [(array, y, place(row, y)) for y in range(COLS)]
    rows = [0, 1, 2, 3, row_even, row_odd]
    for array, col in ((2, col_even), (3, col_odd)):
        listed += [(array, j, place(row, col)) for j, row in enumerate(rows)]
    return listed


def weight_of(blocks, item):
    own, r_even, r_odd, n_even, n_odd, d_even, d_odd = blocks
    if item < OWN:
        return own[item // COLS, item % COLS]
    item -= OWN
    if item < 2 * COLS:
        return (r_even, r_odd)[item // COLS][pl.ds(item % COLS * NODE, NODE), :]
    side, j = (item - 2 * COLS) // (ROWS + 2), (item - 2 * COLS) % (ROWS + 2)
    if j < ROWS:
        return (d_even, d_odd)[side][j]
    return (n_even, n_odd)[side][pl.ds((j - ROWS) * NODE, NODE), :]


def targets_of(table, par):
    columns = sides(par, 1, 0, COLS - 1)

    def target(item, k):
        if item < OWN + 2 * COLS:
            return table[item // COLS, (item % COLS) * 8 + k]
        item -= OWN + 2 * COLS
        side, j = item // (ROWS + 2), item % (ROWS + 2)
        return table[8 + j, columns[side] * 8 + k + 64 * side]

    return target


def table_lines(par, lines, r_even, r_odd, n_even, n_odd):
    row = lax.broadcasted_iota(jnp.int32, (8, 128), 0)
    lane = lax.broadcasted_iota(jnp.int32, (8, 128), 1)
    row_even, row_odd = sides(par, 0, ROWS, -1)
    line = jnp.where(row == ROWS, row_even, jnp.where(row == ROWS + 1, row_odd, row))
    even = Tiles(r_even, PX_BASE)[16].astype(F32)[:8]
    odd = Tiles(r_odd, PX_BASE)[16].astype(F32)[:8]
    first = jnp.where(row == ROWS, even, jnp.where(row == ROWS + 1, odd, lines))
    parts = [first.astype(jnp.int32) + place(line, lane // 8)]
    ends = []
    for msg, col in zip((n_even, n_odd), sides(par, 1, COLS, -1)):
        ends.append(Tiles(msg, PY_BASE)[14].astype(F32)[:8].astype(jnp.int32) + place(line, col))
    parts.append(jnp.where(lane < 64, ends[0], pltpu.roll(ends[1], 64, 1)))
    return jnp.concatenate(parts, 0)


def forward_pair(par, target, arrive, ready, arrived, blocks, plain, received, field, middle, store_first, store_second):
    low = low_lanes(16)
    r_even, r_odd, n_even, n_odd = received

    def spread(pair, first, second):
        both = pair.astype(F32)
        field[first] = doubled(both[:8]).astype(BF16)
        field[second] = doubled(both[8:]).astype(BF16)

    row_bases = sides(par, 0, ROWS, -2)
    col_bases = sides(par, 1, COLS, -2)
    for msg, base in zip((r_even, r_odd), row_bases):
        for k in range(2):
            for p in range(4):
                at = place(base + k, 2 * p)
                spread(msg[k * 4 + p], at, at + 1)
    arrive()
    rows = [0, 1, 2, 3, row_bases[0], row_bases[0] + 1, row_bases[1], row_bases[1] + 1]
    for msg, base in zip((n_even, n_odd), col_bases):
        for j, row in enumerate(rows):
            at = place(row, base)
            spread(msg[j], at, at + 1)
    ready()
    for block in range(OWN):
        field[place(block // COLS, block % COLS)] = doubled(plain(block)).astype(BF16)

    def product(source, item):
        parts = []
        for m in range(4):
            one = source[target(item, 2 * m)]
            two = source[target(item, 2 * m + 1)]
            parts.append(jnp.where(low, one, two))
        picked = jnp.concatenate(parts, 1)
        out = lax.dot_general(
            picked, weight_of(blocks, item), (((1,), (1,)), ((), ())), preferred_element_type=F32
        )
        return unpacked(out)

    arrived()
    for number, (array, index, at) in enumerate(outer_places(par)):
        got = product(field, OWN + number) + joined(received[array][8 + index])
        middle[at] = doubled(got).astype(BF16)
    for block in range(OWN):
        got = store_first(block, product(field, block))
        middle[place(block // COLS, block % COLS)] = doubled(got).astype(BF16)
    for block in range(OWN):
        store_second(block, product(middle, block))


def forward_one(
    flow, lines, own, r_even, r_odd, n_even, n_odd, d_even, d_odd, stored, past, now, m_even, m_odd, p_even, p_odd, table_out,
    coefs_out, n_odd_out, d_even_out, d_odd_out,
    field, middle, table, known,
):
    par = parity()
    begun = flow.copy(stored.at[pl.ds(0, 2 * OWN)], known.at[pl.ds(0, 2 * OWN)])
    rest = flow.copy(stored.at[pl.ds(2 * OWN, KNOWN - 2 * OWN)], known.at[pl.ds(2 * OWN, KNOWN - 2 * OWN)])
    looked = []

    def arrive():
        flow.wait(n_odd)
        table_out[...] = table_lines(par, lines[...], r_even, r_odd, n_even, n_odd)
        looked.append(flow.copy(table_out, table))

    coef = Coefs(known.at[pl.ds(COEF, 4 * ROWS)])

    def ready():
        begun.wait()
        looked[0].wait()

    def first(block, out):
        if block == 0:
            rest.wait()
        got = out + known[ADDEND + block]
        past[block] = got
        full = known[SUM2 + block] + coef(1, block) * got
        past[OWN + block] = full
        now[OWN + block] = -coef(0, block) * full
        return got

    def second(block, out):
        now[block] = out - coef(0, block) * known[SUM1 + block]

    received = (Tiles(r_even, PX_BASE), Tiles(r_odd, PX_BASE), Tiles(n_even, PY_BASE), Tiles(n_odd, PY_BASE))
    forward_pair(
        par, targets_of(table, par), arrive, ready, lambda: flow.wait(d_even, d_odd), (own, r_even, r_odd, n_even, n_odd, d_even, d_odd), lambda block: known[FIELD + block],
        received, field, middle, first, second,
    )
    get, add = (lambda at: now[at]), (lambda at: now[OWN + at])
    px_message(par, get, add, (Tiles(m_even), Tiles(m_odd)))
    coefs_out[...] = known[COEF:KNOWN]
    n_odd_out[...] = n_odd[...]
    d_even_out[...] = d_even[...]
    d_odd_out[...] = d_odd[...]
    py_message(par, get, add, (Tiles(p_even), Tiles(p_odd)))
    for block in range(OWN):
        now[2 * OWN + block] = known[SUM3 + block] + coef(2, block) * past[block] + coef(1, block) * now[block]


def turn_kernel(
    flow, table, own, r_even, r_odd, n_even, n_odd, d_even, d_odd, e_even, e_odd, s_even, s_odd, now, coefs, spread, counted,
    adjoint4, first_out, second_out, m_even, m_odd, field, middle, sums_one, sums_two, field3, field4,
):
    par = parity()
    blocks = (own, r_even, r_odd, n_even, n_odd, d_even, d_odd)
    target = targets_of(table, par)
    coef = Coefs(coefs)

    def first(block, out):
        got = out + now[OWN + block]
        field3[block] = got
        return got

    def second(block, out):
        field4[block] = out - coef(0, block) * now[2 * OWN + block]

    received = (Tiles(e_even), Tiles(e_odd), Tiles(s_even), Tiles(s_odd))
    clear(sums_one, sums_two)
    forward_pair(
        par, target, lambda: None, lambda: None, lambda: None, blocks, lambda block: now[block], received, field, middle, first, second
    )
    def start(block):
        value = injected(4, counted, field4[block], spread, block)
        adjoint4[block] = value
        return value

    def add_first(block):
        return injected(3, counted, field3[block], spread, block)

    def add_second(block):
        memory = coef(0, block) * coef(1, block) * adjoint4[block]
        return injected(2, counted, now[block], spread, block) - memory

    adjoint_pair(
        par, target, blocks, start, add_first, add_second, (first_out, second_out, m_even, m_odd), sums_one, sums_two
    )


def clear(*refs):
    for ref in refs:
        zero = jnp.zeros(ref.shape[1:], F32)
        for at in range(ref.shape[0]):
            ref[at] = zero


def adjoint_pair(par, target, blocks, start, add_first, add_second, outs, middle, last):
    first_out, second_out, m_even, m_odd = outs
    low = low_lanes(16)

    def push(sums_ref, item, rows):
        out = lax.dot_general(
            rows, weight_of(blocks, item), (((1,), (0,)), ((), ())), preferred_element_type=F32
        )
        spots = [target(item, k) for k in range(8)]
        sums = []
        for k in range(8):
            part = out[:, (k // 2) * 128 : (k // 2 + 1) * 128]
            part = jnp.where(low, part, 0.0) if k % 2 == 0 else jnp.where(low, 0.0, part)
            sums.append(sums_ref[spots[k]] + part)
        for k in range(8):
            sums_ref[spots[k]] = sums[k]

    def both(sums_ref, at):
        value = sums_ref[at]
        return value + pltpu.roll(value, 64, 1)

    def plain_of(value):
        return jnp.where(low_lanes(8), value[:8], value[8:])

    for block in range(OWN):
        push(middle, block, packed(start(block)).astype(BF16))
    rows_at = sides(par, 0, ROWS, -1)
    for number, (array, index, at) in enumerate(outer_places(par)):
        value = both(middle, at)
        push(last, OWN + number, value[:, :64].astype(BF16))
    for out, row in zip((m_even, m_odd), rows_at):
        for j in range(0, COLS + 2, 2):
            out[j // 2] = paired(plain_of(both(middle, place(row, j + i - 1))) for i in range(2))
    for x in range(ROWS):
        for j in range(COLS + 2):
            value = plain_of(both(middle, place(x, j - 1)))
            if 1 <= j <= COLS:
                block = x * COLS + j - 1
                value = value + add_first(block)
                push(last, block, packed(value).astype(BF16))
            first_out[x * (COLS + 2) + j] = value
    for out, base in zip((m_even, m_odd), sides(par, 0, ROWS, -2)):
        for k in range(2):
            for j in range(0, WIDE, 2):
                at = COLS // 2 + 1 + (k * WIDE + j) // 2
                out[at] = paired(plain_of(both(last, place(base + k, j + i - 2))) for i in range(2))
    for x in range(ROWS):
        for j in range(WIDE):
            value = plain_of(both(last, place(x, j - 2)))
            if 2 <= j < COLS + 2:
                value = value + add_second(x * COLS + j - 2)
            second_out[x * WIDE + j] = value


def paired(blocks):
    return jnp.concatenate(list(blocks), 0).astype(BF16)


def add_pair(target, at, pair):
    both = pair.astype(F32)
    target[at] += both[:8]
    target[at + 1] += both[8:]


def adjoint_py_kernel(flow, first, second, r_even, r_odd, first_own, second_own, n_even, n_odd, one, two):
    par = parity()
    one[...] = first[...]
    two[...] = second[...]
    for msg, row, base in zip((r_even, r_odd), sides(par, 0, 3, 0), sides(par, 0, 2, 0)):
        for j in range(0, COLS + 2, 2):
            add_pair(one, row * (COLS + 2) + j, msg[j // 2])
        for k in range(2):
            for j in range(0, WIDE, 2):
                add_pair(two, (base + k) * WIDE + j, msg[COLS // 2 + 1 + (k * WIDE + j) // 2])
    for out, col, base in zip((n_even, n_odd), sides(par, 1, COLS + 1, 0), sides(par, 1, COLS + 2, 0)):
        for x in range(ROWS):
            out[2 + x] = paired(two[x * WIDE + base + k] for k in range(2))
        for h in range(2):
            out[h] = paired(one[(2 * h + i) * (COLS + 2) + col] for i in range(2))
    for x in range(ROWS):
        for y in range(COLS):
            first_own[x * COLS + y] = one[x * (COLS + 2) + 1 + y]
            second_own[x * COLS + y] = two[x * WIDE + 2 + y]


def settle(par, first_own, second_own, n_even, n_odd, first, second):
    first[...] = first_own[...]
    second[...] = second_own[...]
    for msg, col, base in zip((n_even, n_odd), sides(par, 1, 7, 0), sides(par, 1, 6, 0)):
        for x in range(ROWS):
            add_pair(second, x * COLS + base, msg[2 + x])
        for h in range(2):
            both = msg[h].astype(F32)
            first[2 * h * COLS + col] += both[:8]
            first[(2 * h + 1) * COLS + col] += both[8:]


def injected(moment, counted, field, spread, block):
    return counted[moment - 1, block] * field - spread[moment - 1, block]


def adjoint_two(
    flow, table, own, r_even, r_odd, n_even, n_odd, d_even, d_odd, first_own, second_own, e_even, e_odd, adjoint4, past, coefs,
    spread, counted, later, first_out, second_out, m_even, m_odd, sums_one, sums_two,
):
    par = parity()
    clear(sums_one, sums_two)
    adjoint3, adjoint2 = later.at[pl.ds(0, OWN)], later.at[pl.ds(OWN, OWN)]
    settle(par, first_own, second_own, e_even, e_odd, adjoint3, adjoint2)
    coef = Coefs(coefs)

    def add_first(block):
        memory = coef(2, block) * adjoint4[block] + coef(1, block) * adjoint3[block]
        return injected(1, counted, past[block], spread, block) - coef(0, block) * memory

    def add_second(block):
        memory = coef(3, block) * adjoint4[block] + coef(2, block) * adjoint3[block] + coef(1, block) * adjoint2[block]
        return -coef(0, block) * memory

    adjoint_pair(
        par, targets_of(table, par), (own, r_even, r_odd, n_even, n_odd, d_even, d_odd), lambda block: adjoint2[block], add_first,
        add_second, (first_out, second_out, m_even, m_odd), sums_one, sums_two,
    )


def gradient_kernel(flow, after, adjoint4, later, stored, past, now, out, known):
    flow.fetch(stored.at[pl.ds(0, KNOWN)], known)
    flow.wait(known)
    for block in range(OWN):
        out[block] = (
            adjoint4[block] * now[2 * OWN + block] + later[block] * past[OWN + block]
            + later[OWN + block] * known[SUM1 + block]
        )
        out[OWN + block] = known[SUM0 + block]


def finish_kernel(
    flow, first_own, second_own, n_even, n_odd, before, result, gradient, adjoint1, adjoint0, scratch
):
    par = parity()
    settle(par, first_own, second_own, n_even, n_odd, adjoint1, adjoint0)
    for x in range(ROWS):
        parts = []
        for y in range(COLS):
            block = x * COLS + y
            scratch[pl.ds(x * 64 + y * 8, 8), :] = adjoint0[block]
            value = before[block] + adjoint1[block] * before[OWN + block]
            parts.append(jnp.sum(value, axis=0, keepdims=True))
        rows = jnp.concatenate(parts, 0)
        gradient[x] = -(rows[:, :64] + rows[:, 64:])
        for r in range(8):
            result[x, :, lanes(r)] = scratch[pl.ds(x * 64 + r, 8, stride=8), :]


def split(value):
    high = value.astype(BF16)
    return high, (value - high.astype(F32)).astype(BF16)


def owner_slots(steps, observed, part, node, slots_of):
    owned = observed.shape[0]
    slots = slots_of.shape[0]
    devices = slots // CAP
    row = lax.broadcasted_iota(jnp.int32, (128, 128), 0)
    col = lax.broadcasted_iota(jnp.int32, (128, 128), 1)
    gate = row // 16
    source = row % 16
    step = jnp.zeros((128, 128), jnp.int32)
    for g in range(8):
        step = jnp.where(gate == g, jnp.broadcast_to(steps[0:1, g : g + 1], (128, 128)), step)
    wanted = 2 * (col % 8) + (col // 8) % 2
    chosen = ((step == col // 16 + 1) & (source == wanted) & (col < 64)).astype(F32).astype(BF16)
    high, low = split(observed[...])
    dot = lambda a, b: lax.dot_general(a, b, (((1,), (0,)), ((), ())), preferred_element_type=F32)
    sums = dot(high, chosen) + dot(low, chosen)
    dest = part[...]
    member = (dest == lax.broadcasted_iota(jnp.int32, (devices, owned), 0)).astype(F32)
    earlier = (
        lax.broadcasted_iota(jnp.int32, (owned, owned), 0) < lax.broadcasted_iota(jnp.int32, (owned, owned), 1)
    ).astype(F32).astype(BF16)
    ahead = dot(member.astype(BF16), earlier)
    rank = jnp.sum(ahead * member, axis=0, keepdims=True).astype(jnp.int32)
    position = dest * CAP + rank
    where = (position == lax.broadcasted_iota(jnp.int32, (slots, owned), 0)).astype(F32).astype(BF16)
    line = lax.broadcasted_iota(jnp.int32, (128, owned), 0)
    which = node[...]
    block = lax.shift_right_logical(which, 6)
    inner = which - block * 64
    marks = jnp.where(line == 64, block, jnp.where(line == 65, inner, jnp.where(line == 66, 1, 0)))
    high, low = split(sums)
    turned = lambda a, b: lax.dot_general(a, b, (((1,), (1,)), ((), ())), preferred_element_type=F32)
    slots_of[...] = dot(where, high) + dot(where, low) + turned(where, marks.astype(F32).astype(BF16))


def holder_kernel(flow, steps, slots, after, spread, counted):
    flow.wait(slots)
    tally = []
    for n in range(4):
        total = jnp.zeros((), F32)
        for g in range(8):
            total = total + jnp.where(steps[g] == n + 1, 1.0, 0.0)
        tally.append(total)
    values = slots[...]
    count = values.shape[0]
    lane = lax.broadcasted_iota(jnp.int32, (count, 128), 1)
    pick = lambda at: jnp.sum(jnp.where(lane == at, values, 0.0), axis=1, keepdims=True)
    place_of = jnp.where(pick(66) > 0.5, pick(64) * 64.0 + pick(65), -1.0).astype(jnp.int32)
    high, low = split(values.T)
    both = jnp.concatenate([high, low], 0)
    low8 = low_lanes(8)
    for chunk in range(OWN * 64 // 256):
        spots = lax.broadcasted_iota(jnp.int32, (count, 256), 1) + chunk * 256
        hot = (place_of == spots).astype(F32).astype(BF16)
        out = lax.dot_general(both, hot, (((1,), (0,)), ((), ())), preferred_element_type=F32)
        out = out[:128] + out[128:]
        for j in range(2):
            first = chunk * 4 + 2 * j
            for n in range(4):
                even = out[n * 16 : n * 16 + 8, j * 128 : (j + 1) * 128]
                odd = out[n * 16 + 8 : n * 16 + 16, j * 128 : (j + 1) * 128]
                spread[n, first] = jnp.where(low8, even, pltpu.roll(odd, 64, 1))
                spread[n, first + 1] = jnp.where(low8, pltpu.roll(even, 64, 1), odd)
            many = jnp.broadcast_to(out[66:67, j * 128 : (j + 1) * 128], (8, 128))
            other = pltpu.roll(many, 64, 1)
            for n in range(4):
                counted[n, first] = jnp.where(low8, many, other) * tally[n]
                counted[n, first + 1] = jnp.where(low8, other, many) * tally[n]


def swap_even(axis):
    return [(i, i ^ 1) for i in range(lax.axis_size(axis))]


def swap_odd(axis):
    inner = range(1, lax.axis_size(axis) - 1, 2)
    return [(i, i + 1) for i in inner] + [(i + 1, i) for i in inner]


def exchange(axis, for_even, for_odd):
    return lax.ppermute(for_even, axis, swap_even(axis)), lax.ppermute(for_odd, axis, swap_odd(axis))


def body(
    checkpoint_field,
    checkpoint_memory,
    stiffness,
    block_offsets,
    chargeability,
    relaxation,
    observed,
    receiver_part,
    receiver_node,
    gate_step,
):
    devices = lax.axis_size(("px", "py"))
    slots = devices * CAP
    turn = pltpu.VMEM((256, 128), F32)
    lookup = pltpu.SMEM((16, 128), jnp.int32)
    places = pltpu.VMEM((PLACES, 16, 128), BF16)
    sums = pltpu.VMEM((PLACES, 16, 128), F32)
    blocks = pltpu.VMEM((OWN, 8, 128), F32)
    px_first = ((PX_BASE + 80, WIDTH), BF16, "v")
    py_first = ((PY_BASE + 64, WIDTH), BF16, "v")
    px_shape = ((16, 16, 128), BF16, "v")
    py_shape = ((14, 16, 128), BF16, "v")
    down = ((ROWS, NODE, WIDTH), BF16, "v")
    two = (2,) + py_first[0]
    m_even, m_odd, both, d_even, d_odd, lines, sent = call(
        start_kernel,
        [
            px_first[:2] + ("h",), px_first[:2] + ("h",), ((PAGES,) + py_first[0], BF16, "h"), down[:2] + ("h",), down[:2] + ("h",),
            ((8, 128), F32, "v"), ((slots, 128), F32, "h"),
        ],
        [
            (gate_step.reshape(1, -1), "h"), (observed, "h"), (receiver_part.reshape(1, -1), "h"),
            (receiver_node.reshape(1, -1), "h"), (block_offsets, "h"), (checkpoint_field, "h"),
            (checkpoint_memory, "h"), (chargeability, "h"), (stiffness, "b"),
        ],
        [blocks, blocks, turn, pltpu.VMEM((slots, 128), F32)]
        + [pltpu.VMEM(shape, BF16) for shape in (px_first[0], px_first[0], two, down[0], down[0])],
        copies=2 * COLS + 2 * ROWS + 8, vmem=65 * 1000 * 1000,
    )
    r_even, r_odd = exchange("px", m_even, m_odd)
    d_even, d_odd = exchange("py", d_even, d_odd)
    sent, r_even = lax.optimization_barrier((sent, r_even))
    held = lax.all_to_all(
        sent.reshape(devices, CAP, 128), ("px", "py"), split_axis=0, concat_axis=0, tiled=True
    ).reshape(slots, 128)
    n_even, n_odd = call(
        first_py_kernel, [py_first, py_first],
        [(r_even, "v"), (r_odd, "v"), (both, "b")],
        copies=2, vmem=50 * 1000 * 1000,
    )
    (known,) = call(
        decay_kernel, [((ROOM, 8, 128), F32, "h")],
        [(n_even, "v"), (checkpoint_field, "h"), (checkpoint_memory, "h"), (chargeability, "h"), (relaxation, "h")],
        [pltpu.VMEM((KNOWN, 8, 128), F32), turn], copies=1, vmem=VMEM_MOST,
    )
    n_even, n_odd = exchange("py", n_even, n_odd)
    held, n_even = lax.optimization_barrier((held, n_even))
    weights = [(a, "v") for a in (stiffness, r_even, r_odd, n_even, n_odd, d_even, d_odd)]
    past, now, m_even, m_odd, p_even, p_odd, table, coefs, *late = call(
        forward_one,
        [
            ((2 * OWN, 8, 128), F32, "v"), ((3 * OWN, 8, 128), F32, "v"), px_shape, px_shape, py_shape, py_shape,
            ((16, 128), jnp.int32, "v"), ((4 * ROWS, 8, 128), F32, "v"), py_first, down, down,
        ],
        [(lines, "v")] + weights[:4] + [(a, "h") for a, _ in weights[4:]] + [(known, "b")],
        [places, places, lookup, pltpu.VMEM((KNOWN, 8, 128), F32)], copies=3,
    )
    weights = weights[:4] + [(a, "v") for a in late]
    r_even, r_odd = exchange("px", m_even, m_odd)
    n_even, n_odd = call(
        second_py_kernel, [py_shape, py_shape],
        [(r_even, "v"), (r_odd, "v"), (p_even, "v"), (p_odd, "v")],
    )
    n_even, n_odd = exchange("py", n_even, n_odd)
    spread, counted = call(
        holder_kernel, [((4, OWN, 8, 128), F32, "v"), ((4, OWN, 8, 128), F32, "v")],
        [(gate_step, "s"), (held, "h"), (m_even, "v")],
    )
    rim = ((COLS // 2 + 1 + WIDE, 16, 128), BF16, "v")
    rim_py = ((6, 16, 128), BF16, "v")
    pair_out = [
        ((ROWS * (COLS + 2), 8, 128), F32, "v"), ((ROWS * WIDE, 8, 128), F32, "v"),
        rim, rim,
    ]
    adjoint4, *rest = call(
        turn_kernel, [PLAIN] + pair_out,
        [(table, "s")] + weights
        + [(r_even, "v"), (r_odd, "v"), (n_even, "v"), (n_odd, "v"), (now, "v"), (coefs, "v"), (spread, "v"), (counted, "v")],
        [places, places, sums, sums, blocks, blocks],
    )

    def gathered(first, second, m_even, m_odd):
        r_even, r_odd = exchange("px", m_even, m_odd)
        own_first, own_second, n_even, n_odd = call(
            adjoint_py_kernel, [PLAIN, PLAIN, rim_py, rim_py],
            [(first, "v"), (second, "v"), (r_even, "v"), (r_odd, "v")],
            [pltpu.VMEM(first.shape, F32), pltpu.VMEM(second.shape, F32)],
        )
        n_even, n_odd = exchange("py", n_even, n_odd)
        return [(a, "v") for a in (own_first, own_second, n_even, n_odd)]

    later, *rest = call(
        adjoint_two, [((2 * OWN, 8, 128), F32, "v")] + pair_out,
        [(table, "s")] + weights + gathered(*rest)
        + [(adjoint4, "v"), (past, "v"), (coefs, "v"), (spread, "v"), (counted, "v")],
        [sums, sums],
    )
    (before,) = call(
        gradient_kernel, [((2 * OWN, 8, 128), F32, "v")],
        [(a, "b" if a is known else "v") for a in (rest[2], adjoint4, later, known, past, now)],
        [pltpu.VMEM((KNOWN, 8, 128), F32)], copies=1,
    )
    field_out, gradient = call(
        finish_kernel, [(checkpoint_field.shape, F32, "v"), (chargeability.shape, F32, "v")],
        [] + gathered(*rest) + [(before, "v")], [blocks, blocks, turn],
    )
    return field_out, gradient


def solution(mesh):
    in_specs = (
        P("px", "py", None),
        P(None, "px", "py", None),
        P("px", "py", None, None),
        P("px", "py", None),
        P("px", "py", None),
        P(None, "px", "py", None),
        P(("px", "py"), None),
        P(("px", "py"), None),
        P(("px", "py")),
        P(),
    )
    out_specs = (P("px", "py", None), P("px", "py", None))
    return jax.shard_map(body, mesh=mesh, in_specs=in_specs, out_specs=out_specs, check_vma=False)
```

```python
import jax
import jax.numpy as jnp
from jax import lax
from jax.experimental import pallas as pl
from jax.experimental.pallas import tpu as pltpu
from jax.sharding import PartitionSpec as P

ROWS, COLS = 4, 8
OWN = ROWS * COLS
CAP = 8
WIDE = COLS + 4
PLACES = (ROWS + 4) * WIDE
F32, BF16 = jnp.float32, jnp.bfloat16
VMEM_BYTES, VMEM_MOST = 16 * 1024 * 1024, 63 * 1000 * 1000
NODE, WIDTH = 64, 512
FIELD, ADDEND, SUM0, SUM1, SUM2, SUM3, COEF = (i * OWN for i in range(7))
PX_BASE, PY_BASE = COLS * NODE, 2 * NODE
KNOWN, ROOM, PAGES = COEF + 4 * ROWS, 12288, 96


def place(row, col):
    return (row + 2) * WIDE + col + 2


def low_lanes(rows):
    return lax.broadcasted_iota(jnp.int32, (rows, 128), 1) < 64


def doubled(plain):
    turned = pltpu.roll(plain, 64, 1)
    low = low_lanes(8)
    return jnp.concatenate([jnp.where(low, plain, turned), jnp.where(low, turned, plain)], 0)


def packed(plain):
    return jnp.concatenate([plain[:, :64], plain[:, 64:]], 0)


def unpacked(rows):
    return jnp.concatenate([rows[:8], rows[8:]], 1)


def halves(plain):
    high = plain.astype(BF16).astype(F32)
    return jnp.concatenate([high, plain - high], 0).astype(BF16)


def joined(pair):
    pair = pair.astype(F32)
    return pair[:8] + pair[8:]


def parity():
    return lax.axis_index("px") % 2, lax.axis_index("py") % 2


def sides(par_ref, axis, near, far):
    even = par_ref[axis] == 0
    return jnp.where(even, near, far), jnp.where(even, far, near)


class Flow:
    def __init__(self, sems):
        self.sems, self.used, self.coming, self.going = sems, 0, {}, []

    def copy(self, source, target):
        made = pltpu.make_async_copy(source, target, self.sems.at[self.used])
        self.used += 1
        made.start()
        return made

    def wait(self, *refs):
        for ref in refs:
            for made in self.coming.pop(id(ref), ()):
                made.wait()

    def fetch(self, source, target):
        self.coming[id(target)] = [self.copy(source, target)]

    def send(self, source, target):
        self.going.append(self.copy(source, target))

    def finish(self):
        for key in list(self.coming):
            for made in self.coming.pop(key):
                made.wait()
        for made in self.going:
            made.wait()


def call(kernel, outs, inputs, scratch=(), copies=0, vmem=VMEM_BYTES):
    spaces = {"s": pltpu.SMEM, "v": pltpu.VMEM, "h": pltpu.HBM, "b": pltpu.HBM}
    arrays = [array for array, _ in inputs]
    fetched = [i for i, (_, kind) in enumerate(inputs) if kind == "h"]
    total = len(fetched) + copies

    def wrapped(*refs):
        refs = list(refs)
        buffers = refs[len(inputs) + len(outs) + len(scratch) :]
        flow = Flow(buffers[-1])
        for buffer, i in zip(buffers, fetched):
            flow.coming[id(buffer)] = [flow.copy(refs[i], buffer)]
            refs[i] = buffer
        kernel(flow, *refs[: len(inputs) + len(outs) + len(scratch)])
        flow.finish()

    buffers = [pltpu.VMEM(arrays[i].shape, arrays[i].dtype) for i in fetched]
    return pl.pallas_call(
        wrapped,
        out_shape=[jax.ShapeDtypeStruct(shape, dtype) for shape, dtype, _ in outs],
        in_specs=[pl.BlockSpec(memory_space=spaces[kind]) for _, kind in inputs],
        out_specs=[pl.BlockSpec(memory_space=spaces[kind]) for _, _, kind in outs],
        scratch_shapes=list(scratch) + buffers + [pltpu.SemaphoreType.DMA((max(total, 1),))],
        compiler_params=pltpu.CompilerParams(vmem_limit_bytes=vmem),
    )(*arrays)


PLAIN = ((OWN, 8, 128), F32, "v")


class Tiles:
    def __init__(self, ref, base=None):
        self.ref, self.base = ref, base

    def at(self, t):
        if self.base is None:
            return (t,)
        return pl.ds(self.base + 16 * (t // 4), 16), pl.ds(128 * (t % 4), 128)

    def __getitem__(self, t):
        return self.ref[self.at(t)]

    def __setitem__(self, t, value):
        self.ref[self.at(t)] = value


def to_plain(native, scratch, out):
    for x in range(ROWS):
        for r in range(8):
            scratch[pl.ds(x * 64 + r * 8, 8), :] = native(x, r)
    for x in range(ROWS):
        for y in range(COLS):
            out[x * COLS + y] = scratch[pl.ds(x * 64 + y, 8, stride=8), :]


def lanes(r):
    return pl.ds(r * 128, 128)


def twice(rows):
    return jnp.concatenate([rows, rows], 1)


def px_message(par, plain, addend, outs):
    bases = sides(par, 0, 2, 0)
    edges = sides(par, 0, 3, 0)
    for out, base, edge in zip(outs, bases, edges):
        for k in range(2):
            for p in range(4):
                at = (base + k) * COLS + 2 * p
                out[k * 4 + p] = jnp.concatenate([plain(at), plain(at + 1)], 0).astype(BF16)
        for y in range(COLS):
            out[8 + y] = halves(addend(edge * COLS + y))


def py_message(par, plain, addend, outs):
    pairs = sides(par, 1, 3, 0)
    edges = sides(par, 1, 7, 0)
    for out, pair, edge in zip(outs, pairs, edges):
        for x in range(ROWS):
            at = x * COLS + 2 * pair
            out[x] = jnp.concatenate([plain(at), plain(at + 1)], 0).astype(BF16)
            out[8 + x] = halves(addend(x * COLS + edge))


def picked_tile(tiles, choice, low, high):
    return jnp.where(choice == 0, tiles[low].astype(F32), tiles[high].astype(F32)).astype(BF16)


def py_fill(par, r_even, r_odd, outs):
    edges = sides(par, 1, 7, 0)
    for out, edge in zip(outs, edges):
        for k in range(2):
            out[4 + k] = picked_tile(r_even, edge, k * 4, k * 4 + 3)
            out[6 + k] = picked_tile(r_odd, edge, k * 4, k * 4 + 3)
        out[12] = picked_tile(r_even, edge, 8, 15)
        out[13] = picked_tile(r_odd, edge, 8, 15)


def shift_lines(offsets):
    row = lax.broadcasted_iota(jnp.int32, (8, 128), 0)
    lane = lax.broadcasted_iota(jnp.int32, (8, 128), 1)
    repeat = ((lane % 8 == row) & (lane < 64)).astype(F32).astype(BF16)
    lines = jnp.zeros((8, 128), F32)
    for x in range(ROWS):
        codes = offsets[x].astype(F32).astype(BF16)
        wide = lax.dot_general(codes, repeat, (((1,), (0,)), ((), ())), preferred_element_type=F32)
        line = jnp.sum(jnp.where(lane // 8 == row, wide, 0.0), axis=0, keepdims=True)
        lines = jnp.where(row == x, line, lines)
    above = (lines > 2.5).astype(F32) + (lines > 5.5).astype(F32)
    return 9.0 * above + lines - 13.0


def start_kernel(
    flow, steps, observed, part, node, offsets, field, memory, charge, stiffness,
    m_even_out, m_odd_out, both_out, d_even_out, d_odd_out, lines, sent,
    plain, addend, scratch, slots_of, m_even, m_odd, both, d_even, d_odd,
):
    par = parity()
    for out, edge in zip((m_even, m_odd), sides(par, 0, ROWS - 1, 0)):
        flow.coming[id(out)] = [
            flow.copy(stiffness.at[edge, y], out.at[pl.ds(y * NODE, NODE), :]) for y in range(COLS)
        ]
    for out, edge in zip((d_even, d_odd), sides(par, 1, COLS - 1, 0)):
        flow.coming[id(out)] = [flow.copy(stiffness.at[x, edge], out.at[x]) for x in range(ROWS)]
    flow.wait(steps, observed, part, node)
    owner_slots(steps, observed, part, node, slots_of)
    flow.send(slots_of, sent)
    flow.wait(offsets)
    found = shift_lines(offsets)
    lines[...] = found
    px_tiles = [Tiles(m_even, PX_BASE), Tiles(m_odd, PX_BASE)]
    py_tiles = [Tiles(both.at[0], PY_BASE), Tiles(both.at[1], PY_BASE)]
    flow.wait(m_even, m_odd, d_even, d_odd)
    for source, out in ((m_even, m_even_out), (m_odd, m_odd_out)):
        flow.send(source.at[pl.ds(0, PX_BASE), :], out.at[pl.ds(0, PX_BASE), :])
    flow.send(d_even, d_even_out)
    flow.send(d_odd, d_odd_out)
    for out, edge in zip(px_tiles, sides(par, 0, ROWS - 1, 0)):
        line = jnp.where(edge == 0, found[0:1], found[ROWS - 1 : ROWS])
        out[16] = jnp.broadcast_to(line, (16, 128)).astype(BF16)
    for out in py_tiles:
        out[14] = jnp.concatenate([found, jnp.zeros((8, 128), F32)], 0).astype(BF16)
    flow.wait(field, memory, charge)
    terms = memory.shape[0]
    to_plain(lambda x, r: field[x, :, lanes(r)], scratch, plain)

    def total(x, r):
        acc = memory[0, x, :, lanes(r)]
        for q in range(1, terms):
            acc = acc + memory[q, x, :, lanes(r)]
        return acc * -twice(charge[x])

    to_plain(total, scratch, addend)
    get, add = (lambda at: plain[at]), (lambda at: addend[at])
    px_message(par, get, add, px_tiles)
    for source, out in ((m_even, m_even_out), (m_odd, m_odd_out)):
        flow.send(source.at[pl.ds(PX_BASE, 80), :], out.at[pl.ds(PX_BASE, 80), :])
    py_message(par, get, add, py_tiles)
    flow.send(both.at[:, pl.ds(PY_BASE, 64), :], both_out.at[pl.ds(0, 2), pl.ds(PY_BASE, 64), :])


def first_py_kernel(flow, r_even, r_odd, given, n_even, n_odd):
    par = parity()
    part = pl.ds(PY_BASE, 64)
    own = [flow.copy(given.at[i, part, :], out.at[part, :]) for i, out in enumerate((n_even, n_odd))]
    tiles = [Tiles(r_even, PX_BASE), Tiles(r_odd, PX_BASE)]
    outs = [Tiles(n_even, PY_BASE), Tiles(n_odd, PY_BASE)]
    row = lax.broadcasted_iota(jnp.int32, (16, 128), 0)
    for out, edge in zip((n_even, n_odd), sides(par, 1, COLS - 1, 0)):
        for k, got in enumerate((r_even, r_odd)):
            out[pl.ds(k * NODE, NODE), :] = got[pl.ds(edge * NODE, NODE), :]
    for copied in own:
        copied.wait()
    py_fill(par, tiles[0], tiles[1], outs)
    for out in outs:
        even, odd = tiles[0][16].astype(F32), tiles[1][16].astype(F32)
        own = out[14].astype(F32)
        out[14] = jnp.where(row == ROWS, even, jnp.where(row == ROWS + 1, odd, own)).astype(BF16)


def second_py_kernel(flow, r_even, r_odd, in_even, in_odd, n_even, n_odd):
    par = parity()
    n_even[...] = in_even[...]
    n_odd[...] = in_odd[...]
    py_fill(par, Tiles(r_even), Tiles(r_odd), (Tiles(n_even), Tiles(n_odd)))


def decay_kernel(flow, after, field, memory, charge, relaxation, out, full, scratch):
    terms = memory.shape[0]
    flow.wait(field, memory, charge, relaxation)
    wide = [twice(charge[x]) for x in range(ROWS)]
    rates = [[twice(relaxation[q, x]) for q in range(terms)] for x in range(ROWS)]
    coefs = []
    for x in range(ROWS):
        w0 = w1 = w2 = 0.0
        for rate in rates[x]:
            w0 = w0 + (1.0 - rate)
            w1 = w1 + rate * (1.0 - rate)
            w2 = w2 + rate * rate * (1.0 - rate)
        coefs.append((wide[x], w0, w1, w2))
        for j in range(4):
            full[COEF + j * ROWS + x] = coefs[x][j]

    def region(base):
        return full.at[pl.ds(base, OWN)]

    def total(x, r):
        acc = memory[0, x, :, lanes(r)]
        for q in range(1, terms):
            acc = acc + memory[q, x, :, lanes(r)]
        return acc

    to_plain(lambda x, r: field[x, :, lanes(r)], scratch, region(FIELD))
    to_plain(total, scratch, region(SUM0))
    to_plain(lambda x, r: total(x, r) * -wide[x], scratch, region(ADDEND))
    for power, base in ((1, SUM1), (2, SUM2), (3, SUM3)):
        scale = [[rate if power == 1 else rate * rate if power == 2 else rate * rate * rate for rate in row] for row in rates]

        def part(x, r):
            acc = coefs[x][power] * field[x, :, lanes(r)]
            for q in range(terms):
                acc = acc + scale[x][q] * memory[q, x, :, lanes(r)]
            return acc

        to_plain(part, scratch, region(base))
    flow.send(full, out.at[pl.ds(0, KNOWN)])


def load_kernel(flow, after, stored, out):
    flow.send(stored.at[pl.ds(0, KNOWN)], out)


class Coefs:
    def __init__(self, ref):
        self.ref = ref

    def __call__(self, j, block):
        return self.ref[j * ROWS + block // COLS, pl.ds(block % COLS, 1), :]


def outer_places(par):
    row_even, row_odd = sides(par, 0, ROWS, -1)
    col_even, col_odd = sides(par, 1, COLS, -1)
    listed = []
    for array, row in ((0, row_even), (1, row_odd)):
        listed += [(array, y, place(row, y)) for y in range(COLS)]
    rows = [0, 1, 2, 3, row_even, row_odd]
    for array, col in ((2, col_even), (3, col_odd)):
        listed += [(array, j, place(row, col)) for j, row in enumerate(rows)]
    return listed


def weight_of(blocks, item):
    own, r_even, r_odd, n_even, n_odd, d_even, d_odd = blocks
    if item < OWN:
        return own[item // COLS, item % COLS]
    item -= OWN
    if item < 2 * COLS:
        return (r_even, r_odd)[item // COLS][pl.ds(item % COLS * NODE, NODE), :]
    side, j = (item - 2 * COLS) // (ROWS + 2), (item - 2 * COLS) % (ROWS + 2)
    if j < ROWS:
        return (d_even, d_odd)[side][j]
    return (n_even, n_odd)[side][pl.ds((j - ROWS) * NODE, NODE), :]


def targets_of(table, par):
    columns = sides(par, 1, 0, COLS - 1)

    def target(item, k):
        if item < OWN + 2 * COLS:
            return table[item // COLS, (item % COLS) * 8 + k]
        item -= OWN + 2 * COLS
        side, j = item // (ROWS + 2), item % (ROWS + 2)
        return table[8 + j, columns[side] * 8 + k + 64 * side]

    return target


def first_lines(par, lines, r_even, r_odd):
    row = lax.broadcasted_iota(jnp.int32, (8, 128), 0)
    lane = lax.broadcasted_iota(jnp.int32, (8, 128), 1)
    row_even, row_odd = sides(par, 0, ROWS, -1)
    line = jnp.where(row == ROWS, row_even, jnp.where(row == ROWS + 1, row_odd, row))
    even = Tiles(r_even, PX_BASE)[16].astype(F32)[:8]
    odd = Tiles(r_odd, PX_BASE)[16].astype(F32)[:8]
    first = jnp.where(row == ROWS, even, jnp.where(row == ROWS + 1, odd, lines))
    return first.astype(jnp.int32) + place(line, lane // 8)


def last_lines(par, n_even, n_odd):
    row = lax.broadcasted_iota(jnp.int32, (8, 128), 0)
    lane = lax.broadcasted_iota(jnp.int32, (8, 128), 1)
    row_even, row_odd = sides(par, 0, ROWS, -1)
    line = jnp.where(row == ROWS, row_even, jnp.where(row == ROWS + 1, row_odd, row))
    ends = []
    for msg, col in zip((n_even, n_odd), sides(par, 1, COLS, -1)):
        ends.append(Tiles(msg, PY_BASE)[14].astype(F32)[:8].astype(jnp.int32) + place(line, col))
    return jnp.where(lane < 64, ends[0], pltpu.roll(ends[1], 64, 1))


def forward_pair(par, target, arrive, ready, arrived, blocks, plain, received, field, middle, store_first, store_second):
    low = low_lanes(16)
    r_even, r_odd, n_even, n_odd = received

    def spread(pair, first, second):
        both = pair.astype(F32)
        field[first] = doubled(both[:8]).astype(BF16)
        field[second] = doubled(both[8:]).astype(BF16)

    row_bases = sides(par, 0, ROWS, -2)
    col_bases = sides(par, 1, COLS, -2)
    for msg, base in zip((r_even, r_odd), row_bases):
        for k in range(2):
            for p in range(4):
                at = place(base + k, 2 * p)
                spread(msg[k * 4 + p], at, at + 1)
    arrive()
    rows = [0, 1, 2, 3, row_bases[0], row_bases[0] + 1, row_bases[1], row_bases[1] + 1]
    for msg, base in zip((n_even, n_odd), col_bases):
        for j, row in enumerate(rows):
            at = place(row, base)
            spread(msg[j], at, at + 1)
    ready()
    for block in range(OWN):
        field[place(block // COLS, block % COLS)] = doubled(plain(block)).astype(BF16)

    def product(source, item):
        parts = []
        for m in range(4):
            one = source[target(item, 2 * m)]
            two = source[target(item, 2 * m + 1)]
            parts.append(jnp.where(low, one, two))
        picked = jnp.concatenate(parts, 1)
        out = lax.dot_general(
            picked, weight_of(blocks, item), (((1,), (1,)), ((), ())), preferred_element_type=F32
        )
        return unpacked(out)

    outer = list(enumerate(outer_places(par)))

    def rim(listed):
        for number, (array, index, at) in listed:
            got = product(field, OWN + number) + joined(received[array][8 + index])
            middle[at] = doubled(got).astype(BF16)

    rim(outer[: 2 * COLS])
    for block in range(OWN):
        got = store_first(block, product(field, block))
        middle[place(block // COLS, block % COLS)] = doubled(got).astype(BF16)
    arrived()
    rim(outer[2 * COLS :])
    for block in range(OWN):
        store_second(block, product(middle, block))


def forward_one(
    flow, lines, own, r_even, r_odd, n_even, n_odd, d_even, d_odd, known, past, now, m_even, m_odd, p_even, p_odd, table_out,
    coefs_out, n_odd_out, d_even_out, d_odd_out,
    field, middle, table,
):
    par = parity()
    halves_of = [pl.ds(0, 8), pl.ds(8, 8)]
    table_out[halves_of[0], :] = first_lines(par, lines[...], r_even, r_odd)
    looked = [flow.copy(table_out.at[halves_of[0], :], table.at[halves_of[0], :])]

    def arrive():
        flow.wait(n_odd)
        table_out[halves_of[1], :] = last_lines(par, n_even, n_odd)
        looked.append(flow.copy(table_out.at[halves_of[1], :], table.at[halves_of[1], :]))

    def arrived():
        looked[1].wait()
        flow.wait(d_even, d_odd)

    coef = Coefs(known.at[pl.ds(COEF, 4 * ROWS)])

    def ready():
        looked[0].wait()

    def first(block, out):
        got = out + known[ADDEND + block]
        past[block] = got
        full = known[SUM2 + block] + coef(1, block) * got
        past[OWN + block] = full
        now[OWN + block] = -coef(0, block) * full
        return got

    def second(block, out):
        now[block] = out - coef(0, block) * known[SUM1 + block]

    received = (Tiles(r_even, PX_BASE), Tiles(r_odd, PX_BASE), Tiles(n_even, PY_BASE), Tiles(n_odd, PY_BASE))
    forward_pair(
        par, targets_of(table, par), arrive, ready, arrived, (own, r_even, r_odd, n_even, n_odd, d_even, d_odd), lambda block: known[FIELD + block],
        received, field, middle, first, second,
    )
    get, add = (lambda at: now[at]), (lambda at: now[OWN + at])
    px_message(par, get, add, (Tiles(m_even), Tiles(m_odd)))
    coefs_out[...] = known[COEF:KNOWN]
    n_odd_out[...] = n_odd[...]
    d_even_out[...] = d_even[...]
    d_odd_out[...] = d_odd[...]
    py_message(par, get, add, (Tiles(p_even), Tiles(p_odd)))
    for block in range(OWN):
        now[2 * OWN + block] = known[SUM3 + block] + coef(2, block) * past[block] + coef(1, block) * now[block]


def turn_kernel(
    flow, table, own, r_even, r_odd, n_even, n_odd, d_even, d_odd, e_even, e_odd, s_even, s_odd, now, coefs, spread, counted,
    adjoint4, first_out, second_out, m_even, m_odd, field, middle, sums_one, sums_two, field3, field4,
):
    par = parity()
    blocks = (own, r_even, r_odd, n_even, n_odd, d_even, d_odd)
    target = targets_of(table, par)
    coef = Coefs(coefs)

    def first(block, out):
        got = out + now[OWN + block]
        field3[block] = got
        return got

    def second(block, out):
        field4[block] = out - coef(0, block) * now[2 * OWN + block]

    received = (Tiles(e_even), Tiles(e_odd), Tiles(s_even), Tiles(s_odd))
    clear(sums_one, sums_two)
    forward_pair(
        par, target, lambda: None, lambda: None, lambda: None, blocks, lambda block: now[block], received, field, middle, first, second
    )
    def start(block):
        value = injected(4, counted, field4[block], spread, block)
        adjoint4[block] = value
        return value

    def add_first(block):
        return injected(3, counted, field3[block], spread, block)

    def add_second(block):
        memory = coef(0, block) * coef(1, block) * adjoint4[block]
        return injected(2, counted, now[block], spread, block) - memory

    adjoint_pair(
        par, target, blocks, start, add_first, add_second, (first_out, second_out, m_even, m_odd), sums_one, sums_two
    )


def clear(*refs):
    for ref in refs:
        zero = jnp.zeros(ref.shape[1:], F32)
        for at in range(ref.shape[0]):
            ref[at] = zero


def adjoint_pair(par, target, blocks, start, add_first, add_second, outs, middle, last):
    first_out, second_out, m_even, m_odd = outs
    low = low_lanes(16)

    def push(sums_ref, item, rows):
        out = lax.dot_general(
            rows, weight_of(blocks, item), (((1,), (0,)), ((), ())), preferred_element_type=F32
        )
        spots = [target(item, k) for k in range(8)]
        sums = []
        for k in range(8):
            part = out[:, (k // 2) * 128 : (k // 2 + 1) * 128]
            part = jnp.where(low, part, 0.0) if k % 2 == 0 else jnp.where(low, 0.0, part)
            sums.append(sums_ref[spots[k]] + part)
        for k in range(8):
            sums_ref[spots[k]] = sums[k]

    def both(sums_ref, at):
        value = sums_ref[at]
        return value + pltpu.roll(value, 64, 1)

    def plain_of(value):
        return jnp.where(low_lanes(8), value[:8], value[8:])

    for block in range(OWN):
        push(middle, block, packed(start(block)).astype(BF16))
    rows_at = sides(par, 0, ROWS, -1)
    for number, (array, index, at) in enumerate(outer_places(par)):
        value = both(middle, at)
        push(last, OWN + number, value[:, :64].astype(BF16))
    for out, row in zip((m_even, m_odd), rows_at):
        for j in range(0, COLS + 2, 2):
            out[j // 2] = paired(plain_of(both(middle, place(row, j + i - 1))) for i in range(2))
    for x in range(ROWS):
        for j in range(COLS + 2):
            value = plain_of(both(middle, place(x, j - 1)))
            if 1 <= j <= COLS:
                block = x * COLS + j - 1
                value = value + add_first(block)
                push(last, block, packed(value).astype(BF16))
            first_out[x * (COLS + 2) + j] = value
    for out, base in zip((m_even, m_odd), sides(par, 0, ROWS, -2)):
        for k in range(2):
            for j in range(0, WIDE, 2):
                at = COLS // 2 + 1 + (k * WIDE + j) // 2
                out[at] = paired(plain_of(both(last, place(base + k, j + i - 2))) for i in range(2))
    for x in range(ROWS):
        for j in range(WIDE):
            value = plain_of(both(last, place(x, j - 2)))
            if 2 <= j < COLS + 2:
                value = value + add_second(x * COLS + j - 2)
            second_out[x * WIDE + j] = value


def paired(blocks):
    return jnp.concatenate(list(blocks), 0).astype(BF16)


def add_pair(target, at, pair):
    both = pair.astype(F32)
    target[at] += both[:8]
    target[at + 1] += both[8:]


def adjoint_py_kernel(flow, first, second, r_even, r_odd, first_own, second_own, n_even, n_odd, one, two):
    par = parity()
    one[...] = first[...]
    two[...] = second[...]
    for msg, row, base in zip((r_even, r_odd), sides(par, 0, 3, 0), sides(par, 0, 2, 0)):
        for j in range(0, COLS + 2, 2):
            add_pair(one, row * (COLS + 2) + j, msg[j // 2])
        for k in range(2):
            for j in range(0, WIDE, 2):
                add_pair(two, (base + k) * WIDE + j, msg[COLS // 2 + 1 + (k * WIDE + j) // 2])
    for out, col, base in zip((n_even, n_odd), sides(par, 1, COLS + 1, 0), sides(par, 1, COLS + 2, 0)):
        for x in range(ROWS):
            out[2 + x] = paired(two[x * WIDE + base + k] for k in range(2))
        for h in range(2):
            out[h] = paired(one[(2 * h + i) * (COLS + 2) + col] for i in range(2))
    for x in range(ROWS):
        for y in range(COLS):
            first_own[x * COLS + y] = one[x * (COLS + 2) + 1 + y]
            second_own[x * COLS + y] = two[x * WIDE + 2 + y]


def settle(par, first_own, second_own, n_even, n_odd, first, second):
    first[...] = first_own[...]
    second[...] = second_own[...]
    for msg, col, base in zip((n_even, n_odd), sides(par, 1, 7, 0), sides(par, 1, 6, 0)):
        for x in range(ROWS):
            add_pair(second, x * COLS + base, msg[2 + x])
        for h in range(2):
            both = msg[h].astype(F32)
            first[2 * h * COLS + col] += both[:8]
            first[(2 * h + 1) * COLS + col] += both[8:]


def injected(moment, counted, field, spread, block):
    return counted[moment - 1, block] * field - spread[moment - 1, block]


def adjoint_two(
    flow, table, own, r_even, r_odd, n_even, n_odd, d_even, d_odd, first_own, second_own, e_even, e_odd, adjoint4, past, coefs,
    spread, counted, later, first_out, second_out, m_even, m_odd, sums_one, sums_two,
):
    par = parity()
    clear(sums_one, sums_two)
    adjoint3, adjoint2 = later.at[pl.ds(0, OWN)], later.at[pl.ds(OWN, OWN)]
    settle(par, first_own, second_own, e_even, e_odd, adjoint3, adjoint2)
    coef = Coefs(coefs)

    def add_first(block):
        memory = coef(2, block) * adjoint4[block] + coef(1, block) * adjoint3[block]
        return injected(1, counted, past[block], spread, block) - coef(0, block) * memory

    def add_second(block):
        memory = coef(3, block) * adjoint4[block] + coef(2, block) * adjoint3[block] + coef(1, block) * adjoint2[block]
        return -coef(0, block) * memory

    adjoint_pair(
        par, targets_of(table, par), (own, r_even, r_odd, n_even, n_odd, d_even, d_odd), lambda block: adjoint2[block], add_first,
        add_second, (first_out, second_out, m_even, m_odd), sums_one, sums_two,
    )


def gradient_kernel(flow, after, adjoint4, later, stored, past, now, out, known):
    flow.fetch(stored.at[pl.ds(0, KNOWN)], known)
    flow.wait(known)
    for block in range(OWN):
        out[block] = (
            adjoint4[block] * now[2 * OWN + block] + later[block] * past[OWN + block]
            + later[OWN + block] * known[SUM1 + block]
        )
        out[OWN + block] = known[SUM0 + block]


def finish_kernel(
    flow, first_own, second_own, n_even, n_odd, before, result, gradient, adjoint1, adjoint0, scratch
):
    par = parity()
    settle(par, first_own, second_own, n_even, n_odd, adjoint1, adjoint0)
    for x in range(ROWS):
        parts = []
        for y in range(COLS):
            block = x * COLS + y
            scratch[pl.ds(x * 64 + y * 8, 8), :] = adjoint0[block]
            value = before[block] + adjoint1[block] * before[OWN + block]
            parts.append(jnp.sum(value, axis=0, keepdims=True))
        rows = jnp.concatenate(parts, 0)
        gradient[x] = -(rows[:, :64] + rows[:, 64:])
        for r in range(8):
            result[x, :, lanes(r)] = scratch[pl.ds(x * 64 + r, 8, stride=8), :]


def split(value):
    high = value.astype(BF16)
    return high, (value - high.astype(F32)).astype(BF16)


def owner_slots(steps, observed, part, node, slots_of):
    owned = observed.shape[0]
    slots = slots_of.shape[0]
    devices = slots // CAP
    row = lax.broadcasted_iota(jnp.int32, (128, 128), 0)
    col = lax.broadcasted_iota(jnp.int32, (128, 128), 1)
    gate = row // 16
    source = row % 16
    step = jnp.zeros((128, 128), jnp.int32)
    for g in range(8):
        step = jnp.where(gate == g, jnp.broadcast_to(steps[0:1, g : g + 1], (128, 128)), step)
    wanted = 2 * (col % 8) + (col // 8) % 2
    chosen = ((step == col // 16 + 1) & (source == wanted) & (col < 64)).astype(F32).astype(BF16)
    high, low = split(observed[...])
    dot = lambda a, b: lax.dot_general(a, b, (((1,), (0,)), ((), ())), preferred_element_type=F32)
    sums = dot(high, chosen) + dot(low, chosen)
    dest = part[...]
    member = (dest == lax.broadcasted_iota(jnp.int32, (devices, owned), 0)).astype(F32)
    earlier = (
        lax.broadcasted_iota(jnp.int32, (owned, owned), 0) < lax.broadcasted_iota(jnp.int32, (owned, owned), 1)
    ).astype(F32).astype(BF16)
    ahead = dot(member.astype(BF16), earlier)
    rank = jnp.sum(ahead * member, axis=0, keepdims=True).astype(jnp.int32)
    position = dest * CAP + rank
    where = (position == lax.broadcasted_iota(jnp.int32, (slots, owned), 0)).astype(F32).astype(BF16)
    line = lax.broadcasted_iota(jnp.int32, (128, owned), 0)
    which = node[...]
    block = lax.shift_right_logical(which, 6)
    inner = which - block * 64
    marks = jnp.where(line == 64, block, jnp.where(line == 65, inner, jnp.where(line == 66, 1, 0)))
    high, low = split(sums)
    turned = lambda a, b: lax.dot_general(a, b, (((1,), (1,)), ((), ())), preferred_element_type=F32)
    slots_of[...] = dot(where, high) + dot(where, low) + turned(where, marks.astype(F32).astype(BF16))


def holder_kernel(flow, steps, slots, after, spread, counted):
    flow.wait(slots)
    tally = []
    for n in range(4):
        total = jnp.zeros((), F32)
        for g in range(8):
            total = total + jnp.where(steps[g] == n + 1, 1.0, 0.0)
        tally.append(total)
    values = slots[...]
    count = values.shape[0]
    lane = lax.broadcasted_iota(jnp.int32, (count, 128), 1)
    pick = lambda at: jnp.sum(jnp.where(lane == at, values, 0.0), axis=1, keepdims=True)
    place_of = jnp.where(pick(66) > 0.5, pick(64) * 64.0 + pick(65), -1.0).astype(jnp.int32)
    high, low = split(values.T)
    both = jnp.concatenate([high, low], 0)
    low8 = low_lanes(8)
    for chunk in range(OWN * 64 // 256):
        spots = lax.broadcasted_iota(jnp.int32, (count, 256), 1) + chunk * 256
        hot = (place_of == spots).astype(F32).astype(BF16)
        out = lax.dot_general(both, hot, (((1,), (0,)), ((), ())), preferred_element_type=F32)
        out = out[:128] + out[128:]
        for j in range(2):
            first = chunk * 4 + 2 * j
            for n in range(4):
                even = out[n * 16 : n * 16 + 8, j * 128 : (j + 1) * 128]
                odd = out[n * 16 + 8 : n * 16 + 16, j * 128 : (j + 1) * 128]
                spread[n, first] = jnp.where(low8, even, pltpu.roll(odd, 64, 1))
                spread[n, first + 1] = jnp.where(low8, pltpu.roll(even, 64, 1), odd)
            many = jnp.broadcast_to(out[66:67, j * 128 : (j + 1) * 128], (8, 128))
            other = pltpu.roll(many, 64, 1)
            for n in range(4):
                counted[n, first] = jnp.where(low8, many, other) * tally[n]
                counted[n, first + 1] = jnp.where(low8, other, many) * tally[n]


def swap_even(axis):
    return [(i, i ^ 1) for i in range(lax.axis_size(axis))]


def swap_odd(axis):
    inner = range(1, lax.axis_size(axis) - 1, 2)
    return [(i, i + 1) for i in inner] + [(i + 1, i) for i in inner]


def exchange(axis, for_even, for_odd):
    return lax.ppermute(for_even, axis, swap_even(axis)), lax.ppermute(for_odd, axis, swap_odd(axis))


def body(
    checkpoint_field,
    checkpoint_memory,
    stiffness,
    block_offsets,
    chargeability,
    relaxation,
    observed,
    receiver_part,
    receiver_node,
    gate_step,
):
    devices = lax.axis_size(("px", "py"))
    slots = devices * CAP
    turn = pltpu.VMEM((256, 128), F32)
    lookup = pltpu.SMEM((16, 128), jnp.int32)
    places = pltpu.VMEM((PLACES, 16, 128), BF16)
    sums = pltpu.VMEM((PLACES, 16, 128), F32)
    blocks = pltpu.VMEM((OWN, 8, 128), F32)
    px_first = ((PX_BASE + 80, WIDTH), BF16, "v")
    py_first = ((PY_BASE + 64, WIDTH), BF16, "v")
    px_shape = ((16, 16, 128), BF16, "v")
    py_shape = ((14, 16, 128), BF16, "v")
    down = ((ROWS, NODE, WIDTH), BF16, "v")
    two = (2,) + py_first[0]
    m_even, m_odd, both, d_even, d_odd, lines, sent = call(
        start_kernel,
        [
            px_first[:2] + ("h",), px_first[:2] + ("h",), ((PAGES,) + py_first[0], BF16, "h"), down[:2] + ("h",), down[:2] + ("h",),
            ((8, 128), F32, "v"), ((slots, 128), F32, "h"),
        ],
        [
            (gate_step.reshape(1, -1), "h"), (observed, "h"), (receiver_part.reshape(1, -1), "h"),
            (receiver_node.reshape(1, -1), "h"), (block_offsets, "h"), (checkpoint_field, "h"),
            (checkpoint_memory, "h"), (chargeability, "h"), (stiffness, "b"),
        ],
        [blocks, blocks, turn, pltpu.VMEM((slots, 128), F32)]
        + [pltpu.VMEM(shape, BF16) for shape in (px_first[0], px_first[0], two, down[0], down[0])],
        copies=2 * COLS + 2 * ROWS + 8, vmem=65 * 1000 * 1000,
    )
    r_even, r_odd = exchange("px", m_even, m_odd)
    d_even, d_odd = exchange("py", d_even, d_odd)
    sent, r_even = lax.optimization_barrier((sent, r_even))
    held = lax.all_to_all(
        sent.reshape(devices, CAP, 128), ("px", "py"), split_axis=0, concat_axis=0, tiled=True
    ).reshape(slots, 128)
    n_even, n_odd = call(
        first_py_kernel, [py_first, py_first],
        [(r_even, "v"), (r_odd, "v"), (both, "b")],
        copies=2, vmem=50 * 1000 * 1000,
    )
    (known,) = call(
        decay_kernel, [((ROOM, 8, 128), F32, "h")],
        [(n_even, "v"), (checkpoint_field, "h"), (checkpoint_memory, "h"), (chargeability, "h"), (relaxation, "h")],
        [pltpu.VMEM((KNOWN, 8, 128), F32), turn], copies=1, vmem=VMEM_MOST,
    )
    n_even, n_odd = exchange("py", n_even, n_odd)
    held, n_even = lax.optimization_barrier((held, n_even))
    (near,) = call(
        load_kernel, [((KNOWN, 8, 128), F32, "v")], [(n_even, "v"), (known, "b")], copies=1,
    )
    weights = [(a, "v") for a in (stiffness, r_even, r_odd, n_even, n_odd, d_even, d_odd)]
    past, now, m_even, m_odd, p_even, p_odd, table, coefs, *late = call(
        forward_one,
        [
            ((2 * OWN, 8, 128), F32, "v"), ((3 * OWN, 8, 128), F32, "v"), px_shape, px_shape, py_shape, py_shape,
            ((16, 128), jnp.int32, "v"), ((4 * ROWS, 8, 128), F32, "v"), py_first, down, down,
        ],
        [(lines, "v")] + weights[:4] + [(a, "h") for a, _ in weights[4:]] + [(near, "v")],
        [places, places, lookup], copies=2,
    )
    weights = weights[:4] + [(a, "v") for a in late]
    r_even, r_odd = exchange("px", m_even, m_odd)
    n_even, n_odd = call(
        second_py_kernel, [py_shape, py_shape],
        [(r_even, "v"), (r_odd, "v"), (p_even, "v"), (p_odd, "v")],
    )
    n_even, n_odd = exchange("py", n_even, n_odd)
    spread, counted = call(
        holder_kernel, [((4, OWN, 8, 128), F32, "v"), ((4, OWN, 8, 128), F32, "v")],
        [(gate_step, "s"), (held, "h"), (m_even, "v")],
    )
    rim = ((COLS // 2 + 1 + WIDE, 16, 128), BF16, "v")
    rim_py = ((6, 16, 128), BF16, "v")
    pair_out = [
        ((ROWS * (COLS + 2), 8, 128), F32, "v"), ((ROWS * WIDE, 8, 128), F32, "v"),
        rim, rim,
    ]
    adjoint4, *rest = call(
        turn_kernel, [PLAIN] + pair_out,
        [(table, "s")] + weights
        + [(r_even, "v"), (r_odd, "v"), (n_even, "v"), (n_odd, "v"), (now, "v"), (coefs, "v"), (spread, "v"), (counted, "v")],
        [places, places, sums, sums, blocks, blocks],
    )

    def gathered(first, second, m_even, m_odd):
        r_even, r_odd = exchange("px", m_even, m_odd)
        own_first, own_second, n_even, n_odd = call(
            adjoint_py_kernel, [PLAIN, PLAIN, rim_py, rim_py],
            [(first, "v"), (second, "v"), (r_even, "v"), (r_odd, "v")],
            [pltpu.VMEM(first.shape, F32), pltpu.VMEM(second.shape, F32)],
        )
        n_even, n_odd = exchange("py", n_even, n_odd)
        return [(a, "v") for a in (own_first, own_second, n_even, n_odd)]

    later, *rest = call(
        adjoint_two, [((2 * OWN, 8, 128), F32, "v")] + pair_out,
        [(table, "s")] + weights + gathered(*rest)
        + [(adjoint4, "v"), (past, "v"), (coefs, "v"), (spread, "v"), (counted, "v")],
        [sums, sums],
    )
    (before,) = call(
        gradient_kernel, [((2 * OWN, 8, 128), F32, "v")],
        [(a, "b" if a is known else "v") for a in (rest[2], adjoint4, later, known, past, now)],
        [pltpu.VMEM((KNOWN, 8, 128), F32)], copies=1,
    )
    field_out, gradient = call(
        finish_kernel, [(checkpoint_field.shape, F32, "v"), (chargeability.shape, F32, "v")],
        [] + gathered(*rest) + [(before, "v")], [blocks, blocks, turn],
    )
    return field_out, gradient


def solution(mesh):
    in_specs = (
        P("px", "py", None),
        P(None, "px", "py", None),
        P("px", "py", None, None),
        P("px", "py", None),
        P("px", "py", None),
        P(None, "px", "py", None),
        P(("px", "py"), None),
        P(("px", "py"), None),
        P(("px", "py")),
        P(),
    )
    out_specs = (P("px", "py", None), P("px", "py", None))
    return jax.shard_map(body, mesh=mesh, in_specs=in_specs, out_specs=out_specs, check_vma=False)
```
